256 devices in a mesh: seq: 128 (over z, x, y_lo, core), dp: 2 (over y_hi).
Axes of the slice: x: 4, y: 4 (y_hi: 2, y_lo: 2; y = y_hi * 2 + y_lo), z: 8, core: 2. Of those that a mesh axis runs over, the one named last changes fastest.
Arguments:
- x_tokens: bfloat16 [2, 32768, 768], P('dp', 'seq'), may hold values from -21 to 21
- cotangent: bfloat16 [2, 32768, 768], P('dp', 'seq'), may hold values from -6 to 6
- w_qkv: bfloat16 [768, 2304], replicated, may hold values from -0.21875 to 0.21875
- w_out: bfloat16 [768, 768], replicated, may hold values from -0.21875 to 0.21875
Outputs:
- sublayer_out: bfloat16 [2, 32768, 768], P('dp', 'seq')
- input_grad: bfloat16 [2, 32768, 768], P('dp', 'seq')
- qkv_grad: float32 [768, 2304], P('seq')
- out_grad: float32 [768, 768], P('seq')
The draws below stay inside these ranges and needn't reach their ends.
All inputs are finite; a program needn't handle non-finite values.
Results may differ from the reference program's by a relative error of at most 0.019.
The reference program's roundings to bfloat16 on the way count: a program that leaves them out, or rounds other values in their place, can miss the bound.
Values may be sent and summed in bfloat16 or wider, within the bound.
No kernel may reach another device: no remote copies, remote signals or barrier semaphores. Data moves between devices by JAX's collectives and lax.ppermute only.
A program may use at most 128 MiB of HBM per device.

```python
from functools import partial
import jax
import jax.numpy as jnp
from jax import lax

DH = 64
D = 768
NR = 128
TOK_DEV = 256
LEVELS = 7
SEQ_LEN = 32768
SEQS = 2
N_SEQ = 128


def draw_x_tokens(key, part):
    key = jax.random.fold_in(key, 7)
    subkeys = jax.random.split(key, 1)
    full_shape = (SEQS, SEQ_LEN, D)
    values = jnp.clip(jax.random.normal(subkeys[0], full_shape, jnp.float32), -6.0, 6.0)
    return values.astype(jnp.bfloat16)


def level_of(own_key, dims, shards, least, high):
    def one(position, blocks):
        steps = jax.random.uniform(jax.random.fold_in(jax.random.fold_in(own_key, 6), position), (blocks,), jnp.float32, least / len(shards), high / len(shards))
        return jnp.repeat(jnp.exp(steps), dims[position] // blocks).reshape((-1,) + (1,) * (len(dims) - position - 1))

    factor_of = one(*shards[0])
    for cut in shards[1:]:
        factor_of = factor_of * one(*cut)
    return factor_of


def bell_draw(stream_key, dims, width, bound, cuts=(), kind=jnp.bfloat16):
    gain = level_of(stream_key, dims, cuts, -0.22, 0.18) if cuts else 1.0
    array = jax.random.normal(stream_key, dims, jnp.float32) * width * gain
    return jnp.minimum(jnp.maximum(array, -bound), bound).astype(kind)


def setup_inputs(seed: int = 0) -> dict:
    seeds = jax.random.split(jax.random.key(seed), 5)
    x_tokens = draw_x_tokens(jax.random.fold_in(seeds[4], 71), 0)
    cotangent = bell_draw(seeds[1], (SEQS, SEQ_LEN, D), 1.0, 6.0, ((0, 2), (1, 128)))
    w_qkv = bell_draw(seeds[2], (D, 3 * D), D ** -0.5, 0.21875)
    w_out = bell_draw(seeds[3], (D, D), D ** -0.5, 0.21875)
    return dict(x_tokens=x_tokens, cotangent=cotangent, w_qkv=w_qkv, w_out=w_out)


half_root = 0.7071067811865476


def product(form, left, right):
    return jnp.einsum(form, left.astype(jnp.float32), right.astype(jnp.float32))


def coarsen(level_nodes):
    groups, height, features = level_nodes.shape
    paired = level_nodes.reshape(groups // 2, height, 2, features).astype(jnp.float32)
    return ((paired[:, :, 0] + paired[:, :, 1]) * half_root).astype(jnp.bfloat16)


def coarsen_back(gradients):
    groups, height, features = gradients.shape
    return jnp.repeat(gradients * half_root, 2, axis=1).reshape(groups * 2, height, features)


def mirror(level_nodes):
    halves_shape = (level_nodes.shape[0] // 2, 2) + level_nodes.shape[1:]
    return jnp.flip(level_nodes.reshape(halves_shape), 1).reshape(level_nodes.shape)


def build_tree(keyval, block_rows):
    current = keyval.reshape(keyval.shape[0] // block_rows, block_rows, keyval.shape[1])
    tree_depth = (keyval.shape[0] // block_rows).bit_length() - 1
    layers = []
    for tier_index in range(tree_depth):
        current = coarsen(current)
        layers.append(current)
    return layers


def pair_attention(block_rows, queries, exact, inner, remote, upstream_heads):
    tokens = queries.shape[0]
    head_size = queries.shape[-1]
    inverse_root = head_size ** -0.5
    pair_span = 2 * block_rows
    grouped_query = queries.reshape(tokens // pair_span, pair_span, 2, head_size)
    exact_key = exact[:, 0].reshape(grouped_query.shape)
    exact_value = exact[:, 1].reshape(grouped_query.shape)
    grouped_back = upstream_heads.reshape(grouped_query.shape)
    pieces = [product("gqhd,gkhd->hgqk", grouped_query, exact_key).reshape(2, tokens, pair_span) * inverse_root]
    dpieces = [product("gqhd,gkhd->hgqk", grouped_back, exact_value).reshape(2, tokens, pair_span)]
    views = []
    for level_nodes in inner:
        group_count = level_nodes.shape[0]
        view_query = queries.reshape(group_count, tokens // group_count, 2, head_size)
        view_back = upstream_heads.reshape(view_query.shape)
        views.append((view_query, view_back))
        pieces.append(product("gqhd,gkhd->hgqk", view_query, level_nodes[:, :, 0]).reshape(2, tokens, block_rows) * inverse_root)
        dpieces.append(product("gqhd,gkhd->hgqk", view_back, level_nodes[:, :, 1]).reshape(2, tokens, block_rows))
    pieces.append(product("qhd,khd->hqk", queries, remote[:, 0]) * inverse_root)
    dpieces.append(product("qhd,khd->hqk", upstream_heads, remote[:, 1]))
    top = jnp.max(pieces[0], axis=-1, keepdims=True)
    for piece in pieces[1:]:
        top = jnp.maximum(top, jnp.max(piece, axis=-1, keepdims=True))
    shifted = [jnp.exp(piece - top) for piece in pieces]
    total = jnp.sum(shifted[0], axis=-1, keepdims=True)
    for piece in shifted[1:]:
        total = total + jnp.sum(piece, axis=-1, keepdims=True)
    probs = [piece / total for piece in shifted]
    w_parts = [piece.astype(jnp.bfloat16) for piece in probs]
    row_delta = jnp.sum(probs[0] * dpieces[0], axis=-1, keepdims=True)
    for place in range(1, len(probs)):
        row_delta = row_delta + jnp.sum(probs[place] * dpieces[place], axis=-1, keepdims=True)
    s_parts = [(probs[place] * (dpieces[place] - row_delta) * inverse_root).astype(jnp.bfloat16) for place in range(len(probs))]
    w_first = w_parts[0].reshape(2, tokens // pair_span, pair_span, pair_span)
    s_first = s_parts[0].reshape(w_first.shape)
    attended = product("hgqk,gkhd->gqhd", w_first, exact_value).reshape(tokens, 2, head_size)
    dquery = product("hgqk,gkhd->gqhd", s_first, exact_key).reshape(tokens, 2, head_size)
    dexact = jnp.stack([product("hgqk,gqhd->gkhd", s_first, grouped_query).reshape(tokens, 2, head_size),
                        product("hgqk,gqhd->gkhd", w_first, grouped_back).reshape(tokens, 2, head_size)], axis=1)
    dinner = []
    for place, level_nodes in enumerate(inner):
        view_query, view_back = views[place]
        group_count = level_nodes.shape[0]
        w_level = w_parts[place + 1].reshape(2, group_count, tokens // group_count, block_rows)
        s_level = s_parts[place + 1].reshape(w_level.shape)
        attended = attended + product("hgqk,gkhd->gqhd", w_level, level_nodes[:, :, 1]).reshape(tokens, 2, head_size)
        dquery = dquery + product("hgqk,gkhd->gqhd", s_level, level_nodes[:, :, 0]).reshape(tokens, 2, head_size)
        dinner.append(jnp.stack([product("hgqk,gqhd->gkhd", s_level, view_query),
                                 product("hgqk,gqhd->gkhd", w_level, view_back)], axis=2))
    attended = attended + product("hqk,khd->qhd", w_parts[-1], remote[:, 1])
    dquery = dquery + product("hqk,khd->qhd", s_parts[-1], remote[:, 0])
    dremote = jnp.stack([product("hqk,qhd->khd", s_parts[-1], queries),
                         product("hqk,qhd->khd", w_parts[-1], upstream_heads)], axis=1)
    return attended, dquery, dexact, tuple(dinner), dremote


def to_pairs(values_in, head_size):
    leading = values_in.shape[:-1]
    pair_count = values_in.shape[-1] // (4 * head_size)
    reshaped = values_in.reshape(leading + (2, pair_count, 2, head_size))
    return jnp.moveaxis(reshaped, len(leading) + 1, 0)


def from_pairs(values_in):
    moved = jnp.moveaxis(values_in, 0, values_in.ndim - 3)
    return moved.reshape(moved.shape[:-4] + (-1,))


def local_attention(block_rows, head_size, queries, keyval, inner, remote, attended_grad):
    tokens = queries.shape[0]
    pair_query = jnp.moveaxis(queries.reshape(tokens, -1, 2, head_size), 1, 0)
    pair_back = jnp.moveaxis(attended_grad.reshape(tokens, -1, 2, head_size), 1, 0)
    pair_exact = to_pairs(keyval, head_size)
    pair_inner = tuple(to_pairs(mirror(level_nodes), head_size) for level_nodes in inner)
    pair_remote = to_pairs(remote, head_size)

    def one_pair(operands):
        return pair_attention(block_rows, *operands)

    attended, dquery, dexact, dinner, dremote = lax.map(one_pair, (pair_query, pair_exact, pair_inner, pair_remote, pair_back))
    attended = jnp.moveaxis(attended, 0, 1).reshape(tokens, -1)
    dquery = jnp.moveaxis(dquery, 0, 1).reshape(tokens, -1)
    dinner = tuple(mirror(from_pairs(gradients)) for gradients in dinner)
    return attended, dquery, from_pairs(dexact), dinner, from_pairs(dremote)


def tree_backward(summary_grad, dinner, dexact):
    current = summary_grad[None]
    for gradients in reversed(dinner):
        current = coarsen_back(current) + gradients
    return coarsen_back(current).reshape(dexact.shape) + dexact


def reference(x_tokens, cotangent, w_qkv, w_out):
    outputs = []
    input_grads = []
    qkv_total = jnp.zeros((D, 3 * D), jnp.float32)
    out_total = jnp.zeros((D, D), jnp.float32)
    for sequence in range(SEQS):
        tokens_in = x_tokens[sequence]
        upstream = cotangent[sequence]
        projected = jnp.dot(tokens_in, w_qkv, preferred_element_type=jnp.float32).astype(jnp.bfloat16)
        queries = projected[:, :D]
        device_keyval = projected[:, D:].reshape(N_SEQ, TOK_DEV, 2 * D)
        layers = jax.vmap(partial(build_tree, block_rows=NR))(device_keyval)
        upper_nodes = layers[-1][:, 0]
        remote_list = []
        for tier_index in range(LEVELS):
            remote_list.append(jnp.repeat(mirror(upper_nodes), 2 ** tier_index, axis=0))
            if tier_index + 1 < LEVELS:
                upper_nodes = coarsen(upper_nodes)
        remote_all = jnp.stack(remote_list, axis=1).reshape(N_SEQ, LEVELS * NR, 2 * D)
        attended_grad = jnp.dot(upstream, w_out.T, preferred_element_type=jnp.float32).astype(jnp.bfloat16)

        def per_device(operands):
            return local_attention(NR, DH, *operands)

        attended_f, dquery, dexact, dinner, dremote = lax.map(
            per_device, (queries.reshape(N_SEQ, TOK_DEV, D), device_keyval, tuple(layers[:-1]), remote_all,
                         attended_grad.reshape(N_SEQ, TOK_DEV, D)))
        attended = attended_f.reshape(SEQ_LEN, D).astype(jnp.bfloat16)
        outputs.append(jnp.dot(attended, w_out, preferred_element_type=jnp.float32).astype(jnp.bfloat16))
        remote_grads = dremote.reshape(N_SEQ, LEVELS, NR, 2 * D)
        carried = None
        for tier_index in reversed(range(LEVELS)):
            grouped = remote_grads[:, tier_index].reshape(N_SEQ // 2 ** tier_index, 2 ** tier_index, NR, 2 * D)
            level_term = mirror(jnp.sum(grouped, axis=1))
            if carried is not None:
                level_term = level_term + coarsen_back(carried)
            carried = level_term
        leaf_grads = jax.vmap(tree_backward)(carried, dinner, dexact)
        proj_grads = jnp.concatenate([dquery.reshape(SEQ_LEN, D), leaf_grads.reshape(SEQ_LEN, 2 * D)], axis=1).astype(jnp.bfloat16)
        input_grads.append(jnp.dot(proj_grads, w_qkv.T, preferred_element_type=jnp.float32).astype(jnp.bfloat16))
        qkv_total = qkv_total + jnp.dot(tokens_in.T, proj_grads, preferred_element_type=jnp.float32)
        out_total = out_total + jnp.dot(attended.T, upstream, preferred_element_type=jnp.float32)
    return jnp.stack(outputs), jnp.stack(input_grads), qkv_total, out_total
```

```python
import jax
import jax.numpy as jnp
from jax import lax
from jax.experimental import pallas as pl
from jax.experimental.pallas import tpu as pltpu
from jax.sharding import Mesh, PartitionSpec as P

D = 768
H = 384
TOK = 256
NR = 128
DH = 64
ZN, XN, YN = 8, 4, 2
ZR = 48
SLOT = 112
HALF_ROOT = 0.7071067811865476
LOG2E = 1.4426950408889634
VMEM = 56 * 1024 * 1024
F32 = jnp.float32
BF16 = jnp.bfloat16


def dot(a, b):
    return lax.dot_general(a, b, (((1,), (0,)), ((), ())), preferred_element_type=F32)


def dot_nt(a, b):
    return lax.dot_general(a, b, (((1,), (1,)), ((), ())), preferred_element_type=F32)


def dot_tn(a, b):
    return lax.dot_general(a, b, (((0,), (0,)), ((), ())), preferred_element_type=F32)


def iota(shape, axis):
    return lax.broadcasted_iota(jnp.int32, shape, axis)


def pair_matrix(rows, cols, valid):
    r, k = iota((rows, cols), 0), iota((rows, cols), 1)
    return (((k >> 1) == r) & (r < valid)).astype(BF16)


def coarsen(node, rows=None, valid=None):
    rows = node.shape[0] // 2 if rows is None else rows
    valid = rows if valid is None else valid
    return (dot(pair_matrix(rows, node.shape[0], valid), node) * HALF_ROOT).astype(BF16)


def spread(grad, rows, valid=None):
    r, k = iota((rows, grad.shape[0]), 0), iota((rows, grad.shape[0]), 1)
    hot = (r >> 1) == k
    if valid is not None:
        hot = hot & (r < valid)
    up = lax.dot_general(
        hot.astype(F32), grad, (((1,), (0,)), ((), ())),
        precision=lax.Precision.HIGHEST, preferred_element_type=F32,
    )
    return up * HALF_ROOT


def whole(*shape):
    return pl.BlockSpec(shape, lambda *_: (0,) * len(shape))


def call(body, grid, ins, outs, scratch=()):
    return pl.pallas_call(
        body,
        grid_spec=pltpu.PrefetchScalarGridSpec(
            num_scalar_prefetch=1,
            grid=grid,
            in_specs=ins,
            out_specs=[s for s, _ in outs],
            scratch_shapes=list(scratch),
        ),
        out_shape=[jax.ShapeDtypeStruct(shape, kind) for _, (shape, kind) in outs],
        compiler_params=pltpu.CompilerParams(vmem_limit_bytes=VMEM),
    )


def project_body(pos, x_own, x_oth, ct_own, ct_oth, wq, wk, wv, wo, perm, q_out, kv_out, ag_out, n1_out, n2_out, n3_out, n4_out, zs_out, xt_out):
    c, z = pos[0], pos[1]
    oth = 1 - c

    def both(first, second):
        return ((c, first), (oth, second))

    for e, x in both(x_own, x_oth):
        kv_out[e, 0] = dot(x[...], wk[...]).astype(BF16)
        kv_out[e, 1] = dot(x[...], wv[...]).astype(BF16)
    for p in range(2):
        for e in range(2):
            n1_out[e, p] = coarsen(kv_out[e, p])
            n2_out[p, e * 64 : (e + 1) * 64] = coarsen(n1_out[e, p])
        n3 = coarsen(n2_out[p])
        n4 = coarsen(n3)
        n5 = coarsen(n4)
        n6 = coarsen(n5, 16, 8)
        n7 = coarsen(n6, 16, 4)
        n3_out[p] = n3
        n4_out[p] = n4
        zs_out[z, p] = jnp.zeros_like(n5)
        zs_out[z ^ 1, p] = n5
        for far in (2, 3):
            zs_out[z ^ far, p] = n6
        for far in (4, 5, 6, 7):
            zs_out[z ^ far, p] = n7
    for e, x in both(x_own, x_oth):
        q_out[e] = dot(x[...], wq[...]).astype(BF16)
        xt_out[e] = dot_nt(perm[...], x[...]).astype(BF16)
    for e, ct in both(ct_own, ct_oth):
        ag_out[e] = dot_nt(ct[...], wo[...]).astype(BF16)


def project(pos, x_own, x_oth, ct_own, ct_oth, w_qkv, w_out, perm):
    col = lambda part: pl.BlockSpec((D, H), lambda i, s: (0, 2 * part + s[0]))
    outs = [
        (2, TOK, H), (2, 2, TOK, H), (2, TOK, H), (2, 2, NR, H), (2, NR, H), (2, 64, H), (2, 32, H), (ZN, 2, 16, H), (2, D, TOK),
    ]
    return call(
        project_body,
        (1,),
        [whole(TOK, D)] * 4 + [col(0), col(1), col(2), pl.BlockSpec((H, D), lambda i, s: (s[0], 0)), whole(D, D)],
        [(whole(*shape), (shape, BF16)) for shape in outs],
    )(pos, x_own, x_oth, ct_own, ct_oth, w_qkv, w_qkv, w_qkv, w_out, perm)


def z_source(z, rows_axis, shape):
    i = iota(shape, rows_axis)
    near = 16 * (z ^ 1) + i
    mid = 16 * (z ^ (2 + ((i - 16) >> 3))) + ((i - 16) & 7)
    far = 16 * (z ^ (4 + ((i - 32) >> 2))) + ((i - 32) & 3)
    return jnp.where(i < 16, near, jnp.where(i < 32, mid, far))


def plane_body(pos, zr, n3, n4, out):
    z, j = pos[1], pos[2]
    hot = (iota((ZR, 128), 1) == z_source(z, 0, (ZR, 128))).astype(BF16)
    for p in range(2):
        rows = dot(hot, zr[:, p].reshape(128, H)).astype(BF16)
        for slot in range(8):
            out[slot, p, :ZR] = rows
        blank = jnp.zeros((64, H), BF16)
        for far in (0, 1):
            out[j ^ far, p, ZR:] = blank
        for far in (2, 3):
            out[j ^ far, p, ZR:] = n3[p]
        for far in (4, 5, 6, 7):
            out[j ^ far, p, ZR : ZR + 32] = n4[p]
            out[j ^ far, p, ZR + 32 :] = blank[:32]


def plane_slots(pos, zr, n3, n4):
    return call(
        plane_body,
        (1,),
        [whole(ZN, 2, 16, H), whole(2, 64, H), whole(2, 32, H)],
        [(whole(8, 2, SLOT, H), ((8, 2, SLOT, H), BF16))],
    )(pos, zr, n3, n4)[0]


def attention_body(pos, q, ag, kv, n1, yr, xr, att_out, dq_out, dkv_out, dn1_out, dy_out, dx_out, keys, s_ref, dw_ref, w_ref, ds_ref, drem):
    j = pos[2]
    for p in range(2):
        for e in range(2):
            keys[e, p, :256] = kv[e, p]
            keys[e, p, 256:384] = n1[1 - e, p]
            keys[e, p, 384:512] = yr[p]
            for far in (2, 3):
                start = 512 + 64 * (far - 2)
                keys[e, p, start : start + 64] = xr[j ^ far, p, ZR:]
            for far in (4, 5, 6, 7):
                start = 640 + 32 * (far - 4)
                keys[e, p, start : start + 32] = xr[j ^ far, p, ZR : ZR + 32]
            for slot in range(8):
                start = 768 + ZR * slot
                keys[e, p, start : start + ZR] = xr[slot, p, :ZR]
    lane = iota((TOK, 128), 1)
    for e in range(2):
        att_t, dq_t = [], []
        dk = dv = None
        for h in range(2):
            mine = (lane >> 6) == h
            qh = jnp.where(mine, q[e], jnp.zeros((), BF16))
            ah = jnp.where(mine, ag[e], jnp.zeros((), BF16))
            s_ref[...] = dot_nt(keys[e, 0], qh)
            dw_ref[...] = dot_nt(keys[e, 1], ah)
            top = jnp.max(s_ref[...], axis=0, keepdims=True)
            s_ref[...] = jnp.exp2((s_ref[...] - top) * (LOG2E * DH ** -0.5))
            total = jnp.sum(s_ref[...], axis=0, keepdims=True)
            inverse = 1.0 / total
            delta = jnp.sum(s_ref[...] * dw_ref[...], axis=0, keepdims=True) * inverse
            prob = s_ref[...] * inverse
            w_ref[...] = prob.astype(BF16)
            ds_ref[...] = (prob * (dw_ref[...] - delta) * DH ** -0.5).astype(BF16)
            att_t.append(dot_tn(keys[e, 1], w_ref[...])[64 * h : 64 * h + 64])
            dq_t.append(dot_tn(keys[e, 0], ds_ref[...])[64 * h : 64 * h + 64])
            dkh, dvh = dot(ds_ref[...], qh), dot(w_ref[...], ah)
            dk = dkh if dk is None else dk + dkh
            dv = dvh if dv is None else dv + dvh
        att_out[e] = jnp.concatenate(att_t, axis=0).T.astype(BF16)
        dq_out[e] = jnp.concatenate(dq_t, axis=0).T.astype(BF16)
        for p, grad in ((0, dk), (1, dv)):
            dkv_out[e, p] = grad[:256]
            dn1_out[1 - e, p] = grad[256:384]
            if e == 0:
                drem[p] = grad[384:]
            else:
                drem[p] = drem[p] + grad[384:]
    for p in range(2):
        rows = drem[p].astype(BF16)
        dy_out[p] = rows[:128]
        blank = jnp.zeros((64, 128), BF16)
        for far in (0, 1):
            dx_out[j ^ far, p, ZR:] = blank
        for far in (2, 3):
            start = 128 + 64 * (far - 2)
            dx_out[j ^ far, p, ZR:] = rows[start : start + 64]
        for far in (4, 5, 6, 7):
            start = 256 + 32 * (far - 4)
            dx_out[j ^ far, p, ZR : ZR + 32] = rows[start : start + 32]
            dx_out[j ^ far, p, ZR + 32 :] = blank[:32]
        for slot in range(8):
            start = 384 + ZR * slot
            dx_out[slot, p, :ZR] = rows[start : start + ZR]


def attention(pos, q, ag, kv, n1, yr, xr):
    def cut(*lead):
        return pl.BlockSpec(lead + (128,), lambda i, s: (0,) * len(lead) + (i,))

    outs = [
        ((2, TOK), BF16), ((2, TOK), BF16), ((2, 2, TOK), F32), ((2, 2, NR), F32), ((2, NR), BF16), ((8, 2, SLOT), BF16),
    ]
    n = 1152
    return call(
        attention_body,
        (H // 128,),
        [cut(2, TOK), cut(2, TOK), cut(2, 2, TOK), cut(2, 2, NR), cut(2, NR), cut(8, 2, SLOT)],
        [(cut(*lead), (lead + (H,), kind)) for lead, kind in outs],
        [
            pltpu.VMEM((2, 2, n, 128), BF16), pltpu.VMEM((n, TOK), F32), pltpu.VMEM((n, TOK), F32),
            pltpu.VMEM((n, TOK), BF16), pltpu.VMEM((n, TOK), BF16), pltpu.VMEM((2, 768, 128), F32),
        ],
    )(pos, q, ag, kv, n1, yr, xr)


def output_body(pos, att_own, att_oth, ct_own, ct_oth, w_own, w_oth, p_own, p_oth, out, grad_out):
    c = pos[0]
    out[...] = (dot(att_own[c], w_own[...]) + dot(att_oth[c], w_oth[...])).astype(BF16)
    total = None
    for e, ct in ((c, ct_own), (1 - c, ct_oth)):
        att_t = (dot_nt(p_own[...], att_own[e]) + dot_nt(p_oth[...], att_oth[e])).astype(BF16)
        term = dot(att_t, ct[...])
        total = term if total is None else total + term
    grad_out[...] = total.astype(BF16).reshape(8, 96, H)


def output_side(pos, att_own, att_oth, ct_own, ct_oth, w_out, perm):
    row = lambda flip: pl.BlockSpec((H, D), lambda i, s: (s[0] ^ flip, 0))
    col = lambda flip, rows: pl.BlockSpec((rows, H), lambda i, s: (0, s[0] ^ flip))
    return call(
        output_body,
        (1,),
        [whole(2, TOK, H)] * 2 + [col(0, TOK)] * 2 + [row(0), row(1), col(0, D), col(1, D)],
        [(whole(TOK, D), ((TOK, D), BF16)), (whole(8, 96, H), ((8, 96, H), BF16))],
    )(pos, att_own, att_oth, ct_own, ct_oth, w_out, w_out, perm, perm)


def back_body(pos, xr, out):
    z = pos[1]
    hot = (iota((128, ZR), 0) == z_source(z, 1, (128, ZR))).astype(BF16)
    for p in range(2):
        total = xr[0, p, :ZR].astype(F32)
        for slot in range(1, 8):
            total = total + xr[slot, p, :ZR].astype(F32)
        out[:, p] = dot(hot, total.astype(BF16)).astype(BF16).reshape(8, 16, H)


def back_slots(pos, xr):
    return call(
        back_body,
        (1,),
        [whole(8, 2, SLOT, H)],
        [(whole(ZN, 2, 16, H), ((ZN, 2, 16, H), BF16))],
    )(pos, xr)[0]


def leaf_body(pos, zr, xr, yr, dn1, dkv, dq, xt, pg_out, gqk_out, gv_out):
    z, j = pos[1], pos[2]

    def gather(ref, index, fars, p, lo, hi):
        total = None
        for far in fars:
            term = ref[index ^ far, p, lo:hi].astype(F32)
            total = term if total is None else total + term
        return total

    for p in range(2):
        g7 = gather(zr, z, (4, 5, 6, 7), p, 0, 16)
        g6 = gather(zr, z, (2, 3), p, 0, 16) + spread(g7, 16, 8)
        g5 = gather(zr, z, (1,), p, 0, 16) + spread(g6, 16)
        g4 = gather(xr, j, (4, 5, 6, 7), p, ZR, ZR + 32) + spread(g5, 32)
        g3 = gather(xr, j, (2, 3), p, ZR, ZR + 64) + spread(g4, 64)
        g2 = yr[p].astype(F32) + spread(g3, 128)
        for e in range(2):
            g1 = dn1[e, p] + spread(g2[64 * e : 64 * e + 64], 128)
            leaf = dkv[e, p] + spread(g1, 256)
            pg_out[e, :, H * (1 + p) : H * (2 + p)] = leaf.astype(BF16)
    for e in range(2):
        pg_out[e, :, :H] = dq[e]
    for part, out in ((0, gqk_out.at[0]), (1, gqk_out.at[1]), (2, gv_out)):
        total = dot(xt[0], pg_out[0, :, H * part : H * part + H]) + dot(xt[1], pg_out[1, :, H * part : H * part + H])
        out[...] = total.astype(BF16).reshape(8, 96, H)


def leaf_grads(pos, zr, xr, yr, dn1, dkv, dq, xt):
    return call(
        leaf_body,
        (1,),
        [
            whole(ZN, 2, 16, H), whole(8, 2, SLOT, H), whole(2, NR, H), whole(2, 2, NR, H), whole(2, 2, TOK, H),
            whole(2, TOK, H), whole(2, D, TOK),
        ],
        [
            (whole(2, TOK, 3 * H), ((2, TOK, 3 * H), BF16)),
            (whole(2, 8, 96, H), ((2, 8, 96, H), BF16)),
            (whole(8, 96, H), ((8, 96, H), BF16)),
        ],
    )(pos, zr, xr, yr, dn1, dkv, dq, xt)


def input_body(pos, pg_own, pg_oth, *rest):
    out = rest[-1]
    total = None
    for part in range(3):
        for pg, w in ((pg_own, rest[part]), (pg_oth, rest[3 + part])):
            term = dot_nt(pg[:, H * part : H * part + H], w[...])
            total = term if total is None else total + term
    out[...] = total.astype(BF16)


def input_side(pos, pg_own, pg_oth, w_qkv):
    col = lambda part, flip: pl.BlockSpec((D, H), lambda i, s: (0, 2 * part + (s[0] ^ flip)))
    return call(
        input_body,
        (1,),
        [whole(TOK, 3 * H)] * 2 + [col(part, flip) for flip in (0, 1) for part in range(3)],
        [(whole(TOK, D), ((TOK, D), BF16))],
    )(pos, pg_own, pg_oth, *[w_qkv] * 6)[0]


def swap(value, axis):
    return lax.ppermute(value, axis, [(0, 1), (1, 0)])


def shards(x_tokens, cotangent, w_qkv, w_out):
    x_own, ct_own = x_tokens[0], cotangent[0]
    c, z = lax.axis_index("c"), lax.axis_index("z")
    j = 2 * lax.axis_index("x") + lax.axis_index("y")
    pos = jnp.stack([c, z, j]).astype(jnp.int32)
    x_oth, ct_oth = swap(x_own, "c"), swap(ct_own, "c")
    f = jnp.arange(D, dtype=jnp.int32)
    source = 96 * (f // 12 % 8) + 12 * (f // 96) + f % 12
    perm = (source[:, None] == f[None, :]).astype(BF16)

    q, kv, ag, n1, n2, n3, n4, zs, xt = project(pos, x_own, x_oth, ct_own, ct_oth, w_qkv, w_out, perm)
    yr = swap(n2, "y")
    zr = lax.all_to_all(zs, "z", 0, 0)
    xs = plane_slots(pos, zr, n3, n4)
    xr = lax.all_to_all(xs, ("x", "y"), 0, 0)
    att, dq, dkv, dn1, dy, dx = attention(pos, q, ag, kv, n1, yr, xr)

    att_oth = swap(att, "c")
    dy_r = swap(dy, "y")
    dx_r = lax.all_to_all(dx, ("x", "y"), 0, 0)
    dz = back_slots(pos, dx_r)
    dz_r = lax.all_to_all(dz, "z", 0, 0)
    layer_out, g_out = output_side(pos, att, att_oth, ct_own, ct_oth, w_out, perm)
    pg, g_qk, g_v = leaf_grads(pos, dz_r, dx_r, dy_r, dn1, dkv, dq, xt)
    pg_own = lax.dynamic_index_in_dim(pg, c, 0, keepdims=False)
    pg_oth = swap(lax.dynamic_index_in_dim(pg, 1 - c, 0, keepdims=False), "c")
    input_grad = input_side(pos, pg_own, pg_oth, w_qkv)

    first = jnp.concatenate([g_qk[0], g_out], axis=-1)
    second = jnp.concatenate([g_qk[1], g_v], axis=-1)
    terms = jnp.stack([first, second], axis=1).reshape(16, 96, D)
    terms = lax.all_to_all(terms, ("x", "y", "dp"), 0, 0)
    terms = jnp.sum(terms.astype(F32), axis=0).astype(BF16).reshape(ZN, 12, D)
    terms = lax.all_to_all(terms, "z", 0, 0)
    mine = jnp.sum(terms.astype(F32), axis=0).astype(BF16)
    other = swap(mine, "dp")
    low = lax.axis_index("dp") == 0
    rows = jnp.concatenate([jnp.where(low, mine, other), jnp.where(low, other, mine)], axis=1)
    keep = lax.dynamic_slice_in_dim(rows, 6 * c, 6, 0)
    got = swap(lax.dynamic_slice_in_dim(rows, 6 - 6 * c, 6, 0), "c")
    left, right = jnp.where(c == 0, keep, got), jnp.where(c == 0, got, keep)
    part = lambda k: [left[:, H * k : H * k + H], right[:, H * k : H * k + H]]
    qkv_grad = jnp.concatenate(part(0) + part(2) + part(3), axis=1).astype(F32)
    out_grad = jnp.concatenate(part(1), axis=1).astype(F32)
    return (layer_out[None], input_grad[None], qkv_grad, out_grad)


def solution(mesh):
    split = Mesh(mesh.devices.reshape(ZN, XN, YN, 2, 2), ("z", "x", "y", "c", "dp"))
    seq = ("z", "x", "y", "c")
    return jax.shard_map(
        shards,
        mesh=split,
        in_specs=(P("dp", seq, None), P("dp", seq, None), P(), P()),
        out_specs=(P("dp", seq, None), P("dp", seq, None), P(seq, None), P(seq, None)),
        check_vma=False,
    )
```

```python
import jax
import jax.numpy as jnp
from jax import lax
from jax.experimental import pallas as pl
from jax.experimental.pallas import tpu as pltpu
from jax.sharding import Mesh, PartitionSpec as P

D = 768
H = 384
TOK = 256
NR = 128
DH = 64
ZN, XN, YN = 8, 4, 2
ZR = 48
HALF_ROOT = 0.7071067811865476
LOG2E = 1.4426950408889634
VMEM = 56 * 1024 * 1024
F32 = jnp.float32
BF16 = jnp.bfloat16


def dot(a, b):
    return lax.dot_general(a, b, (((1,), (0,)), ((), ())), preferred_element_type=F32)


def dot_nt(a, b):
    return lax.dot_general(a, b, (((1,), (1,)), ((), ())), preferred_element_type=F32)


def dot_tn(a, b):
    return lax.dot_general(a, b, (((0,), (0,)), ((), ())), preferred_element_type=F32)


def iota(shape, axis):
    return lax.broadcasted_iota(jnp.int32, shape, axis)


def pair_matrix(rows, cols, valid):
    r, k = iota((rows, cols), 0), iota((rows, cols), 1)
    return (((k >> 1) == r) & (r < valid)).astype(BF16)


def coarsen(node, rows=None, valid=None):
    rows = node.shape[0] // 2 if rows is None else rows
    valid = rows if valid is None else valid
    return (dot(pair_matrix(rows, node.shape[0], valid), node) * HALF_ROOT).astype(BF16)


def spread(grad, rows, valid=None):
    height = grad.shape[0]
    r, k = iota((rows, 2 * height), 0), iota((rows, 2 * height), 1)
    hot = (r >> 1) == (k & (height - 1))
    if valid is not None:
        hot = hot & (r < valid)
    high = grad.astype(BF16)
    low = (grad - high.astype(F32)).astype(BF16)
    return dot(hot.astype(BF16), jnp.concatenate([high, low], axis=0)) * HALF_ROOT


def whole(*shape):
    return pl.BlockSpec(shape, lambda *_: (0,) * len(shape))


def call(body, grid, ins, outs, scratch=()):
    return pl.pallas_call(
        body,
        grid_spec=pltpu.PrefetchScalarGridSpec(
            num_scalar_prefetch=1,
            grid=grid,
            in_specs=ins,
            out_specs=[s for s, _ in outs],
            scratch_shapes=list(scratch),
        ),
        out_shape=[jax.ShapeDtypeStruct(shape, kind) for _, (shape, kind) in outs],
        compiler_params=pltpu.CompilerParams(vmem_limit_bytes=VMEM),
    )


def tree_body(pos, x_own, x_oth, wk, wv, kv_out, n1_out, n2_out, zs_out):
    c, z = pos[0], pos[1]
    for e, x in ((c, x_own), (1 - c, x_oth)):
        kv_out[e, 0] = dot(x[...], wk[...]).astype(BF16)
        kv_out[e, 1] = dot(x[...], wv[...]).astype(BF16)
    blank = jnp.zeros((16, H), BF16)
    for p in range(2):
        for e in range(2):
            n1_out[e, p] = coarsen(kv_out[e, p])
            n2_out[p, e * 64 : (e + 1) * 64] = coarsen(n1_out[e, p])
        n5 = coarsen(coarsen(coarsen(n2_out[p])))
        n6 = coarsen(n5, 16, 8)
        n7 = coarsen(n6, 16, 4)
        zs_out[z, p] = blank
        zs_out[z ^ 1, p] = n5
        for far in (2, 3):
            zs_out[z ^ far, p] = n6
        for far in (4, 5, 6, 7):
            zs_out[z ^ far, p] = n7


def tree(pos, x_own, x_oth, w_qkv):
    col = lambda part: pl.BlockSpec((D, H), lambda i, s: (0, 2 * part + s[0]))
    outs = [(2, 2, TOK, H), (2, 2, NR, H), (2, NR, H), (ZN, 2, 16, H)]
    return call(
        tree_body,
        (1,),
        [whole(TOK, D)] * 2 + [col(1), col(2)],
        [(whole(*shape), (shape, BF16)) for shape in outs],
    )(pos, x_own, x_oth, w_qkv, w_qkv)


def project_body(pos, x_own, x_oth, ct_own, ct_oth, wq, wo, perm, q_out, ag_out, xt_out):
    c = pos[0]
    for e, x, ct in ((c, x_own, ct_own), (1 - c, x_oth, ct_oth)):
        q_out[e] = dot(x[...], wq[...]).astype(BF16)
        ag_out[e] = dot_nt(ct[...], wo[...]).astype(BF16)
        xt_out[e] = dot_nt(perm[...], x[...]).astype(BF16)


def project(pos, x_own, x_oth, ct_own, ct_oth, w_qkv, w_out, perm):
    outs = [(2, TOK, H), (2, TOK, H), (2, D, TOK)]
    return call(
        project_body,
        (1,),
        [whole(TOK, D)] * 4
        + [pl.BlockSpec((D, H), lambda i, s: (0, s[0])), pl.BlockSpec((H, D), lambda i, s: (s[0], 0)), whole(D, D)],
        [(whole(*shape), (shape, BF16)) for shape in outs],
    )(pos, x_own, x_oth, ct_own, ct_oth, w_qkv, w_out, perm)


def pair_body(pos, own, oth, near_out, far_out):
    y = pos[2] & 1
    for p in range(2):
        for half, n2 in ((y, own), (1 - y, oth)):
            near_out[half, p] = coarsen(n2[p])
            far_out[half, p] = coarsen(near_out[half, p])


def pair_nodes(pos, own, oth):
    outs = [(2, 2, 64, H), (2, 2, 32, H)]
    return call(
        pair_body, (1,), [whole(2, NR, H)] * 2, [(whole(*shape), (shape, BF16)) for shape in outs]
    )(pos, own, oth)


def pair_back_body(pos, near, far_a, far_b, dy, keep_out, send_out):
    y = pos[2] & 1
    for p in range(2):
        for half, out in ((y, None), (1 - y, send_out)):
            grad = near[half, p].astype(F32) + spread(far_a[half, p].astype(F32) + far_b[half, p].astype(F32), 64)
            if out is None:
                keep_out[p] = grad
            else:
                out[p] = (dy[p].astype(F32) + spread(grad, NR)).astype(BF16)


def pair_back(pos, near, far_a, far_b, dy):
    return call(
        pair_back_body,
        (1,),
        [whole(2, 2, 64, H), whole(2, 2, 32, H), whole(2, 2, 32, H), whole(2, NR, H)],
        [(whole(2, 64, H), ((2, 64, H), F32)), (whole(2, NR, H), ((2, NR, H), BF16))],
    )(pos, near, far_a, far_b, dy)


def z_source(z, rows_axis, shape):
    i = iota(shape, rows_axis)
    near = 16 * (z ^ 1) + i
    mid = 16 * (z ^ (2 + ((i - 16) >> 3))) + ((i - 16) & 7)
    far = 16 * (z ^ (4 + ((i - 32) >> 2))) + ((i - 32) & 3)
    return jnp.where(i < 16, near, jnp.where(i < 32, mid, far))


def plane_body(pos, zr, out):
    hot = (iota((ZR, 128), 1) == z_source(pos[1], 0, (ZR, 128))).astype(BF16)
    for p in range(2):
        rows = dot(hot, zr[:, p].reshape(128, H)).astype(BF16)
        for slot in range(8):
            out[slot, p] = rows


def plane_slots(pos, zr):
    return call(
        plane_body,
        (1,),
        [whole(ZN, 2, 16, H)],
        [(whole(8, 2, ZR, H), ((8, 2, ZR, H), BF16))],
    )(pos, zr)[0]


def attention_body(pos, q, ag, kv, n1, yr, near, far_a, far_b, xr, att_out, dq_out, dkv_out, dn1_out, dy_out, dnear_out, dfar_a_out, dfar_b_out, dx_out, keys, s_ref, dw_ref, w_ref, ds_ref, drem):
    for p in range(2):
        for e in range(2):
            keys[e, p, :256] = kv[e, p]
            keys[e, p, 256:384] = n1[1 - e, p]
            keys[e, p, 384:512] = yr[p]
            for half in range(2):
                start = 512 + 64 * half
                keys[e, p, start : start + 64] = near[half, p]
                start = 640 + 32 * half
                keys[e, p, start : start + 32] = far_a[half, p]
                start = 704 + 32 * half
                keys[e, p, start : start + 32] = far_b[half, p]
            for slot in range(8):
                start = 768 + ZR * slot
                keys[e, p, start : start + ZR] = xr[slot, p]
    lane = iota((TOK, 128), 1)
    for e in range(2):
        att_t, dq_t = [], []
        dk = dv = None
        for h in range(2):
            mine = (lane >> 6) == h
            qh = jnp.where(mine, q[e], jnp.zeros((), BF16))
            ah = jnp.where(mine, ag[e], jnp.zeros((), BF16))
            s_ref[...] = dot_nt(keys[e, 0], qh)
            dw_ref[...] = dot_nt(keys[e, 1], ah)
            top = jnp.max(s_ref[...], axis=0, keepdims=True)
            s_ref[...] = jnp.exp2((s_ref[...] - top) * (LOG2E * DH ** -0.5))
            total = jnp.sum(s_ref[...], axis=0, keepdims=True)
            inverse = 1.0 / total
            delta = jnp.sum(s_ref[...] * dw_ref[...], axis=0, keepdims=True) * inverse
            prob = s_ref[...] * inverse
            w_ref[...] = prob.astype(BF16)
            ds_ref[...] = (prob * (dw_ref[...] - delta) * DH ** -0.5).astype(BF16)
            att_t.append(dot_tn(keys[e, 1], w_ref[...])[64 * h : 64 * h + 64])
            dq_t.append(dot_tn(keys[e, 0], ds_ref[...])[64 * h : 64 * h + 64])
            dkh, dvh = dot(ds_ref[...], qh), dot(w_ref[...], ah)
            dk = dkh if dk is None else dk + dkh
            dv = dvh if dv is None else dv + dvh
        att_out[e] = jnp.concatenate(att_t, axis=0).T.astype(BF16)
        dq_out[e] = jnp.concatenate(dq_t, axis=0).T.astype(BF16)
        for p, grad in ((0, dk), (1, dv)):
            dkv_out[e, p] = grad[:256]
            dn1_out[1 - e, p] = grad[256:384]
            if e == 0:
                drem[p] = grad[384:]
            else:
                drem[p] = drem[p] + grad[384:]
    for p in range(2):
        rows = drem[p].astype(BF16)
        dy_out[p] = rows[:128]
        for half in range(2):
            start = 128 + 64 * half
            dnear_out[half, p] = rows[start : start + 64]
            start = 256 + 32 * half
            dfar_a_out[half, p] = rows[start : start + 32]
            start = 320 + 32 * half
            dfar_b_out[half, p] = rows[start : start + 32]
        for slot in range(8):
            start = 384 + ZR * slot
            dx_out[slot, p] = rows[start : start + ZR]


def attention(pos, q, ag, kv, n1, yr, near, far_a, far_b, xr):
    def cut(*lead):
        return pl.BlockSpec(lead + (128,), lambda i, s: (0,) * len(lead) + (i,))

    outs = [
        ((2, TOK), BF16), ((2, TOK), BF16), ((2, 2, TOK), F32), ((2, 2, NR), F32), ((2, NR), BF16),
        ((2, 2, 64), BF16), ((2, 2, 32), BF16), ((2, 2, 32), BF16), ((8, 2, ZR), BF16),
    ]
    n = 1152
    return call(
        attention_body,
        (H // 128,),
        [cut(2, TOK), cut(2, TOK), cut(2, 2, TOK), cut(2, 2, NR), cut(2, NR), cut(2, 2, 64), cut(2, 2, 32), cut(2, 2, 32), cut(8, 2, ZR)],
        [(cut(*lead), (lead + (H,), kind)) for lead, kind in outs],
        [
            pltpu.VMEM((2, 2, n, 128), BF16), pltpu.VMEM((n, TOK), F32), pltpu.VMEM((n, TOK), F32),
            pltpu.VMEM((n, TOK), BF16), pltpu.VMEM((n, TOK), BF16), pltpu.VMEM((2, 768, 128), F32),
        ],
    )(pos, q, ag, kv, n1, yr, near, far_a, far_b, xr)


def output_body(pos, att_own, att_oth, ct_own, ct_oth, dq, xt, w_own, w_oth, p_own, p_oth, out, grad_out):
    c = pos[0]
    total = dot(xt[0], dq[0]) + dot(xt[1], dq[1])
    grad_out[:, 0] = total.astype(BF16).reshape(8, 96, H)
    total = None
    for e, ct in ((c, ct_own), (1 - c, ct_oth)):
        att_t = (dot_nt(p_own[...], att_own[e]) + dot_nt(p_oth[...], att_oth[e])).astype(BF16)
        term = dot(att_t, ct[...])
        total = term if total is None else total + term
    grad_out[:, 1] = total.astype(BF16).reshape(8, 96, H)
    out[...] = (dot(att_own[c], w_own[...]) + dot(att_oth[c], w_oth[...])).astype(BF16)


def output_side(pos, att_own, att_oth, ct_own, ct_oth, dq, xt, w_out, perm):
    row = lambda flip: pl.BlockSpec((H, D), lambda i, s: (s[0] ^ flip, 0))
    col = lambda flip, rows: pl.BlockSpec((rows, H), lambda i, s: (0, s[0] ^ flip))
    return call(
        output_body,
        (1,),
        [whole(2, TOK, H)] * 2 + [col(0, TOK)] * 2 + [whole(2, TOK, H), whole(2, D, TOK)] + [row(0), row(1), col(0, D), col(1, D)],
        [(whole(TOK, D), ((TOK, D), BF16)), (whole(8, 2, 96, H), ((8, 2, 96, H), BF16))],
    )(pos, att_own, att_oth, ct_own, ct_oth, dq, xt, w_out, w_out, perm, perm)


def back_body(pos, xr, out):
    hot = (iota((128, ZR), 0) == z_source(pos[1], 1, (128, ZR))).astype(BF16)
    for p in range(2):
        total = xr[0, p].astype(F32)
        for slot in range(1, 8):
            total = total + xr[slot, p].astype(F32)
        out[:, p] = dot(hot, total.astype(BF16)).astype(BF16).reshape(8, 16, H)


def back_slots(pos, xr):
    return call(
        back_body,
        (1,),
        [whole(8, 2, ZR, H)],
        [(whole(ZN, 2, 16, H), ((ZN, 2, 16, H), BF16))],
    )(pos, xr)[0]


def leaf_body(pos, zr, keep, yr, dn1, dkv, dq, xt, pg_out, grad_out):
    z = pos[1]

    def gather(ref, index, fars, p, rows):
        total = None
        for far in fars:
            term = ref[index ^ far, p, :rows].astype(F32)
            total = term if total is None else total + term
        return total

    for p in range(2):
        g7 = gather(zr, z, (4, 5, 6, 7), p, 16)
        g6 = gather(zr, z, (2, 3), p, 16) + spread(g7, 16, 8)
        g5 = gather(zr, z, (1,), p, 16) + spread(g6, 16)
        g3 = keep[p] + spread(spread(g5, 32), 64)
        g2 = yr[p].astype(F32) + spread(g3, 128)
        for e in range(2):
            g1 = dn1[e, p] + spread(g2[64 * e : 64 * e + 64], 128)
            leaf = dkv[e, p] + spread(g1, 256)
            pg_out[e, :, H * (1 + p) : H * (2 + p)] = leaf.astype(BF16)
        cols = slice(H * (1 + p), H * (2 + p))
        total = dot(xt[0], pg_out[0, :, cols]) + dot(xt[1], pg_out[1, :, cols])
        grad_out[:, p] = total.astype(BF16).reshape(8, 96, H)
    for e in range(2):
        pg_out[e, :, :H] = dq[e]


def leaf_grads(pos, zr, keep, yr, dn1, dkv, dq, xt):
    return call(
        leaf_body,
        (1,),
        [
            whole(ZN, 2, 16, H), whole(2, 64, H), whole(2, NR, H), whole(2, 2, NR, H), whole(2, 2, TOK, H),
            whole(2, TOK, H), whole(2, D, TOK),
        ],
        [
            (whole(2, TOK, 3 * H), ((2, TOK, 3 * H), BF16)),
            (whole(8, 2, 96, H), ((8, 2, 96, H), BF16)),
        ],
    )(pos, zr, keep, yr, dn1, dkv, dq, xt)


def input_body(pos, pg_own, pg_oth, *rest):
    out = rest[-1]
    total = None
    for part in range(3):
        for pg, w in ((pg_own, rest[part]), (pg_oth, rest[3 + part])):
            term = dot_nt(pg[:, H * part : H * part + H], w[...])
            total = term if total is None else total + term
    out[...] = total.astype(BF16)


def input_side(pos, pg_own, pg_oth, w_qkv):
    col = lambda part, flip: pl.BlockSpec((D, H), lambda i, s: (0, 2 * part + (s[0] ^ flip)))
    return call(
        input_body,
        (1,),
        [whole(TOK, 3 * H)] * 2 + [col(part, flip) for flip in (0, 1) for part in range(3)],
        [(whole(TOK, D), ((TOK, D), BF16))],
    )(pos, pg_own, pg_oth, *[w_qkv] * 6)[0]


def total_of(ref):
    total = ref[0].astype(F32)
    for slot in range(1, ref.shape[0]):
        total = total + ref[slot].astype(F32)
    return total


def middle_body(pos, first, second, out):
    i, k = iota((256, 96), 0), iota((256, 96), 1)
    row, half = i & 7, (i >> 3) & 1
    hit = (k == 6 * (i >> 4) + row) & (row < 6)
    rows = dot((hit & (half == 0)).astype(BF16), first[...])
    rows = rows + dot((hit & (half == 1)).astype(BF16), total_of(second).astype(BF16))
    rows = rows.astype(BF16).reshape(ZN, 2, 16, H)
    for copy in range(2):
        out[:, :, copy] = rows


def middle_sum(pos, first, second):
    shape = (ZN, 2, 2, 16, H)
    return call(middle_body, (1,), [whole(96, H), whole(16, 96, H)], [(whole(*shape), (shape, BF16))])(pos, first, second)[0]


def last_body(pos, terms, qkv_out, out_out):
    for core in range(2):
        for dp in range(2):
            total = terms[0, core, dp].astype(F32)
            for z in range(1, ZN):
                total = total + terms[z, core, dp].astype(F32)
            if dp == 0:
                qkv_out[:, H * core : H * core + H] = total[:6]
            else:
                out_out[:, H * core : H * core + H] = total[:6]
            start = D * (1 + dp) + H * core
            qkv_out[:, start : start + H] = total[8:14]


def last_sum(pos, terms):
    return call(
        last_body,
        (1,),
        [whole(ZN, 2, 2, 16, H)],
        [(whole(6, 3 * D), ((6, 3 * D), F32)), (whole(6, D), ((6, D), F32))],
    )(pos, terms)


def swap(value, axis):
    return lax.ppermute(value, axis, [(0, 1), (1, 0)])


def along_x(value, far):
    return lax.ppermute(value, "x", [(i, i ^ far) for i in range(XN)])


def shards(x_tokens, cotangent, w_qkv, w_out):
    x_own, ct_own = x_tokens[0], cotangent[0]
    c, z = lax.axis_index("c"), lax.axis_index("z")
    j = 2 * lax.axis_index("x") + lax.axis_index("y")
    pos = jnp.stack([c, z, j]).astype(jnp.int32)
    x_oth, ct_oth = swap(x_own, "c"), swap(ct_own, "c")
    f = jnp.arange(D, dtype=jnp.int32)
    source = 96 * (f // 12 % 8) + 12 * (f // 96) + f % 12
    perm = (source[:, None] == f[None, :]).astype(BF16)

    kv, n1, n2, zs = tree(pos, x_own, x_oth, w_qkv)
    zr = lax.all_to_all(zs, "z", 0, 0)
    yr = swap(n2, "y")
    near, far = pair_nodes(pos, n2, yr)
    near, far_a, far_b = along_x(near, 1), along_x(far, 2), along_x(far, 3)
    q, ag, xt = project(pos, x_own, x_oth, ct_own, ct_oth, w_qkv, w_out, perm)
    zr, q, ag, xt, near, far_a, far_b = lax.optimization_barrier((zr, q, ag, xt, near, far_a, far_b))
    xr = lax.all_to_all(plane_slots(pos, zr), ("x", "y"), 0, 0)
    att, dq, dkv, dn1, dy, dnear, dfar_a, dfar_b, dx = attention(pos, q, ag, kv, n1, yr, near, far_a, far_b, xr)

    dx_r = lax.all_to_all(dx, ("x", "y"), 0, 0)
    att_oth = swap(att, "c")
    keep, dy = pair_back(pos, along_x(dnear, 1), along_x(dfar_a, 2), along_x(dfar_b, 3), dy)
    dy_r = swap(dy, "y")
    layer_out, terms = output_side(pos, att, att_oth, ct_own, ct_oth, dq, xt, w_out, perm)
    first = lax.psum_scatter(terms.reshape(XN, 4, 96, H), "x", scatter_dimension=0)
    first = lax.psum_scatter(first, ("y", "dp"), scatter_dimension=0)
    dz_r = lax.all_to_all(back_slots(pos, dx_r), "z", 0, 0)
    pg, terms = leaf_grads(pos, dz_r, keep, dy_r, dn1, dkv, dq, xt)
    second = lax.all_to_all(terms.reshape(16, 96, H), ("x", "y", "dp"), 0, 0)
    pg_own = lax.dynamic_index_in_dim(pg, c, 0, keepdims=False)
    pg_oth = swap(lax.dynamic_index_in_dim(pg, 1 - c, 0, keepdims=False), "c")
    input_grad = input_side(pos, pg_own, pg_oth, w_qkv)
    second, input_grad = lax.optimization_barrier((second, input_grad))
    terms = middle_sum(pos, first, second).reshape(32, 16, H)
    terms = lax.all_to_all(terms, ("z", "c", "dp"), 0, 0)
    qkv_grad, out_grad = last_sum(pos, terms.reshape(ZN, 2, 2, 16, H))
    return (layer_out[None], input_grad[None], qkv_grad, out_grad)


def solution(mesh):
    split = Mesh(mesh.devices.reshape(ZN, XN, YN, 2, 2), ("z", "x", "y", "c", "dp"))
    seq = ("z", "x", "y", "c")
    return jax.shard_map(
        shards,
        mesh=split,
        in_specs=(P("dp", seq, None), P("dp", seq, None), P(), P()),
        out_specs=(P("dp", seq, None), P("dp", seq, None), P(seq, None), P(seq, None)),
        check_vma=False,
    )
```

```python
import jax
import jax.numpy as jnp
import numpy as np
from jax import lax
from jax.experimental import pallas as pl
from jax.experimental.pallas import tpu as pltpu
from jax.sharding import Mesh, PartitionSpec as P

D = 768
H = 384
TOK = 256
NR = 128
DH = 64
ZN, XN, YN = 8, 4, 2
ZR = 48
HALF_ROOT = 0.7071067811865476
LOG2E = 1.4426950408889634
VMEM = 56 * 1024 * 1024
F32 = jnp.float32
BF16 = jnp.bfloat16


def dot(a, b):
    return lax.dot_general(a, b, (((1,), (0,)), ((), ())), preferred_element_type=F32)


def dot_nt(a, b):
    return lax.dot_general(a, b, (((1,), (1,)), ((), ())), preferred_element_type=F32)


def dot_tn(a, b):
    return lax.dot_general(a, b, (((0,), (0,)), ((), ())), preferred_element_type=F32)


def iota(shape, axis):
    return lax.broadcasted_iota(jnp.int32, shape, axis)


def pair_matrix(rows, cols, valid):
    r, k = iota((rows, cols), 0), iota((rows, cols), 1)
    return (((k >> 1) == r) & (r < valid)).astype(BF16)


def coarsen(node, rows=None, valid=None):
    rows = node.shape[0] // 2 if rows is None else rows
    valid = rows if valid is None else valid
    return (dot(pair_matrix(rows, node.shape[0], valid), node) * HALF_ROOT).astype(BF16)


def spread(grad, rows, valid=None):
    height = grad.shape[0]
    r, k = iota((rows, 2 * height), 0), iota((rows, 2 * height), 1)
    hot = (r >> 1) == (k & (height - 1))
    if valid is not None:
        hot = hot & (r < valid)
    high = grad.astype(BF16)
    low = (grad - high.astype(F32)).astype(BF16)
    return dot(hot.astype(BF16), jnp.concatenate([high, low], axis=0)) * HALF_ROOT


def whole(*shape):
    return pl.BlockSpec(shape, lambda *_: (0,) * len(shape))


def call(body, grid, ins, outs, scratch=()):
    return pl.pallas_call(
        body,
        grid_spec=pltpu.PrefetchScalarGridSpec(
            num_scalar_prefetch=1,
            grid=grid,
            in_specs=ins,
            out_specs=[s for s, _ in outs],
            scratch_shapes=list(scratch),
        ),
        out_shape=[jax.ShapeDtypeStruct(shape, kind) for _, (shape, kind) in outs],
        compiler_params=pltpu.CompilerParams(vmem_limit_bytes=VMEM),
    )


def tree_body(pos, x_own, x_oth, wk, wv, kv_out, n1_out, n2_out, zs_out):
    c, z = pos[0], pos[1]
    for e, x in ((c, x_own), (1 - c, x_oth)):
        kv_out[e, 0] = dot(x[...], wk[...]).astype(BF16)
        kv_out[e, 1] = dot(x[...], wv[...]).astype(BF16)

    def store(ref, *index):
        def put(node):
            for p in range(2):
                ref[index + (p,)] = node[:, H * p : H * p + H]

        return put

    halves = []
    for e in range(2):
        n1 = coarsen(jnp.concatenate([kv_out[e, 0], kv_out[e, 1]], axis=1))
        store(n1_out, e)(n1)
        halves.append(coarsen(n1))
    n2 = jnp.concatenate(halves, axis=0)
    store(n2_out)(n2)
    n5 = coarsen(coarsen(coarsen(n2)))
    n6 = coarsen(n5, 16, 8)
    n7 = coarsen(n6, 16, 4)
    store(zs_out, z)(jnp.zeros_like(n5))
    store(zs_out, z ^ 1)(n5)
    for far in (2, 3):
        store(zs_out, z ^ far)(n6)
    for far in (4, 5, 6, 7):
        store(zs_out, z ^ far)(n7)


def tree(pos, x_own, x_oth, w_qkv):
    col = lambda part: pl.BlockSpec((D, H), lambda i, s: (0, 2 * part + s[0]))
    outs = [(2, 2, TOK, H), (2, 2, NR, H), (2, NR, H), (ZN, 2, 16, H)]
    return call(
        tree_body,
        (1,),
        [whole(TOK, D)] * 2 + [col(1), col(2)],
        [(whole(*shape), (shape, BF16)) for shape in outs],
    )(pos, x_own, x_oth, w_qkv, w_qkv)


def project_body(pos, x_own, x_oth, ct_own, ct_oth, wq, wo, perm, q_out, ag_out, xt_out):
    c = pos[0]
    for e, x, ct in ((c, x_own, ct_own), (1 - c, x_oth, ct_oth)):
        q_out[e] = dot(x[...], wq[...]).astype(BF16)
        ag_out[e] = dot_nt(ct[...], wo[...]).astype(BF16)
        xt_out[e] = dot_nt(perm[...], x[...]).astype(BF16)


def project(pos, x_own, x_oth, ct_own, ct_oth, w_qkv, w_out, perm):
    outs = [(2, TOK, H), (2, TOK, H), (2, D, TOK)]
    return call(
        project_body,
        (1,),
        [whole(TOK, D)] * 4
        + [pl.BlockSpec((D, H), lambda i, s: (0, s[0])), pl.BlockSpec((H, D), lambda i, s: (s[0], 0)), whole(D, D)],
        [(whole(*shape), (shape, BF16)) for shape in outs],
    )(pos, x_own, x_oth, ct_own, ct_oth, w_qkv, w_out, perm)


def pair_body(pos, own, oth, near_out, far_out):
    y = pos[2] & 1
    for p in range(2):
        for half, n2 in ((y, own), (1 - y, oth)):
            near_out[half, p] = coarsen(n2[p])
            far_out[half, p] = coarsen(near_out[half, p])


def pair_nodes(pos, own, oth):
    outs = [(2, 2, 64, H), (2, 2, 32, H)]
    return call(
        pair_body, (1,), [whole(2, NR, H)] * 2, [(whole(*shape), (shape, BF16)) for shape in outs]
    )(pos, own, oth)


def pair_back_body(pos, near, far_a, far_b, dy, keep_out, send_out):
    y = pos[2] & 1
    for p in range(2):
        for half, out in ((y, None), (1 - y, send_out)):
            grad = near[half, p].astype(F32) + spread(far_a[half, p].astype(F32) + far_b[half, p].astype(F32), 64)
            if out is None:
                keep_out[p] = grad
            else:
                out[p] = (dy[p].astype(F32) + spread(grad, NR)).astype(BF16)


def pair_back(pos, near, far_a, far_b, dy):
    return call(
        pair_back_body,
        (1,),
        [whole(2, 2, 64, H), whole(2, 2, 32, H), whole(2, 2, 32, H), whole(2, NR, H)],
        [(whole(2, 64, H), ((2, 64, H), F32)), (whole(2, NR, H), ((2, NR, H), BF16))],
    )(pos, near, far_a, far_b, dy)


def z_source(z, rows_axis, shape):
    i = iota(shape, rows_axis)
    near = 16 * (z ^ 1) + i
    mid = 16 * (z ^ (2 + ((i - 16) >> 3))) + ((i - 16) & 7)
    far = 16 * (z ^ (4 + ((i - 32) >> 2))) + ((i - 32) & 3)
    return jnp.where(i < 16, near, jnp.where(i < 32, mid, far))


def plane_body(pos, zr, out):
    hot = (iota((ZR, 128), 1) == z_source(pos[1], 0, (ZR, 128))).astype(BF16)
    both = jnp.concatenate([zr[:, p].reshape(128, H) for p in range(2)], axis=1)
    rows = dot(hot, both).astype(BF16)
    for slot in range(8):
        for p in range(2):
            out[slot, p] = rows[:, H * p : H * p + H]


def plane_slots(pos, zr):
    return call(
        plane_body,
        (1,),
        [whole(ZN, 2, 16, H)],
        [(whole(8, 2, ZR, H), ((8, 2, ZR, H), BF16))],
    )(pos, zr)[0]


def attention_body(pos, q, ag, kv, n1, yr, near, far_a, far_b, xr, att_out, dq_out, dkv_out, dn1_out, dy_out, dnear_out, dfar_a_out, dfar_b_out, dx_out, keys, s_ref, dw_ref, w_ref, ds_ref, drem):
    for p in range(2):
        for e in range(2):
            keys[e, p, :256] = kv[e, p]
            keys[e, p, 256:384] = n1[1 - e, p]
            keys[e, p, 384:512] = yr[p]
            for half in range(2):
                start = 512 + 64 * half
                keys[e, p, start : start + 64] = near[half, p]
                start = 640 + 32 * half
                keys[e, p, start : start + 32] = far_a[half, p]
                start = 704 + 32 * half
                keys[e, p, start : start + 32] = far_b[half, p]
            for slot in range(8):
                start = 768 + ZR * slot
                keys[e, p, start : start + ZR] = xr[slot, p]
    lane = iota((TOK, 128), 1)
    for e in range(2):
        att_t, dq_t = [], []
        dk = dv = None
        for h in range(2):
            mine = (lane >> 6) == h
            qh = jnp.where(mine, q[e], jnp.zeros((), BF16))
            ah = jnp.where(mine, ag[e], jnp.zeros((), BF16))
            s_ref[...] = dot_nt(keys[e, 0], qh)
            dw_ref[...] = dot_nt(keys[e, 1], ah)
            top = jnp.max(s_ref[...], axis=0, keepdims=True)
            s_ref[...] = jnp.exp2((s_ref[...] - top) * (LOG2E * DH ** -0.5))
            total = jnp.sum(s_ref[...], axis=0, keepdims=True)
            inverse = 1.0 / total
            delta = jnp.sum(s_ref[...] * dw_ref[...], axis=0, keepdims=True) * inverse
            prob = s_ref[...] * inverse
            w_ref[...] = prob.astype(BF16)
            ds_ref[...] = (prob * (dw_ref[...] - delta) * DH ** -0.5).astype(BF16)
            att_t.append(dot_tn(keys[e, 1], w_ref[...])[64 * h : 64 * h + 64])
            dq_t.append(dot_tn(keys[e, 0], ds_ref[...])[64 * h : 64 * h + 64])
            dkh, dvh = dot(ds_ref[...], qh), dot(w_ref[...], ah)
            dk = dkh if dk is None else dk + dkh
            dv = dvh if dv is None else dv + dvh
        att_out[e] = jnp.concatenate(att_t, axis=0).T.astype(BF16)
        dq_out[e] = jnp.concatenate(dq_t, axis=0).T.astype(BF16)
        for p, grad in ((0, dk), (1, dv)):
            dkv_out[e, p] = grad[:256]
            dn1_out[1 - e, p] = grad[256:384]
            if e == 0:
                drem[p] = grad[384:]
            else:
                drem[p] = drem[p] + grad[384:]
    for p in range(2):
        rows = drem[p].astype(BF16)
        dy_out[p] = rows[:128]
        for half in range(2):
            start = 128 + 64 * half
            dnear_out[half, p] = rows[start : start + 64]
            start = 256 + 32 * half
            dfar_a_out[half, p] = rows[start : start + 32]
            start = 320 + 32 * half
            dfar_b_out[half, p] = rows[start : start + 32]
        for slot in range(8):
            start = 384 + ZR * slot
            dx_out[slot, p] = rows[start : start + ZR]


def attention(pos, q, ag, kv, n1, yr, near, far_a, far_b, xr):
    def cut(*lead):
        return pl.BlockSpec(lead + (128,), lambda i, s: (0,) * len(lead) + (i,))

    outs = [
        ((2, TOK), BF16), ((2, TOK), BF16), ((2, 2, TOK), F32), ((2, 2, NR), F32), ((2, NR), BF16),
        ((2, 2, 64), BF16), ((2, 2, 32), BF16), ((2, 2, 32), BF16), ((8, 2, ZR), BF16),
    ]
    n = 1152
    return call(
        attention_body,
        (H // 128,),
        [cut(2, TOK), cut(2, TOK), cut(2, 2, TOK), cut(2, 2, NR), cut(2, NR), cut(2, 2, 64), cut(2, 2, 32), cut(2, 2, 32), cut(8, 2, ZR)],
        [(cut(*lead), (lead + (H,), kind)) for lead, kind in outs],
        [
            pltpu.VMEM((2, 2, n, 128), BF16), pltpu.VMEM((n, TOK), F32), pltpu.VMEM((n, TOK), F32),
            pltpu.VMEM((n, TOK), BF16), pltpu.VMEM((n, TOK), BF16), pltpu.VMEM((2, 768, 128), F32),
        ],
    )(pos, q, ag, kv, n1, yr, near, far_a, far_b, xr)


def output_body(pos, att_own, att_oth, ct_own, ct_oth, dq, xt, w_own, w_oth, p_own, p_oth, out, *rest):
    c, x = pos[0], pos[2] >> 1
    slots = rest[-1]
    total = dot(xt[0], dq[0]) + dot(xt[1], dq[1])
    slots[:, :, 0] = total.astype(BF16).reshape(XN, YN, 96, H)
    total = None
    for e, ct in ((c, ct_own), (1 - c, ct_oth)):
        att_t = (dot_nt(p_own[...], att_own[e]) + dot_nt(p_oth[...], att_oth[e])).astype(BF16)
        term = dot(att_t, ct[...])
        total = term if total is None else total + term
    slots[:, :, 1] = total.astype(BF16).reshape(XN, YN, 96, H)
    for far in range(XN):
        rest[far][...] = slots[x ^ far]
    out[...] = (dot(att_own[c], w_own[...]) + dot(att_oth[c], w_oth[...])).astype(BF16)


def output_side(pos, att_own, att_oth, ct_own, ct_oth, dq, xt, w_out, perm):
    row = lambda flip: pl.BlockSpec((H, D), lambda i, s: (s[0] ^ flip, 0))
    col = lambda flip, rows: pl.BlockSpec((rows, H), lambda i, s: (0, s[0] ^ flip))
    slot = (YN, 2, 96, H)
    return call(
        output_body,
        (1,),
        [whole(2, TOK, H)] * 2 + [col(0, TOK)] * 2 + [whole(2, TOK, H), whole(2, D, TOK)] + [row(0), row(1), col(0, D), col(1, D)],
        [(whole(TOK, D), ((TOK, D), BF16))] + [(whole(*slot), (slot, BF16))] * XN,
        [pltpu.VMEM((XN,) + slot, BF16)],
    )(pos, att_own, att_oth, ct_own, ct_oth, dq, xt, w_out, w_out, perm, perm)


def x_sum_body(pos, t0, t1, t2, t3, *rest):
    y, dp = pos[2] & 1, pos[3]
    slots = rest[-1]
    total = (t0[...].astype(F32) + t1[...].astype(F32)) + (t2[...].astype(F32) + t3[...].astype(F32))
    slots[...] = total.astype(BF16)
    for far in range(4):
        rest[far][...] = slots[y ^ (far >> 1), dp ^ (far & 1)]


def x_sum(pos, *terms):
    shape = (YN, 2, 96, H)
    return call(
        x_sum_body,
        (1,),
        [whole(*shape)] * 4,
        [(whole(96, H), ((96, H), BF16))] * 4,
        [pltpu.VMEM(shape, BF16)],
    )(pos, *terms)


def back_body(pos, xr, out):
    hot = (iota((128, ZR), 0) == z_source(pos[1], 1, (128, ZR))).astype(BF16)
    for p in range(2):
        total = xr[0, p].astype(F32)
        for slot in range(1, 8):
            total = total + xr[slot, p].astype(F32)
        out[:, p] = dot(hot, total.astype(BF16)).astype(BF16).reshape(8, 16, H)


def back_slots(pos, xr):
    return call(
        back_body,
        (1,),
        [whole(8, 2, ZR, H)],
        [(whole(ZN, 2, 16, H), ((ZN, 2, 16, H), BF16))],
    )(pos, xr)[0]


def base_body(pos, dkv, dn1, yr, keep, out):
    def hot(rows, width, shift, start):
        r, k = iota((rows, width), 0), iota((rows, width), 1)
        return (((r >> shift) + start) == (k & (NR - 1 if width > NR else width - 1))).astype(BF16)

    def split(grad):
        high = grad.astype(BF16)
        return high, (grad - high.astype(F32)).astype(BF16)

    for p in range(2):
        keep_high, keep_low = split(keep[p])
        for e in range(2):
            total = dkv[e, p] + dot(hot(TOK, 2 * NR, 1, 0), jnp.concatenate(split(dn1[e, p]), axis=0)) * HALF_ROOT
            total = total + dot(hot(TOK, NR, 2, 64 * e), yr[p]) * 0.5
            up = hot(TOK, 64, 3, 32 * e)
            out[e, p] = total + (dot(up, keep_high) + dot(up, keep_low)) * (0.5 * HALF_ROOT)


def base_grads(pos, dkv, dn1, yr, keep):
    shape = (2, 2, TOK, H)
    return call(
        base_body,
        (1,),
        [whole(*shape), whole(2, 2, NR, H), whole(2, NR, H), whole(2, 64, H)],
        [(whole(*shape), (shape, F32))],
    )(pos, dkv, dn1, yr, keep)[0]


def leaf_body(pos, zr, base, dq, xt, pg_out, grad_out):
    t, k = iota((2 * TOK, 128), 0), iota((2 * TOK, 128), 1)
    far, row = (k >> 4) ^ pos[1], k & 15
    odd = jnp.where((far == 1) & (row == t >> 5), 0.25, jnp.where((far >= 4) & (row == t >> 7), 0.125, 0.0)).astype(BF16)
    even = jnp.where(((far >> 1) == 1) & (row == t >> 6), 0.125, 0.0).astype(BF16)
    both = jnp.concatenate([zr[:, p].reshape(128, H) for p in range(2)], axis=1)
    up = dot(odd, both) * HALF_ROOT + dot(even, both)
    for p in range(2):
        cols = slice(H * (1 + p), H * (2 + p))
        total = None
        for e in range(2):
            leaf = (base[e, p] + up[TOK * e : TOK * e + TOK, H * p : H * p + H]).astype(BF16)
            pg_out[e, :, cols] = leaf
            term = dot(xt[e], leaf)
            total = term if total is None else total + term
        grad_out[:, p] = total.astype(BF16).reshape(8, 96, H)
    for e in range(2):
        pg_out[e, :, :H] = dq[e]


def leaf_grads(pos, zr, base, dq, xt):
    return call(
        leaf_body,
        (1,),
        [whole(ZN, 2, 16, H), whole(2, 2, TOK, H), whole(2, TOK, H), whole(2, D, TOK)],
        [
            (whole(2, TOK, 3 * H), ((2, TOK, 3 * H), BF16)),
            (whole(8, 2, 96, H), ((8, 2, 96, H), BF16)),
        ],
    )(pos, zr, base, dq, xt)


def input_body(pos, pg_own, pg_oth, *rest):
    out = rest[-1]
    total = None
    for part in range(3):
        for pg, w in ((pg_own, rest[part]), (pg_oth, rest[3 + part])):
            term = dot_nt(pg[:, H * part : H * part + H], w[...])
            total = term if total is None else total + term
    out[...] = total.astype(BF16)


def input_side(pos, pg_own, pg_oth, w_qkv):
    col = lambda part, flip: pl.BlockSpec((D, H), lambda i, s: (0, 2 * part + (s[0] ^ flip)))
    return call(
        input_body,
        (1,),
        [whole(TOK, 3 * H)] * 2 + [col(part, flip) for flip in (0, 1) for part in range(3)],
        [(whole(TOK, D), ((TOK, D), BF16))],
    )(pos, pg_own, pg_oth, *[w_qkv] * 6)[0]


def total_of(refs):
    total = refs[0].astype(F32)
    for ref in refs[1:]:
        total = total + ref.astype(F32)
    return total


def middle_body(pos, f0, f1, f2, f3, second, out):
    first = total_of([f0[...], f1[...], f2[...], f3[...]]).astype(BF16)
    i, k = iota((256, 96), 0), iota((256, 96), 1)
    row, half = i & 7, (i >> 3) & 1
    hit = (k == 6 * (i >> 4) + row) & (row < 6)
    rows = dot((hit & (half == 0)).astype(BF16), first)
    rows = rows + dot((hit & (half == 1)).astype(BF16), total_of([second[slot] for slot in range(16)]).astype(BF16))
    out[...] = rows.astype(BF16).reshape(ZN, 2, 16, H)


def middle_sum(pos, firsts, second):
    shape = (ZN, 2, 16, H)
    return call(
        middle_body, (1,), [whole(96, H)] * 4 + [whole(16, 96, H)], [(whole(*shape), (shape, BF16))]
    )(pos, *firsts, second)[0]


def z_sum_body(pos, terms, own_out, oth_out):
    for core, out in ((pos[0], own_out), (1 - pos[0], oth_out)):
        out[...] = total_of([terms[z, core] for z in range(ZN)]).astype(BF16)


def z_sum(pos, terms):
    return call(
        z_sum_body,
        (1,),
        [whole(ZN, 2, 16, H)],
        [(whole(16, H), ((16, H), BF16))] * 2,
    )(pos, terms)


def last_body(pos, own, from_dp, from_core, from_both, qkv_out, out_out, parts):
    core, dp = pos[0], pos[3]
    parts[core, dp] = own[...]
    parts[core, 1 - dp] = from_dp[...]
    parts[1 - core, dp] = from_core[...]
    parts[1 - core, 1 - dp] = from_both[...]
    for core in range(2):
        low, high = parts[core, 0].astype(F32), parts[core, 1].astype(F32)
        cols = lambda part: slice(D * part + H * core, D * part + H * core + H)
        qkv_out[:, cols(0)] = low[:6]
        qkv_out[:, cols(1)] = low[8:14]
        qkv_out[:, cols(2)] = high[8:14]
        out_out[:, cols(0)] = high[:6]


def last_rows(pos, *parts):
    return call(
        last_body,
        (1,),
        [whole(16, H)] * 4,
        [(whole(6, 3 * D), ((6, 3 * D), F32)), (whole(6, D), ((6, D), F32))],
        [pltpu.VMEM((2, 2, 16, H), BF16)],
    )(pos, *parts)


def swap(value, axis):
    return lax.ppermute(value, axis, [(0, 1), (1, 0)])


def along(value, axes, far, count=4):
    return lax.ppermute(value, axes, [(i, i ^ far) for i in range(count)])


def row_order():
    f = np.arange(D)
    source = 96 * (f // 12 % 8) + 12 * (f // 96) + f % 12
    return jnp.asarray(source[:, None] == f[None, :], BF16)


def shards(x_tokens, cotangent, w_qkv, w_out):
    x_own, ct_own = x_tokens[0], cotangent[0]
    c, z, dp = lax.axis_index("c"), lax.axis_index("z"), lax.axis_index("dp")
    j = 2 * lax.axis_index("x") + lax.axis_index("y")
    pos = jnp.stack([c, z, j, dp]).astype(jnp.int32)
    x_oth, ct_oth = swap(x_own, "c"), swap(ct_own, "c")
    perm = row_order()

    kv, n1, n2, zs = tree(pos, x_own, x_oth, w_qkv)
    zr = lax.all_to_all(zs, "z", 0, 0)
    yr = swap(n2, "y")
    near, far = pair_nodes(pos, n2, yr)
    near, far_a, far_b = along(near, "x", 1), along(far, "x", 2), along(far, "x", 3)
    zr, near, far_a, far_b, ct_oth = lax.optimization_barrier((zr, near, far_a, far_b, ct_oth))
    xr = lax.all_to_all(plane_slots(pos, zr), ("x", "y"), 0, 0)
    q, ag, xt = project(pos, x_own, x_oth, ct_own, ct_oth, w_qkv, w_out, perm)
    att, dq, dkv, dn1, dy, dnear, dfar_a, dfar_b, dx = attention(pos, q, ag, kv, n1, yr, near, far_a, far_b, xr)

    dx_r = lax.all_to_all(dx, ("x", "y"), 0, 0)
    att_oth = swap(att, "c")
    back = (along(dnear, "x", 1), along(dfar_a, "x", 2), along(dfar_b, "x", 3))
    layer_out, *terms = output_side(pos, att, att_oth, ct_own, ct_oth, dq, xt, w_out, perm)
    dx_r, back, terms = lax.optimization_barrier((dx_r, back, terms))
    dz_r = lax.all_to_all(back_slots(pos, dx_r), "z", 0, 0)
    firsts = terms[:1] + [along(terms[far], "x", far) for far in (1, 2, 3)]
    keep, dy = pair_back(pos, *back, dy)
    base = base_grads(pos, dkv, dn1, swap(dy, "y"), keep)
    dz_r, base, firsts = lax.optimization_barrier((dz_r, base, firsts))
    pg, terms = leaf_grads(pos, dz_r, base, dq, xt)
    second = lax.all_to_all(terms.reshape(16, 96, H), ("x", "y", "dp"), 0, 0)
    firsts = list(x_sum(pos, *firsts))
    firsts = firsts[:1] + [along(firsts[far], ("y", "dp"), far) for far in (1, 2, 3)]
    pg_own = lax.dynamic_index_in_dim(pg, c, 0, keepdims=False)
    pg_oth = swap(lax.dynamic_index_in_dim(pg, 1 - c, 0, keepdims=False), "c")
    input_grad = input_side(pos, pg_own, pg_oth, w_qkv)
    second, input_grad, firsts = lax.optimization_barrier((second, input_grad, firsts))
    terms = lax.all_to_all(middle_sum(pos, firsts, second), "z", 0, 0)
    own, oth = z_sum(pos, terms)
    pair = ("c", "dp")
    qkv_grad, out_grad = last_rows(pos, own, along(own, pair, 1), along(oth, pair, 2), along(oth, pair, 3))
    return (layer_out[None], input_grad[None], qkv_grad, out_grad)


def solution(mesh):
    split = Mesh(mesh.devices.reshape(ZN, XN, YN, 2, 2), ("z", "x", "y", "c", "dp"))
    seq = ("z", "x", "y", "c")
    return jax.shard_map(
        shards,
        mesh=split,
        in_specs=(P("dp", seq, None), P("dp", seq, None), P(), P()),
        out_specs=(P("dp", seq, None), P("dp", seq, None), P(seq, None), P(seq, None)),
        check_vma=False,
    )
```

```python
import jax
import jax.numpy as jnp
import numpy as np
from jax import lax
from jax.experimental import pallas as pl
from jax.experimental.pallas import tpu as pltpu
from jax.sharding import Mesh, PartitionSpec as P

D = 768
H = 384
TOK = 256
NR = 128
DH = 64
ZN, XN, YN = 8, 4, 2
ZR = 48
HALF_ROOT = 0.7071067811865476
LOG2E = 1.4426950408889634
VMEM = 56 * 1024 * 1024
F32 = jnp.float32
BF16 = jnp.bfloat16


def dot(a, b):
    return lax.dot_general(a, b, (((1,), (0,)), ((), ())), preferred_element_type=F32)


def dot_nt(a, b):
    return lax.dot_general(a, b, (((1,), (1,)), ((), ())), preferred_element_type=F32)


def dot_tn(a, b):
    return lax.dot_general(a, b, (((0,), (0,)), ((), ())), preferred_element_type=F32)


def iota(shape, axis):
    return lax.broadcasted_iota(jnp.int32, shape, axis)


def pair_matrix(rows, cols, valid):
    r, k = iota((rows, cols), 0), iota((rows, cols), 1)
    return (((k >> 1) == r) & (r < valid)).astype(BF16)


def coarsen(node, rows=None, valid=None):
    rows = node.shape[0] // 2 if rows is None else rows
    valid = rows if valid is None else valid
    return (dot(pair_matrix(rows, node.shape[0], valid), node) * HALF_ROOT).astype(BF16)


def spread(grad, rows, valid=None):
    height = grad.shape[0]
    r, k = iota((rows, 2 * height), 0), iota((rows, 2 * height), 1)
    hot = (r >> 1) == (k & (height - 1))
    if valid is not None:
        hot = hot & (r < valid)
    high = grad.astype(BF16)
    low = (grad - high.astype(F32)).astype(BF16)
    return dot(hot.astype(BF16), jnp.concatenate([high, low], axis=0)) * HALF_ROOT


def whole(*shape):
    return pl.BlockSpec(shape, lambda *_: (0,) * len(shape))


def call(body, grid, ins, outs, scratch=()):
    return pl.pallas_call(
        body,
        grid_spec=pltpu.PrefetchScalarGridSpec(
            num_scalar_prefetch=1,
            grid=grid,
            in_specs=ins,
            out_specs=[s for s, _ in outs],
            scratch_shapes=list(scratch),
        ),
        out_shape=[jax.ShapeDtypeStruct(shape, kind) for _, (shape, kind) in outs],
        compiler_params=pltpu.CompilerParams(vmem_limit_bytes=VMEM),
    )


def tree_body(pos, x_own, x_oth, wk, wv, kv_out, n1_out, n2_out, zs_out):
    c, z = pos[0], pos[1]
    for e, x in ((c, x_own), (1 - c, x_oth)):
        kv_out[e, 0] = dot(x[...], wk[...]).astype(BF16)
        kv_out[e, 1] = dot(x[...], wv[...]).astype(BF16)

    def store(ref, *index):
        def put(node):
            for p in range(2):
                ref[index + (p,)] = node[:, H * p : H * p + H]

        return put

    halves = []
    for e in range(2):
        n1 = coarsen(jnp.concatenate([kv_out[e, 0], kv_out[e, 1]], axis=1))
        store(n1_out, e)(n1)
        halves.append(coarsen(n1))
    n2 = jnp.concatenate(halves, axis=0)
    store(n2_out)(n2)
    n5 = coarsen(coarsen(coarsen(n2)))
    n6 = coarsen(n5, 16, 8)
    n7 = coarsen(n6, 16, 4)
    store(zs_out, z)(jnp.zeros_like(n5))
    store(zs_out, z ^ 1)(n5)
    for far in (2, 3):
        store(zs_out, z ^ far)(n6)
    for far in (4, 5, 6, 7):
        store(zs_out, z ^ far)(n7)


def tree(pos, x_own, x_oth, w_qkv):
    col = lambda part: pl.BlockSpec((D, H), lambda i, s: (0, 2 * part + s[0]))
    outs = [(2, 2, TOK, H), (2, 2, NR, H), (2, NR, H), (ZN, 2, 16, H)]
    return call(
        tree_body,
        (1,),
        [whole(TOK, D)] * 2 + [col(1), col(2)],
        [(whole(*shape), (shape, BF16)) for shape in outs],
    )(pos, x_own, x_oth, w_qkv, w_qkv)


def project_body(pos, x_own, x_oth, ct_own, ct_oth, wq, wo, perm, q_out, ag_out, xt_out):
    c = pos[0]
    for e, x, ct in ((c, x_own, ct_own), (1 - c, x_oth, ct_oth)):
        q_out[e] = dot(x[...], wq[...]).astype(BF16)
        ag_out[e] = dot_nt(ct[...], wo[...]).astype(BF16)
        xt_out[e] = dot_nt(perm[...], x[...]).astype(BF16)


def project(pos, x_own, x_oth, ct_own, ct_oth, w_qkv, w_out, perm):
    outs = [(2, TOK, H), (2, TOK, H), (2, D, TOK)]
    return call(
        project_body,
        (1,),
        [whole(TOK, D)] * 4
        + [pl.BlockSpec((D, H), lambda i, s: (0, s[0])), pl.BlockSpec((H, D), lambda i, s: (s[0], 0)), whole(D, D)],
        [(whole(*shape), (shape, BF16)) for shape in outs],
    )(pos, x_own, x_oth, ct_own, ct_oth, w_qkv, w_out, perm)


def pair_body(pos, own, oth, near_out, far_out):
    y = pos[2] & 1
    for p in range(2):
        for half, n2 in ((y, own), (1 - y, oth)):
            near_out[half, p] = coarsen(n2[p])
            far_out[half, p] = coarsen(near_out[half, p])


def pair_nodes(pos, own, oth):
    outs = [(2, 2, 64, H), (2, 2, 32, H)]
    return call(
        pair_body, (1,), [whole(2, NR, H)] * 2, [(whole(*shape), (shape, BF16)) for shape in outs]
    )(pos, own, oth)


def pair_back_body(pos, near, far_a, far_b, dy, keep_out, send_out):
    y = pos[2] & 1
    for p in range(2):
        for half, out in ((y, None), (1 - y, send_out)):
            grad = near[half, p].astype(F32) + spread(far_a[half, p].astype(F32) + far_b[half, p].astype(F32), 64)
            if out is None:
                keep_out[p] = grad
            else:
                out[p] = (dy[p].astype(F32) + spread(grad, NR)).astype(BF16)


def pair_back(pos, near, far_a, far_b, dy):
    return call(
        pair_back_body,
        (1,),
        [whole(2, 2, 64, H), whole(2, 2, 32, H), whole(2, 2, 32, H), whole(2, NR, H)],
        [(whole(2, 64, H), ((2, 64, H), F32)), (whole(2, NR, H), ((2, NR, H), BF16))],
    )(pos, near, far_a, far_b, dy)


def z_source(z, rows_axis, shape):
    i = iota(shape, rows_axis)
    near = 16 * (z ^ 1) + i
    mid = 16 * (z ^ (2 + ((i - 16) >> 3))) + ((i - 16) & 7)
    far = 16 * (z ^ (4 + ((i - 32) >> 2))) + ((i - 32) & 3)
    return jnp.where(i < 16, near, jnp.where(i < 32, mid, far))


def plane_body(pos, zr, out):
    hot = (iota((ZR, 128), 1) == z_source(pos[1], 0, (ZR, 128))).astype(BF16)
    both = jnp.concatenate([zr[:, p].reshape(128, H) for p in range(2)], axis=1)
    rows = dot(hot, both).astype(BF16)
    for slot in range(8):
        for p in range(2):
            out[slot, p] = rows[:, H * p : H * p + H]


def plane_slots(pos, zr):
    return call(
        plane_body,
        (1,),
        [whole(ZN, 2, 16, H)],
        [(whole(8, 2, ZR, H), ((8, 2, ZR, H), BF16))],
    )(pos, zr)[0]


def attention_body(pos, q, ag, kv, n1, yr, near, far_a, far_b, xr, att_out, dq_out, dkv_out, dn1_out, dy_out, dnear_out, dfar_a_out, dfar_b_out, dx_out, keys, keys_t, s_ref, dw_ref, w_ref, ds_ref, drem):
    for p in range(2):
        for e in range(2):
            keys[e, p, :256] = kv[e, p]
            keys[e, p, 256:384] = n1[1 - e, p]
            keys[e, p, 384:512] = yr[p]
            for half in range(2):
                start = 512 + 64 * half
                keys[e, p, start : start + 64] = near[half, p]
                start = 640 + 32 * half
                keys[e, p, start : start + 32] = far_a[half, p]
                start = 704 + 32 * half
                keys[e, p, start : start + 32] = far_b[half, p]
            for slot in range(8):
                start = 768 + ZR * slot
                keys[e, p, start : start + ZR] = xr[slot, p]
    for p in range(2):
        for e in range(2):
            keys_t[e, p] = keys[e, p].T
    lane = iota((TOK, 128), 1)
    steps = [(e, h) for e in range(2) for h in range(2)]
    masked = {}

    def scores(step):
        e, h = steps[step]
        mine = (lane >> 6) == h
        qh = jnp.where(mine, q[e], jnp.zeros((), BF16))
        ah = jnp.where(mine, ag[e], jnp.zeros((), BF16))
        masked[step] = (qh, ah)
        s_ref[step % 2] = dot_nt(keys[e, 0], qh)
        dw_ref[step % 2] = dot_nt(keys[e, 1], ah)

    scores(0)
    for step, (e, h) in enumerate(steps):
        if step + 1 < len(steps):
            scores(step + 1)
        if h == 0:
            att_t, dq_t = [], []
            dk = dv = None
        s, dw, b = s_ref.at[step % 2], dw_ref.at[step % 2], step % 2
        qh, ah = masked[step]
        top = jnp.max(s[...], axis=0, keepdims=True)
        un = jnp.exp2((s[...] - top) * (LOG2E * DH ** -0.5))
        s[...] = un
        inverse = 1.0 / jnp.sum(un, axis=0, keepdims=True)
        delta = jnp.sum(un * dw[...], axis=0, keepdims=True) * inverse
        prob = s[...] * inverse
        w_ref[b] = prob.astype(BF16)
        ds_ref[b] = (prob * ((dw[...] - delta) * DH ** -0.5)).astype(BF16)
        att_t.append(dot(keys_t[e, 1, 64 * h : 64 * h + 64], w_ref[b]))
        dq_t.append(dot(keys_t[e, 0, 64 * h : 64 * h + 64], ds_ref[b]))
        dkh, dvh = dot(ds_ref[b], qh), dot(w_ref[b], ah)
        dk = dkh if dk is None else dk + dkh
        dv = dvh if dv is None else dv + dvh
        if h == 0:
            continue
        att_out[e] = jnp.concatenate(att_t, axis=0).T.astype(BF16)
        dq_out[e] = jnp.concatenate(dq_t, axis=0).T.astype(BF16)
        for p, grad in ((0, dk), (1, dv)):
            dkv_out[e, p] = grad[:256]
            dn1_out[1 - e, p] = grad[256:384]
            if e == 0:
                drem[p] = grad[384:]
            else:
                drem[p] = drem[p] + grad[384:]
    for p in range(2):
        rows = drem[p].astype(BF16)
        dy_out[p] = rows[:128]
        for half in range(2):
            start = 128 + 64 * half
            dnear_out[half, p] = rows[start : start + 64]
            start = 256 + 32 * half
            dfar_a_out[half, p] = rows[start : start + 32]
            start = 320 + 32 * half
            dfar_b_out[half, p] = rows[start : start + 32]
        for slot in range(8):
            start = 384 + ZR * slot
            dx_out[slot, p] = rows[start : start + ZR]


def attention(pos, q, ag, kv, n1, yr, near, far_a, far_b, xr):
    def cut(*lead):
        return pl.BlockSpec(lead + (128,), lambda i, s: (0,) * len(lead) + (i,))

    outs = [
        ((2, TOK), BF16), ((2, TOK), BF16), ((2, 2, TOK), F32), ((2, 2, NR), F32), ((2, NR), BF16),
        ((2, 2, 64), BF16), ((2, 2, 32), BF16), ((2, 2, 32), BF16), ((8, 2, ZR), BF16),
    ]
    n = 1152
    return call(
        attention_body,
        (H // 128,),
        [cut(2, TOK), cut(2, TOK), cut(2, 2, TOK), cut(2, 2, NR), cut(2, NR), cut(2, 2, 64), cut(2, 2, 32), cut(2, 2, 32), cut(8, 2, ZR)],
        [(cut(*lead), (lead + (H,), kind)) for lead, kind in outs],
        [
            pltpu.VMEM((2, 2, n, 128), BF16), pltpu.VMEM((2, 2, 128, n), BF16), pltpu.VMEM((2, n, TOK), F32), pltpu.VMEM((2, n, TOK), F32),
            pltpu.VMEM((2, n, TOK), BF16), pltpu.VMEM((2, n, TOK), BF16), pltpu.VMEM((2, 768, 128), F32),
        ],
    )(pos, q, ag, kv, n1, yr, near, far_a, far_b, xr)


def output_body(pos, att_own, att_oth, w_own, w_oth, out):
    c = pos[0]
    out[...] = (dot(att_own[c], w_own[...]) + dot(att_oth[c], w_oth[...])).astype(BF16)


def output_side(pos, att_own, att_oth, w_out):
    row = lambda flip: pl.BlockSpec((H, D), lambda i, s: (s[0] ^ flip, 0))
    return call(
        output_body,
        (1,),
        [whole(2, TOK, H)] * 2 + [row(0), row(1)],
        [(whole(TOK, D), ((TOK, D), BF16))],
    )(pos, att_own, att_oth, w_out, w_out)[0]


def terms_body(pos, att_own, att_oth, ct_own, ct_oth, dq, xt, p_own, p_oth, *rest):
    c, x = pos[0], pos[2] >> 1
    slots = rest[-1]
    total = dot(xt[0], dq[0]) + dot(xt[1], dq[1])
    slots[:, :, 0] = total.astype(BF16).reshape(XN, YN, 96, H)
    total = None
    for e, ct in ((c, ct_own), (1 - c, ct_oth)):
        att_t = (dot_nt(p_own[...], att_own[e]) + dot_nt(p_oth[...], att_oth[e])).astype(BF16)
        term = dot(att_t, ct[...])
        total = term if total is None else total + term
    slots[:, :, 1] = total.astype(BF16).reshape(XN, YN, 96, H)
    for far in range(XN):
        rest[far][...] = slots[x ^ far]


def output_terms(pos, att_own, att_oth, ct_own, ct_oth, dq, xt, perm):
    col = lambda flip, rows: pl.BlockSpec((rows, H), lambda i, s: (0, s[0] ^ flip))
    slot = (YN, 2, 96, H)
    return call(
        terms_body,
        (1,),
        [whole(2, TOK, H)] * 2 + [col(0, TOK)] * 2 + [whole(2, TOK, H), whole(2, D, TOK), col(0, D), col(1, D)],
        [(whole(*slot), (slot, BF16))] * XN,
        [pltpu.VMEM((XN,) + slot, BF16)],
    )(pos, att_own, att_oth, ct_own, ct_oth, dq, xt, perm, perm)


def x_sum_body(pos, t0, t1, t2, t3, *rest):
    y, dp = pos[2] & 1, pos[3]
    slots = rest[-1]
    total = (t0[...].astype(F32) + t1[...].astype(F32)) + (t2[...].astype(F32) + t3[...].astype(F32))
    slots[...] = total.astype(BF16)
    for far in range(4):
        rest[far][...] = slots[y ^ (far >> 1), dp ^ (far & 1)]


def x_sum(pos, *terms):
    shape = (YN, 2, 96, H)
    return call(
        x_sum_body,
        (1,),
        [whole(*shape)] * 4,
        [(whole(96, H), ((96, H), BF16))] * 4,
        [pltpu.VMEM(shape, BF16)],
    )(pos, *terms)


def back_body(pos, xr, out):
    hot = (iota((128, ZR), 0) == z_source(pos[1], 1, (128, ZR))).astype(BF16)
    for p in range(2):
        total = xr[0, p].astype(F32)
        for slot in range(1, 8):
            total = total + xr[slot, p].astype(F32)
        out[:, p] = dot(hot, total.astype(BF16)).astype(BF16).reshape(8, 16, H)


def back_slots(pos, xr):
    return call(
        back_body,
        (1,),
        [whole(8, 2, ZR, H)],
        [(whole(ZN, 2, 16, H), ((ZN, 2, 16, H), BF16))],
    )(pos, xr)[0]


def leaf_body(pos, zr, dkv, dn1, yr, keep, dq, xt, pg_out, grad_out):
    def split(grad):
        high = grad.astype(BF16)
        return [high, (grad - high.astype(F32)).astype(BF16)]

    def hot(hit, scale):
        return jnp.where(hit, scale, 0.0).astype(BF16)

    def wide(ref):
        return jnp.concatenate([ref[0], ref[1]], axis=1)

    zs = jnp.concatenate([zr[:, p].reshape(128, H) for p in range(2)], axis=1)
    near = split(wide(keep))
    for e in range(2):
        t, k = iota((TOK, 128), 0), iota((TOK, 128), 1)
        far, row, chip = (k >> 4) ^ pos[1], k & 15, t + TOK * e
        first = hot(t >> 1 == k, 1.0)
        third = hot(chip >> 3 == k & 63, 0.5)
        odd = hot((far == 1) & (row == chip >> 5), 0.25) + hot((far >= 4) & (row == chip >> 7), 0.125)
        even = [hot(chip >> 2 == k, 0.5), hot((far >> 1 == 1) & (row == chip >> 6), 0.125)]
        up = dot(jnp.concatenate([first, first, third, odd], axis=1), jnp.concatenate(split(wide(dn1.at[e])) + near + [zs], axis=0))
        up = up * HALF_ROOT + dot(jnp.concatenate(even, axis=1), jnp.concatenate([wide(yr), zs], axis=0))
        for p in range(2):
            pg_out[e, :, H * (1 + p) : H * (2 + p)] = (dkv[e, p] + up[:, H * p : H * p + H]).astype(BF16)
        pg_out[e, :, :H] = dq[e]
    for p in range(2):
        cols = slice(H * (1 + p), H * (2 + p))
        total = dot(xt[0], pg_out[0, :, cols]) + dot(xt[1], pg_out[1, :, cols])
        grad_out[:, p] = total.astype(BF16).reshape(8, 96, H)


def leaf_grads(pos, zr, dkv, dn1, yr, keep, dq, xt):
    return call(
        leaf_body,
        (1,),
        [
            whole(ZN, 2, 16, H), whole(2, 2, TOK, H), whole(2, 2, NR, H), whole(2, NR, H), whole(2, 64, H),
            whole(2, TOK, H), whole(2, D, TOK),
        ],
        [
            (whole(2, TOK, 3 * H), ((2, TOK, 3 * H), BF16)),
            (whole(8, 2, 96, H), ((8, 2, 96, H), BF16)),
        ],
    )(pos, zr, dkv, dn1, yr, keep, dq, xt)


def input_body(pos, pg_own, pg_oth, *rest):
    out = rest[-1]
    total = None
    for part in range(3):
        for pg, w in ((pg_own, rest[part]), (pg_oth, rest[3 + part])):
            term = dot_nt(pg[:, H * part : H * part + H], w[...])
            total = term if total is None else total + term
    out[...] = total.astype(BF16)


def input_side(pos, pg_own, pg_oth, w_qkv):
    col = lambda part, flip: pl.BlockSpec((D, H), lambda i, s: (0, 2 * part + (s[0] ^ flip)))
    return call(
        input_body,
        (1,),
        [whole(TOK, 3 * H)] * 2 + [col(part, flip) for flip in (0, 1) for part in range(3)],
        [(whole(TOK, D), ((TOK, D), BF16))],
    )(pos, pg_own, pg_oth, *[w_qkv] * 6)[0]


def total_of(refs):
    total = refs[0].astype(F32)
    for ref in refs[1:]:
        total = total + ref.astype(F32)
    return total


def middle_body(pos, f0, f1, f2, f3, second, out):
    first = total_of([f0[...], f1[...], f2[...], f3[...]]).astype(BF16)
    i, k = iota((256, 96), 0), iota((256, 96), 1)
    row, half = i & 7, (i >> 3) & 1
    hit = (k == 6 * (i >> 4) + row) & (row < 6)
    rows = dot((hit & (half == 0)).astype(BF16), first)
    rows = rows + dot((hit & (half == 1)).astype(BF16), total_of([second[slot] for slot in range(16)]).astype(BF16))
    out[...] = rows.astype(BF16).reshape(ZN, 2, 16, H)


def middle_sum(pos, firsts, second):
    shape = (ZN, 2, 16, H)
    return call(
        middle_body, (1,), [whole(96, H)] * 4 + [whole(16, 96, H)], [(whole(*shape), (shape, BF16))]
    )(pos, *firsts, second)[0]


def z_sum_body(pos, terms, own_out, oth_out):
    for core, out in ((pos[0], own_out), (1 - pos[0], oth_out)):
        out[...] = total_of([terms[z, core] for z in range(ZN)]).astype(BF16)


def z_sum(pos, terms):
    return call(
        z_sum_body,
        (1,),
        [whole(ZN, 2, 16, H)],
        [(whole(16, H), ((16, H), BF16))] * 2,
    )(pos, terms)


def last_body(pos, own, from_dp, from_core, from_both, qkv_out, out_out, parts):
    core, dp = pos[0], pos[3]
    parts[core, dp] = own[...]
    parts[core, 1 - dp] = from_dp[...]
    parts[1 - core, dp] = from_core[...]
    parts[1 - core, 1 - dp] = from_both[...]
    for core in range(2):
        low, high = parts[core, 0].astype(F32), parts[core, 1].astype(F32)
        cols = lambda part: slice(D * part + H * core, D * part + H * core + H)
        qkv_out[:, cols(0)] = low[:6]
        qkv_out[:, cols(1)] = low[8:14]
        qkv_out[:, cols(2)] = high[8:14]
        out_out[:, cols(0)] = high[:6]


def last_rows(pos, *parts):
    return call(
        last_body,
        (1,),
        [whole(16, H)] * 4,
        [(whole(6, 3 * D), ((6, 3 * D), F32)), (whole(6, D), ((6, D), F32))],
        [pltpu.VMEM((2, 2, 16, H), BF16)],
    )(pos, *parts)


def swap(value, axis):
    return lax.ppermute(value, axis, [(0, 1), (1, 0)])


def along(value, axes, far, count=4):
    return lax.ppermute(value, axes, [(i, i ^ far) for i in range(count)])


def row_order():
    f = np.arange(D)
    source = 96 * (f // 12 % 8) + 12 * (f // 96) + f % 12
    return jnp.asarray(source[:, None] == f[None, :], BF16)


def shards(x_tokens, cotangent, w_qkv, w_out):
    x_own, ct_own = x_tokens[0], cotangent[0]
    c, z, dp = lax.axis_index("c"), lax.axis_index("z"), lax.axis_index("dp")
    j = 2 * lax.axis_index("x") + lax.axis_index("y")
    pos = jnp.stack([c, z, j, dp]).astype(jnp.int32)
    x_oth, ct_oth = swap(x_own, "c"), swap(ct_own, "c")
    perm = row_order()

    kv, n1, n2, zs = tree(pos, x_own, x_oth, w_qkv)
    zr = lax.all_to_all(zs, "z", 0, 0)
    yr = swap(n2, "y")
    near, far = pair_nodes(pos, n2, yr)
    zr, near, far, ct_oth = lax.optimization_barrier((zr, near, far, ct_oth))
    near, far_a, far_b = along(near, "x", 1), along(far, "x", 2), along(far, "x", 3)
    xr = lax.all_to_all(plane_slots(pos, zr), ("x", "y"), 0, 0)
    q, ag, xt = project(pos, x_own, x_oth, ct_own, ct_oth, w_qkv, w_out, perm)
    att, dq, dkv, dn1, dy, dnear, dfar_a, dfar_b, dx = attention(pos, q, ag, kv, n1, yr, near, far_a, far_b, xr)

    dx_r = lax.all_to_all(dx, ("x", "y"), 0, 0)
    att_oth = swap(att, "c")
    back = (along(dnear, "x", 1), along(dfar_a, "x", 2), along(dfar_b, "x", 3))
    first, *firsts = output_terms(pos, att, att_oth, ct_own, ct_oth, dq, xt, perm)
    dx_r, back, first = lax.optimization_barrier((dx_r, back, first))
    dz_r = lax.all_to_all(back_slots(pos, dx_r), "z", 0, 0)
    firsts = x_sum(pos, first, *[along(firsts[far - 1], "x", far) for far in (1, 2, 3)])
    keep, dy = pair_back(pos, *back, dy)
    dz_r, firsts = lax.optimization_barrier((dz_r, firsts))
    pg, terms = leaf_grads(pos, dz_r, dkv, dn1, swap(dy, "y"), keep, dq, xt)
    second = lax.all_to_all(terms.reshape(16, 96, H), ("x", "y", "dp"), 0, 0)
    firsts = list(firsts[:1]) + [along(firsts[far], ("y", "dp"), far) for far in (1, 2, 3)]
    pg_own = lax.dynamic_index_in_dim(pg, c, 0, keepdims=False)
    pg_oth = swap(lax.dynamic_index_in_dim(pg, 1 - c, 0, keepdims=False), "c")
    input_grad = input_side(pos, pg_own, pg_oth, w_qkv)
    second, input_grad, firsts = lax.optimization_barrier((second, input_grad, firsts))
    terms = middle_sum(pos, firsts, second)
    terms, att, att_oth = lax.optimization_barrier((terms, att, att_oth))
    terms = lax.all_to_all(terms, "z", 0, 0)
    layer_out = output_side(pos, att, att_oth, w_out)
    terms, layer_out = lax.optimization_barrier((terms, layer_out))
    own, oth = z_sum(pos, terms)
    pair = ("c", "dp")
    qkv_grad, out_grad = last_rows(pos, own, along(own, pair, 1), along(oth, pair, 2), along(oth, pair, 3))
    return (layer_out[None], input_grad[None], qkv_grad, out_grad)


def solution(mesh):
    split = Mesh(mesh.devices.reshape(ZN, XN, YN, 2, 2), ("z", "x", "y", "c", "dp"))
    seq = ("z", "x", "y", "c")
    return jax.shard_map(
        shards,
        mesh=split,
        in_specs=(P("dp", seq, None), P("dp", seq, None), P(), P()),
        out_specs=(P("dp", seq, None), P("dp", seq, None), P(seq, None), P(seq, None)),
        check_vma=False,
    )
```

```python
import jax
import jax.numpy as jnp
import numpy as np
from jax import lax
from jax.experimental import pallas as pl
from jax.experimental.pallas import tpu as pltpu
from jax.sharding import Mesh, PartitionSpec as P

D = 768
H = 384
TOK = 256
NR = 128
DH = 64
ZN, XN, YN = 8, 4, 2
ZR = 48
HALF_ROOT = 0.7071067811865476
LOG2E = 1.4426950408889634
VMEM = 56 * 1024 * 1024
F32 = jnp.float32
BF16 = jnp.bfloat16


def dot(a, b):
    return lax.dot_general(a, b, (((1,), (0,)), ((), ())), preferred_element_type=F32)


def dot_nt(a, b):
    return lax.dot_general(a, b, (((1,), (1,)), ((), ())), preferred_element_type=F32)


def dot_tn(a, b):
    return lax.dot_general(a, b, (((0,), (0,)), ((), ())), preferred_element_type=F32)


def iota(shape, axis):
    return lax.broadcasted_iota(jnp.int32, shape, axis)


def pair_matrix(rows, cols, valid):
    r, k = iota((rows, cols), 0), iota((rows, cols), 1)
    return (((k >> 1) == r) & (r < valid)).astype(BF16)


def coarsen(node, rows=None, valid=None):
    rows = node.shape[0] // 2 if rows is None else rows
    valid = rows if valid is None else valid
    return (dot(pair_matrix(rows, node.shape[0], valid), node) * HALF_ROOT).astype(BF16)


def whole(*shape):
    return pl.BlockSpec(shape, lambda *_: (0,) * len(shape))


def call(body, grid, ins, outs, scratch=(), aliases={}):
    return pl.pallas_call(
        body,
        grid_spec=pltpu.PrefetchScalarGridSpec(
            num_scalar_prefetch=1,
            grid=grid,
            in_specs=ins,
            out_specs=[s for s, _ in outs],
            scratch_shapes=list(scratch),
        ),
        out_shape=[jax.ShapeDtypeStruct(shape, kind) for _, (shape, kind) in outs],
        input_output_aliases=dict(aliases),
        compiler_params=pltpu.CompilerParams(vmem_limit_bytes=VMEM),
    )


def tree_body(pos, x_own, x_oth, wk, wv, kv_out, n1_out, n2_out, n3_out, n4_out, zs_out):
    c, z = pos[0], pos[1]
    for e, x in ((c, x_own), (1 - c, x_oth)):
        kv_out[e, 0] = dot(x[...], wk[...]).astype(BF16)
        kv_out[e, 1] = dot(x[...], wv[...]).astype(BF16)

    def store(ref, *index):
        def put(node):
            for p in range(2):
                ref[index + (p,)] = node[:, H * p : H * p + H]

        return put

    halves = []
    for e in range(2):
        n1 = coarsen(jnp.concatenate([kv_out[e, 0], kv_out[e, 1]], axis=1))
        store(n1_out, e)(n1)
        halves.append(coarsen(n1))
    n2 = jnp.concatenate(halves, axis=0)
    store(n2_out)(n2)
    n3 = coarsen(n2)
    store(n3_out)(n3)
    n4 = coarsen(n3)
    store(n4_out)(n4)
    n5 = coarsen(n4)
    n6 = coarsen(n5, 16, 8)
    n7 = coarsen(n6, 16, 4)
    store(zs_out, z)(jnp.zeros_like(n5))
    store(zs_out, z ^ 1)(n5)
    for far in (2, 3):
        store(zs_out, z ^ far)(n6)
    for far in (4, 5, 6, 7):
        store(zs_out, z ^ far)(n7)


def tree(pos, x_own, x_oth, w_qkv):
    col = lambda part: pl.BlockSpec((D, H), lambda i, s: (0, 2 * part + s[0]))
    outs = [(2, 2, TOK, H), (2, 2, NR, H), (2, NR, H), (2, 64, H), (2, 32, H), (ZN, 2, 16, H)]
    return call(
        tree_body,
        (1,),
        [whole(TOK, D)] * 2 + [col(1), col(2)],
        [(whole(*shape), (shape, BF16)) for shape in outs],
    )(pos, x_own, x_oth, w_qkv, w_qkv)


def project_body(pos, x_own, x_oth, ct_own, ct_oth, wq, wo, perm, q_out, ag_out, xt_out):
    c = pos[0]
    for e, x, ct in ((c, x_own, ct_own), (1 - c, x_oth, ct_oth)):
        q_out[e] = dot(x[...], wq[...]).astype(BF16)
        ag_out[e] = dot_nt(ct[...], wo[...]).astype(BF16)
        xt_out[e] = dot_nt(perm[...], x[...]).astype(BF16)


def project(pos, x_own, x_oth, ct_own, ct_oth, w_qkv, w_out, perm):
    outs = [(2, TOK, H), (2, TOK, H), (2, D, TOK)]
    return call(
        project_body,
        (1,),
        [whole(TOK, D)] * 4
        + [pl.BlockSpec((D, H), lambda i, s: (0, s[0])), pl.BlockSpec((H, D), lambda i, s: (s[0], 0)), whole(D, D)],
        [(whole(*shape), (shape, BF16)) for shape in outs],
    )(pos, x_own, x_oth, ct_own, ct_oth, w_qkv, w_out, perm)


def z_source(z, rows_axis, shape):
    i = iota(shape, rows_axis)
    near = 16 * (z ^ 1) + i
    mid = 16 * (z ^ (2 + ((i - 16) >> 3))) + ((i - 16) & 7)
    far = 16 * (z ^ (4 + ((i - 32) >> 2))) + ((i - 32) & 3)
    return jnp.where(i < 16, near, jnp.where(i < 32, mid, far))


def plane_body(pos, zr, out):
    hot = (iota((ZR, 128), 1) == z_source(pos[1], 0, (ZR, 128))).astype(BF16)
    both = jnp.concatenate([zr[:, p].reshape(128, H) for p in range(2)], axis=1)
    rows = dot(hot, both).astype(BF16)
    for slot in range(8):
        for p in range(2):
            out[slot, p] = rows[:, H * p : H * p + H]


def plane_slots(pos, zr):
    return call(
        plane_body,
        (1,),
        [whole(ZN, 2, 16, H)],
        [(whole(8, 2, ZR, H), ((8, 2, ZR, H), BF16))],
    )(pos, zr)[0]


def attention_body(pos, q, ag, kv, n1, yr, wr, wy, xr, att_out, dq_out, dkv_out, dn1_out, dy_out, dw_out, dx_out, keys, keys_t, s_ref, dw_ref, w_ref, ds_ref, drem):
    for p in range(2):
        for e in range(2):
            keys[e, p, :256] = kv[e, p]
            keys[e, p, 256:384] = n1[1 - e, p]
            keys[e, p, 384:512] = yr[p]
            keys[e, p, 512:640] = wr[p]
            keys[e, p, 640:768] = wy[p]
            for slot in range(8):
                start = 768 + ZR * slot
                keys[e, p, start : start + ZR] = xr[slot, p]
    for p in range(2):
        for e in range(2):
            keys_t[e, p] = keys[e, p].T
    lane = iota((TOK, 128), 1)
    steps = [(e, h) for e in range(2) for h in range(2)]
    masked = {}

    def scores(step):
        e, h = steps[step]
        mine = (lane >> 6) == h
        qh = jnp.where(mine, q[e], jnp.zeros((), BF16))
        ah = jnp.where(mine, ag[e], jnp.zeros((), BF16))
        masked[step] = (qh, ah)
        s_ref[step % 2] = dot_nt(keys[e, 0], qh)
        dw_ref[step % 2] = dot_nt(keys[e, 1], ah)

    scores(0)
    for step, (e, h) in enumerate(steps):
        if step + 1 < len(steps):
            scores(step + 1)
        if h == 0:
            att_t, dq_t = [], []
            dk = dv = None
        s, dw, b = s_ref.at[step % 2], dw_ref.at[step % 2], step % 2
        qh, ah = masked[step]
        top = jnp.max(s[...], axis=0, keepdims=True)
        un = jnp.exp2((s[...] - top) * (LOG2E * DH ** -0.5))
        s[...] = un
        inverse = 1.0 / jnp.sum(un, axis=0, keepdims=True)
        delta = jnp.sum(un * dw[...], axis=0, keepdims=True) * inverse
        prob = s[...] * inverse
        w_ref[b] = prob.astype(BF16)
        ds_ref[b] = (prob * ((dw[...] - delta) * DH ** -0.5)).astype(BF16)
        att_t.append(dot(keys_t[e, 1, 64 * h : 64 * h + 64], w_ref[b]))
        dq_t.append(dot(keys_t[e, 0, 64 * h : 64 * h + 64], ds_ref[b]))
        dkh, dvh = dot(ds_ref[b], qh), dot(w_ref[b], ah)
        dk = dkh if dk is None else dk + dkh
        dv = dvh if dv is None else dv + dvh
        if h == 0:
            continue
        att_out[e] = jnp.concatenate(att_t, axis=0).T.astype(BF16)
        dq_out[e] = jnp.concatenate(dq_t, axis=0).T.astype(BF16)
        for p, grad in ((0, dk), (1, dv)):
            dkv_out[e, p] = grad[:256]
            dn1_out[1 - e, p] = grad[256:384]
            if e == 0:
                drem[p] = grad[384:]
            else:
                drem[p] = drem[p] + grad[384:]
    for p in range(2):
        rows = drem[p].astype(BF16)
        dy_out[p, :NR] = rows[:128]
        dy_out[p, NR:] = rows[256:384]
        dw_out[p] = drem[p, 128:256]
        for slot in range(8):
            start = 384 + ZR * slot
            dx_out[slot, p] = rows[start : start + ZR]


def attention(pos, q, ag, kv, n1, yr, wr, wy, xr):
    def cut(*lead):
        return pl.BlockSpec(lead + (128,), lambda i, s: (0,) * len(lead) + (i,))

    outs = [
        ((2, TOK), BF16), ((2, TOK), BF16), ((2, 2, TOK), F32), ((2, 2, NR), F32), ((2, 2 * NR), BF16),
        ((2, NR), F32), ((8, 2, ZR), BF16),
    ]
    n = 1152
    return call(
        attention_body,
        (H // 128,),
        [cut(2, TOK), cut(2, TOK), cut(2, 2, TOK), cut(2, 2, NR), cut(2, NR), cut(2, NR), cut(2, NR), cut(8, 2, ZR)],
        [(cut(*lead), (lead + (H,), kind)) for lead, kind in outs],
        [
            pltpu.VMEM((2, 2, n, 128), BF16), pltpu.VMEM((2, 2, 128, n), BF16), pltpu.VMEM((2, n, TOK), F32), pltpu.VMEM((2, n, TOK), F32),
            pltpu.VMEM((2, n, TOK), BF16), pltpu.VMEM((2, n, TOK), BF16), pltpu.VMEM((2, 768, 128), F32),
        ],
    )(pos, q, ag, kv, n1, yr, wr, wy, xr)


def output_body(pos, att_own, att_oth, w_own, w_oth, out):
    c = pos[0]
    out[...] = (dot(att_own[c], w_own[...]) + dot(att_oth[c], w_oth[...])).astype(BF16)


def output_side(pos, att_own, att_oth, w_out):
    row = lambda flip: pl.BlockSpec((H, D), lambda i, s: (s[0] ^ flip, 0))
    return call(
        output_body,
        (1,),
        [whole(2, TOK, H)] * 2 + [row(0), row(1)],
        [(whole(TOK, D), ((TOK, D), BF16))],
    )(pos, att_own, att_oth, w_out, w_out)[0]


def terms_body(pos, att_own, att_oth, ct_own, ct_oth, dq, xt, p_own, p_oth, out):
    c = pos[0]
    total = dot(xt[0], dq[0]) + dot(xt[1], dq[1])
    out[:, 0, 0] = total.astype(BF16).reshape(8, 96, H)
    total = None
    for e, ct in ((c, ct_own), (1 - c, ct_oth)):
        att_t = (dot_nt(p_own[...], att_own[e]) + dot_nt(p_oth[...], att_oth[e])).astype(BF16)
        term = dot(att_t, ct[...])
        total = term if total is None else total + term
    out[:, 1, 0] = total.astype(BF16).reshape(8, 96, H)


TERMS = (8, 2, 2, 96, H)


def terms_half(index):
    return pl.BlockSpec((8, 2, 1, 96, H), lambda i, s: (0, 0, index, 0, 0))


def output_terms(pos, att_own, att_oth, ct_own, ct_oth, dq, xt, perm):
    col = lambda flip, rows: pl.BlockSpec((rows, H), lambda i, s: (0, s[0] ^ flip))
    return call(
        terms_body,
        (1,),
        [whole(2, TOK, H)] * 2 + [col(0, TOK)] * 2 + [whole(2, TOK, H), whole(2, D, TOK), col(0, D), col(1, D)],
        [(terms_half(0), (TERMS, BF16))],
    )(pos, att_own, att_oth, ct_own, ct_oth, dq, xt, perm, perm)[0]


def back_body(pos, xr, out):
    hot = (iota((128, ZR), 0) == z_source(pos[1], 1, (128, ZR))).astype(BF16)
    for p in range(2):
        total = xr[0, p].astype(F32)
        for slot in range(1, 8):
            total = total + xr[slot, p].astype(F32)
        out[:, p] = dot(hot, total.astype(BF16)).astype(BF16).reshape(8, 16, H)


def back_slots(pos, xr):
    return call(
        back_body,
        (1,),
        [whole(8, 2, ZR, H)],
        [(whole(ZN, 2, 16, H), ((ZN, 2, 16, H), BF16))],
    )(pos, xr)[0]


def hand_back_body(pos, dw, dy, *outs):
    start = 0
    for out in outs:
        rows = out.shape[1]
        for p in range(2):
            total = dw[p, start : start + rows] + dy[p, NR + start : NR + start + rows].astype(F32)
            out[p] = total.astype(BF16)
        start += rows


def hand_back(pos, dw, dy):
    return call(
        hand_back_body,
        (1,),
        [whole(2, NR, H), whole(2, 2 * NR, H)],
        [(whole(2, rows, H), ((2, rows, H), BF16)) for rows in (64, 32, 32)],
    )(pos, dw, dy)


def leaf_body(pos, zr, dkv, dn1, dy, g3, g4_a, g4_b, dq, xt, _, pg_out, grad_out):
    def split(grad):
        high = grad.astype(BF16)
        return [high, (grad - high.astype(F32)).astype(BF16)]

    def hot(hit, scale):
        return jnp.where(hit, scale, 0.0).astype(BF16)

    def wide(ref):
        return jnp.concatenate([ref[0], ref[1]], axis=1)

    zs = jnp.concatenate([zr[:, p].reshape(128, H) for p in range(2)], axis=1)
    ws = jnp.concatenate([wide(g3), wide(g4_a), wide(g4_b)], axis=0)
    ys = jnp.concatenate([dy[p, :NR] for p in range(2)], axis=1)
    for e in range(2):
        t, k = iota((TOK, 128), 0), iota((TOK, 128), 1)
        far, row, chip = (k >> 4) ^ pos[1], k & 15, t + TOK * e
        first = hot(t >> 1 == k, 1.0)
        third = hot(chip >> 3 == k, 0.5)
        odd = hot((far == 1) & (row == chip >> 5), 0.25) + hot((far >= 4) & (row == chip >> 7), 0.125)
        second = hot(chip >> 2 == k, 0.5)
        fourth = hot((k >= 64) & (chip >> 4 == k & 31), 0.25)
        even = hot((far >> 1 == 1) & (row == chip >> 6), 0.125)
        up = dot(jnp.concatenate([first, first, third, odd], axis=1), jnp.concatenate(split(wide(dn1.at[e])) + [ws, zs], axis=0))
        up = up * HALF_ROOT + dot(jnp.concatenate([second, fourth, even], axis=1), jnp.concatenate([ys, ws, zs], axis=0))
        for p in range(2):
            pg_out[e, :, H * (1 + p) : H * (2 + p)] = (dkv[e, p] + up[:, H * p : H * p + H]).astype(BF16)
        pg_out[e, :, :H] = dq[e]
    for p in range(2):
        cols = slice(H * (1 + p), H * (2 + p))
        total = dot(xt[0], pg_out[0, :, cols]) + dot(xt[1], pg_out[1, :, cols])
        grad_out[:, p, 0] = total.astype(BF16).reshape(8, 96, H)


def leaf_grads(pos, zr, dkv, dn1, dy, g3, g4_a, g4_b, dq, xt, terms):
    return call(
        leaf_body,
        (1,),
        [
            whole(ZN, 2, 16, H), whole(2, 2, TOK, H), whole(2, 2, NR, H), whole(2, 2 * NR, H), whole(2, 64, H), whole(2, 32, H),
            whole(2, 32, H), whole(2, TOK, H), whole(2, D, TOK), pl.BlockSpec(memory_space=pl.ANY),
        ],
        [(whole(2, TOK, 3 * H), ((2, TOK, 3 * H), BF16)), (terms_half(1), (TERMS, BF16))],
        aliases={10: 1},
    )(pos, zr, dkv, dn1, dy, g3, g4_a, g4_b, dq, xt, terms)


def input_body(pos, pg_own, pg_oth, *rest):
    out = rest[-1]
    total = None
    for part in range(3):
        for pg, w in ((pg_own, rest[part]), (pg_oth, rest[3 + part])):
            term = dot_nt(pg[:, H * part : H * part + H], w[...])
            total = term if total is None else total + term
    out[...] = total.astype(BF16)


def input_side(pos, pg_own, pg_oth, w_qkv):
    col = lambda part, flip: pl.BlockSpec((D, H), lambda i, s: (0, 2 * part + (s[0] ^ flip)))
    return call(
        input_body,
        (1,),
        [whole(TOK, 3 * H)] * 2 + [col(part, flip) for flip in (0, 1) for part in range(3)],
        [(whole(TOK, D), ((TOK, D), BF16))],
    )(pos, pg_own, pg_oth, *[w_qkv] * 6)[0]


def total_of(refs):
    total = refs[0].astype(F32)
    for ref in refs[1:]:
        total = total + ref.astype(F32)
    return total


def middle_body(pos, terms, out):
    i, k = iota((256, 96), 0), iota((256, 96), 1)
    row, half = i & 7, (i >> 3) & 1
    hit = (k == 6 * (i >> 4) + row) & (row < 6)
    rows = None
    for group in range(2):
        total = total_of([terms[slot, group] for slot in range(16)]).astype(BF16)
        part = dot((hit & (half == group)).astype(BF16), total)
        rows = part if rows is None else rows + part
    out[...] = rows.astype(BF16).reshape(ZN, 2, 16, H)


def middle_sum(pos, terms):
    shape = (ZN, 2, 16, H)
    return call(middle_body, (1,), [whole(16, 2, 96, H)], [(whole(*shape), (shape, BF16))])(pos, terms)[0]


def z_sum_body(pos, terms, own_out, oth_out):
    for core, out in ((pos[0], own_out), (1 - pos[0], oth_out)):
        out[...] = total_of([terms[z, core] for z in range(ZN)]).astype(BF16)


def z_sum(pos, terms):
    return call(
        z_sum_body,
        (1,),
        [whole(ZN, 2, 16, H)],
        [(whole(16, H), ((16, H), BF16))] * 2,
    )(pos, terms)


def last_body(pos, own, from_dp, from_core, from_both, qkv_out, out_out, parts):
    core, dp = pos[0], pos[3]
    parts[core, dp] = own[...]
    parts[core, 1 - dp] = from_dp[...]
    parts[1 - core, dp] = from_core[...]
    parts[1 - core, 1 - dp] = from_both[...]
    for core in range(2):
        low, high = parts[core, 0].astype(F32), parts[core, 1].astype(F32)
        cols = lambda part: slice(D * part + H * core, D * part + H * core + H)
        qkv_out[:, cols(0)] = low[:6]
        qkv_out[:, cols(1)] = low[8:14]
        qkv_out[:, cols(2)] = high[8:14]
        out_out[:, cols(0)] = high[:6]


def last_rows(pos, *parts):
    return call(
        last_body,
        (1,),
        [whole(16, H)] * 4,
        [(whole(6, 3 * D), ((6, 3 * D), F32)), (whole(6, D), ((6, D), F32))],
        [pltpu.VMEM((2, 2, 16, H), BF16)],
    )(pos, *parts)


def swap(value, axis):
    return lax.ppermute(value, axis, [(0, 1), (1, 0)])


def along(value, axes, far, count=4):
    return lax.ppermute(value, axes, [(i, i ^ far) for i in range(count)])


def row_order():
    f = np.arange(D)
    source = 96 * (f // 12 % 8) + 12 * (f // 96) + f % 12
    return jnp.asarray(source[:, None] == f[None, :], BF16)


def shards(x_tokens, cotangent, w_qkv, w_out):
    x_own, ct_own = x_tokens[0], cotangent[0]
    c, z, dp = lax.axis_index("c"), lax.axis_index("z"), lax.axis_index("dp")
    j = 2 * lax.axis_index("x") + lax.axis_index("y")
    pos = jnp.stack([c, z, j, dp]).astype(jnp.int32)
    x_oth, ct_oth = swap(x_own, "c"), swap(ct_own, "c")
    perm = row_order()

    kv, n1, n2, n3, n4, zs = tree(pos, x_own, x_oth, w_qkv)
    yr = swap(n2, "y")
    wr = jnp.concatenate([along(n3, "x", 1), along(n4, "x", 2), along(n4, "x", 3)], axis=1)
    wy = swap(wr, "y")
    zr = lax.all_to_all(zs, "z", 0, 0)
    zr, yr, wy, ct_oth = lax.optimization_barrier((zr, yr, wy, ct_oth))
    xr = lax.all_to_all(plane_slots(pos, zr), ("x", "y"), 0, 0)
    q, ag, xt = project(pos, x_own, x_oth, ct_own, ct_oth, w_qkv, w_out, perm)
    att, dq, dkv, dn1, dy, dw, dx = attention(pos, q, ag, kv, n1, yr, wr, wy, xr)

    dx_r = lax.all_to_all(dx, ("x", "y"), 0, 0)
    att_oth = swap(att, "c")
    dy = swap(dy, "y")
    terms = output_terms(pos, att, att_oth, ct_own, ct_oth, dq, xt, perm)
    dx_r, terms, dy = lax.optimization_barrier((dx_r, terms, dy))
    dz_r = lax.all_to_all(back_slots(pos, dx_r), "z", 0, 0)
    g3, g4_a, g4_b = hand_back(pos, dw, dy)
    g3, g4_a, g4_b = along(g3, "x", 1), along(g4_a, "x", 2), along(g4_b, "x", 3)
    dz_r, g3, g4_a, g4_b = lax.optimization_barrier((dz_r, g3, g4_a, g4_b))
    pg, terms = leaf_grads(pos, dz_r, dkv, dn1, dy, g3, g4_a, g4_b, dq, xt, terms)
    terms = lax.all_to_all(terms.reshape(16, 2, 96, H), ("x", "y", "dp"), 0, 0)
    pg_own = lax.dynamic_index_in_dim(pg, c, 0, keepdims=False)
    pg_oth = swap(lax.dynamic_index_in_dim(pg, 1 - c, 0, keepdims=False), "c")
    input_grad = input_side(pos, pg_own, pg_oth, w_qkv)
    layer_out = output_side(pos, att, att_oth, w_out)
    terms, input_grad, layer_out = lax.optimization_barrier((terms, input_grad, layer_out))
    terms = lax.all_to_all(middle_sum(pos, terms), "z", 0, 0)
    own, oth = z_sum(pos, terms)
    pair = ("c", "dp")
    qkv_grad, out_grad = last_rows(pos, own, along(own, pair, 1), along(oth, pair, 2), along(oth, pair, 3))
    return (layer_out[None], input_grad[None], qkv_grad, out_grad)


def solution(mesh):
    split = Mesh(mesh.devices.reshape(ZN, XN, YN, 2, 2), ("z", "x", "y", "c", "dp"))
    seq = ("z", "x", "y", "c")
    return jax.shard_map(
        shards,
        mesh=split,
        in_specs=(P("dp", seq, None), P("dp", seq, None), P(), P()),
        out_specs=(P("dp", seq, None), P("dp", seq, None), P(seq, None), P(seq, None)),
        check_vma=False,
    )
```

```python
import jax
import jax.numpy as jnp
import numpy as np
from jax import lax
from jax.experimental import pallas as pl
from jax.experimental.pallas import tpu as pltpu
from jax.sharding import Mesh, PartitionSpec as P

D = 768
H = 384
TOK = 256
NR = 128
DH = 64
ZN, XN, YN = 8, 4, 2
ZR = 48
HALF_ROOT = 0.7071067811865476
LOG2E = 1.4426950408889634
VMEM = 56 * 1024 * 1024
F32 = jnp.float32
BF16 = jnp.bfloat16


def dot(a, b):
    return lax.dot_general(a, b, (((1,), (0,)), ((), ())), preferred_element_type=F32)


def dot_nt(a, b):
    return lax.dot_general(a, b, (((1,), (1,)), ((), ())), preferred_element_type=F32)


def dot_tn(a, b):
    return lax.dot_general(a, b, (((0,), (0,)), ((), ())), preferred_element_type=F32)


def iota(shape, axis):
    return lax.broadcasted_iota(jnp.int32, shape, axis)


def pair_matrix(rows, cols, valid):
    r, k = iota((rows, cols), 0), iota((rows, cols), 1)
    return (((k >> 1) == r) & (r < valid)).astype(BF16)


def coarsen(node, rows=None, valid=None):
    rows = node.shape[0] // 2 if rows is None else rows
    valid = rows if valid is None else valid
    return (dot(pair_matrix(rows, node.shape[0], valid), node) * HALF_ROOT).astype(BF16)


def whole(*shape):
    return pl.BlockSpec(shape, lambda *_: (0,) * len(shape))


def call(body, grid, ins, outs, scratch=()):
    return pl.pallas_call(
        body,
        grid_spec=pltpu.PrefetchScalarGridSpec(
            num_scalar_prefetch=1,
            grid=grid,
            in_specs=ins,
            out_specs=[s for s, _ in outs],
            scratch_shapes=list(scratch),
        ),
        out_shape=[jax.ShapeDtypeStruct(shape, kind) for _, (shape, kind) in outs],
        compiler_params=pltpu.CompilerParams(vmem_limit_bytes=VMEM),
    )


def tree_body(pos, x_own, x_oth, wk, wv, kv_out, n1_out, n2_out, n3_out, n4_out, zs_out):
    c, z = pos[0], pos[1]
    for e, x in ((c, x_own), (1 - c, x_oth)):
        kv_out[e, 0] = dot(x[...], wk[...]).astype(BF16)
        kv_out[e, 1] = dot(x[...], wv[...]).astype(BF16)

    def store(ref, *index):
        def put(node):
            for p in range(2):
                ref[index + (p,)] = node[:, H * p : H * p + H]

        return put

    halves = []
    for e in range(2):
        n1 = coarsen(jnp.concatenate([kv_out[e, 0], kv_out[e, 1]], axis=1))
        store(n1_out, e)(n1)
        halves.append(coarsen(n1))
    n2 = jnp.concatenate(halves, axis=0)
    store(n2_out)(n2)
    n3 = coarsen(n2)
    store(n3_out)(n3)
    n4 = coarsen(n3)
    store(n4_out)(n4)
    n5 = coarsen(n4)
    n6 = coarsen(n5, 16, 8)
    n7 = coarsen(n6, 16, 4)
    store(zs_out, z)(jnp.zeros_like(n5))
    store(zs_out, z ^ 1)(n5)
    for far in (2, 3):
        store(zs_out, z ^ far)(n6)
    for far in (4, 5, 6, 7):
        store(zs_out, z ^ far)(n7)


def tree(pos, x_own, x_oth, w_qkv):
    col = lambda part: pl.BlockSpec((D, H), lambda i, s: (0, 2 * part + s[0]))
    outs = [(2, 2, TOK, H), (2, 2, NR, H), (2, NR, H), (2, 64, H), (2, 32, H), (ZN, 2, 16, H)]
    return call(
        tree_body,
        (1,),
        [whole(TOK, D)] * 2 + [col(1), col(2)],
        [(whole(*shape), (shape, BF16)) for shape in outs],
    )(pos, x_own, x_oth, w_qkv, w_qkv)


def project_body(pos, x_own, x_oth, ct_own, ct_oth, wq, wo, perm, q_out, ag_out, xt_out):
    c = pos[0]
    for e, x, ct in ((c, x_own, ct_own), (1 - c, x_oth, ct_oth)):
        q_out[e] = dot(x[...], wq[...]).astype(BF16)
        ag_out[e] = dot_nt(ct[...], wo[...]).astype(BF16)
        xt_out[e] = dot_nt(perm[...], x[...]).astype(BF16)


def project(pos, x_own, x_oth, ct_own, ct_oth, w_qkv, w_out, perm):
    outs = [(2, TOK, H), (2, TOK, H), (2, D, TOK)]
    return call(
        project_body,
        (1,),
        [whole(TOK, D)] * 4
        + [pl.BlockSpec((D, H), lambda i, s: (0, s[0])), pl.BlockSpec((H, D), lambda i, s: (s[0], 0)), whole(D, D)],
        [(whole(*shape), (shape, BF16)) for shape in outs],
    )(pos, x_own, x_oth, ct_own, ct_oth, w_qkv, w_out, perm)


def z_source(z, rows_axis, shape):
    i = iota(shape, rows_axis)
    near = 16 * (z ^ 1) + i
    mid = 16 * (z ^ (2 + ((i - 16) >> 3))) + ((i - 16) & 7)
    far = 16 * (z ^ (4 + ((i - 32) >> 2))) + ((i - 32) & 3)
    return jnp.where(i < 16, near, jnp.where(i < 32, mid, far))


def plane_body(pos, zr, out):
    hot = (iota((ZR, 128), 1) == z_source(pos[1], 0, (ZR, 128))).astype(BF16)
    both = jnp.concatenate([zr[:, p].reshape(128, H) for p in range(2)], axis=1)
    rows = dot(hot, both).astype(BF16)
    for slot in range(8):
        for p in range(2):
            out[slot, p] = rows[:, H * p : H * p + H]


def plane_slots(pos, zr):
    return call(
        plane_body,
        (1,),
        [whole(ZN, 2, 16, H)],
        [(whole(8, 2, ZR, H), ((8, 2, ZR, H), BF16))],
    )(pos, zr)[0]


def attention_body(pos, q, ag, kv, n1, yr, wr, wy, xr, att_out, dq_out, dkv_out, dn1_out, dy_out, dwy_out, dw_out, dx_out, keys, keys_t, s_ref, dw_ref, w_ref, ds_ref, drem):
    for p in range(2):
        for e in range(2):
            keys[e, p, :256] = kv[e, p]
            keys[e, p, 256:384] = n1[1 - e, p]
            keys[e, p, 384:512] = yr[p]
            keys[e, p, 512:640] = wr[p]
            keys[e, p, 640:768] = wy[p]
            for slot in range(8):
                start = 768 + ZR * slot
                keys[e, p, start : start + ZR] = xr[slot, p]
    for p in range(2):
        for e in range(2):
            keys_t[e, p] = keys[e, p].T
    lane = iota((TOK, 128), 1)
    steps = [(e, h) for e in range(2) for h in range(2)]
    masked = {}

    def scores(step):
        e, h = steps[step]
        mine = (lane >> 6) == h
        qh = jnp.where(mine, q[e], jnp.zeros((), BF16))
        ah = jnp.where(mine, ag[e], jnp.zeros((), BF16))
        masked[step] = (qh, ah)
        s_ref[step % 2] = dot_nt(keys[e, 0], qh)
        dw_ref[step % 2] = dot_nt(keys[e, 1], ah)

    scores(0)
    for step, (e, h) in enumerate(steps):
        if step + 1 < len(steps):
            scores(step + 1)
        if h == 0:
            att_t, dq_t = [], []
            dk = dv = None
        s, dw, b = s_ref.at[step % 2], dw_ref.at[step % 2], step % 2
        qh, ah = masked[step]
        top = jnp.max(s[...], axis=0, keepdims=True)
        un = jnp.exp2((s[...] - top) * (LOG2E * DH ** -0.5))
        s[...] = un
        inverse = 1.0 / jnp.sum(un, axis=0, keepdims=True)
        delta = jnp.sum(un * dw[...], axis=0, keepdims=True) * inverse
        prob = s[...] * inverse
        w_ref[b] = prob.astype(BF16)
        ds_ref[b] = (prob * ((dw[...] - delta) * DH ** -0.5)).astype(BF16)
        att_t.append(dot(keys_t[e, 1, 64 * h : 64 * h + 64], w_ref[b]))
        dq_t.append(dot(keys_t[e, 0, 64 * h : 64 * h + 64], ds_ref[b]))
        dkh, dvh = dot(ds_ref[b], qh), dot(w_ref[b], ah)
        dk = dkh if dk is None else dk + dkh
        dv = dvh if dv is None else dv + dvh
        if h == 0:
            continue
        att_out[e] = jnp.concatenate(att_t, axis=0).T.astype(BF16)
        dq_out[e] = jnp.concatenate(dq_t, axis=0).T.astype(BF16)
        for p, grad in ((0, dk), (1, dv)):
            dkv_out[e, p] = grad[:256]
            dn1_out[1 - e, p] = grad[256:384]
            if e == 0:
                drem[p] = grad[384:]
            else:
                drem[p] = drem[p] + grad[384:]
    for p in range(2):
        rows = drem[p].astype(BF16)
        dy_out[p] = rows[:128]
        dwy_out[p] = rows[256:384]
        dw_out[p] = drem[p, 128:256]
        for slot in range(8):
            start = 384 + ZR * slot
            dx_out[slot, p] = rows[start : start + ZR]


def attention(pos, q, ag, kv, n1, yr, wr, wy, xr):
    def cut(*lead):
        return pl.BlockSpec(lead + (128,), lambda i, s: (0,) * len(lead) + (i,))

    outs = [
        ((2, TOK), BF16), ((2, TOK), BF16), ((2, 2, TOK), F32), ((2, 2, NR), F32), ((2, NR), BF16), ((2, NR), BF16),
        ((2, NR), F32), ((8, 2, ZR), BF16),
    ]
    n = 1152
    return call(
        attention_body,
        (H // 128,),
        [cut(2, TOK), cut(2, TOK), cut(2, 2, TOK), cut(2, 2, NR), cut(2, NR), cut(2, NR), cut(2, NR), cut(8, 2, ZR)],
        [(cut(*lead), (lead + (H,), kind)) for lead, kind in outs],
        [
            pltpu.VMEM((2, 2, n, 128), BF16), pltpu.VMEM((2, 2, 128, n), BF16), pltpu.VMEM((2, n, TOK), F32), pltpu.VMEM((2, n, TOK), F32),
            pltpu.VMEM((2, n, TOK), BF16), pltpu.VMEM((2, n, TOK), BF16), pltpu.VMEM((2, 768, 128), F32),
        ],
    )(pos, q, ag, kv, n1, yr, wr, wy, xr)


def output_body(pos, att_own, att_oth, w_own, w_oth, out):
    c = pos[0]
    out[...] = (dot(att_own[c], w_own[...]) + dot(att_oth[c], w_oth[...])).astype(BF16)


def output_side(pos, att_own, att_oth, w_out):
    row = lambda flip: pl.BlockSpec((H, D), lambda i, s: (s[0] ^ flip, 0))
    return call(
        output_body,
        (1,),
        [whole(2, TOK, H)] * 2 + [row(0), row(1)],
        [(whole(TOK, D), ((TOK, D), BF16))],
    )(pos, att_own, att_oth, w_out, w_out)[0]


def terms_body(pos, att_own, att_oth, ct_own, ct_oth, dq, xt, p_own, p_oth, *rest):
    c, x = pos[0], pos[2] >> 1
    slots = rest[-1]
    total = dot(xt[0], dq[0]) + dot(xt[1], dq[1])
    slots[:, :, 0] = total.astype(BF16).reshape(XN, YN, 96, H)
    total = None
    for e, ct in ((c, ct_own), (1 - c, ct_oth)):
        att_t = (dot_nt(p_own[...], att_own[e]) + dot_nt(p_oth[...], att_oth[e])).astype(BF16)
        term = dot(att_t, ct[...])
        total = term if total is None else total + term
    slots[:, :, 1] = total.astype(BF16).reshape(XN, YN, 96, H)
    for far in range(XN):
        rest[far][...] = slots[x ^ far]


def output_terms(pos, att_own, att_oth, ct_own, ct_oth, dq, xt, perm):
    col = lambda flip, rows: pl.BlockSpec((rows, H), lambda i, s: (0, s[0] ^ flip))
    slot = (YN, 2, 96, H)
    return call(
        terms_body,
        (1,),
        [whole(2, TOK, H)] * 2 + [col(0, TOK)] * 2 + [whole(2, TOK, H), whole(2, D, TOK), col(0, D), col(1, D)],
        [(whole(*slot), (slot, BF16))] * XN,
        [pltpu.VMEM((XN,) + slot, BF16)],
    )(pos, att_own, att_oth, ct_own, ct_oth, dq, xt, perm, perm)


def x_sum_body(pos, t0, t1, t2, t3, *rest):
    y, dp = pos[2] & 1, pos[3]
    slots = rest[-1]
    total = (t0[...].astype(F32) + t1[...].astype(F32)) + (t2[...].astype(F32) + t3[...].astype(F32))
    slots[...] = total.astype(BF16)
    for far in range(4):
        rest[far][...] = slots[y ^ (far >> 1), dp ^ (far & 1)]


def x_sum(pos, *terms):
    shape = (YN, 2, 96, H)
    return call(
        x_sum_body,
        (1,),
        [whole(*shape)] * 4,
        [(whole(96, H), ((96, H), BF16))] * 4,
        [pltpu.VMEM(shape, BF16)],
    )(pos, *terms)


def back_body(pos, xr, out):
    hot = (iota((128, ZR), 0) == z_source(pos[1], 1, (128, ZR))).astype(BF16)
    for p in range(2):
        total = xr[0, p].astype(F32)
        for slot in range(1, 8):
            total = total + xr[slot, p].astype(F32)
        out[:, p] = dot(hot, total.astype(BF16)).astype(BF16).reshape(8, 16, H)


def back_slots(pos, xr):
    return call(
        back_body,
        (1,),
        [whole(8, 2, ZR, H)],
        [(whole(ZN, 2, 16, H), ((ZN, 2, 16, H), BF16))],
    )(pos, xr)[0]


def hand_back_body(pos, dw, dwy, *outs):
    start = 0
    for out in outs:
        rows = out.shape[1]
        for p in range(2):
            total = dw[p, start : start + rows] + dwy[p, start : start + rows].astype(F32)
            out[p] = total.astype(BF16)
        start += rows


def hand_back(pos, dw, dwy):
    return call(
        hand_back_body,
        (1,),
        [whole(2, NR, H)] * 2,
        [(whole(2, rows, H), ((2, rows, H), BF16)) for rows in (64, 32, 32)],
    )(pos, dw, dwy)


def leaf_body(pos, zr, dkv, dn1, dy, g3, g4_a, g4_b, dq, xt, pg_out, grad_out):
    def split(grad):
        high = grad.astype(BF16)
        return [high, (grad - high.astype(F32)).astype(BF16)]

    def hot(hit, scale):
        return jnp.where(hit, scale, 0.0).astype(BF16)

    def wide(ref):
        return jnp.concatenate([ref[0], ref[1]], axis=1)

    zs = jnp.concatenate([zr[:, p].reshape(128, H) for p in range(2)], axis=1)
    ws = jnp.concatenate([wide(g3), wide(g4_a), wide(g4_b)], axis=0)
    ys = wide(dy)
    for e in range(2):
        t, k = iota((TOK, 128), 0), iota((TOK, 128), 1)
        far, row, chip = (k >> 4) ^ pos[1], k & 15, t + TOK * e
        first = hot(t >> 1 == k, 1.0)
        third = hot(chip >> 3 == k, 0.5)
        odd = hot((far == 1) & (row == chip >> 5), 0.25) + hot((far >= 4) & (row == chip >> 7), 0.125)
        second = hot(chip >> 2 == k, 0.5)
        fourth = hot((k >= 64) & (chip >> 4 == k & 31), 0.25)
        even = hot((far >> 1 == 1) & (row == chip >> 6), 0.125)
        up = dot(jnp.concatenate([first, first, third, odd], axis=1), jnp.concatenate(split(wide(dn1.at[e])) + [ws, zs], axis=0))
        up = up * HALF_ROOT + dot(jnp.concatenate([second, fourth, even], axis=1), jnp.concatenate([ys, ws, zs], axis=0))
        for p in range(2):
            pg_out[e, :, H * (1 + p) : H * (2 + p)] = (dkv[e, p] + up[:, H * p : H * p + H]).astype(BF16)
        pg_out[e, :, :H] = dq[e]
    for p in range(2):
        cols = slice(H * (1 + p), H * (2 + p))
        total = dot(xt[0], pg_out[0, :, cols]) + dot(xt[1], pg_out[1, :, cols])
        grad_out[:, p] = total.astype(BF16).reshape(8, 96, H)


def leaf_grads(pos, zr, dkv, dn1, dy, g3, g4_a, g4_b, dq, xt):
    return call(
        leaf_body,
        (1,),
        [
            whole(ZN, 2, 16, H), whole(2, 2, TOK, H), whole(2, 2, NR, H), whole(2, NR, H), whole(2, 64, H), whole(2, 32, H),
            whole(2, 32, H), whole(2, TOK, H), whole(2, D, TOK),
        ],
        [(whole(2, TOK, 3 * H), ((2, TOK, 3 * H), BF16)), (whole(8, 2, 96, H), ((8, 2, 96, H), BF16))],
    )(pos, zr, dkv, dn1, dy, g3, g4_a, g4_b, dq, xt)


def input_body(pos, pg_own, pg_oth, *rest):
    out = rest[-1]
    total = None
    for part in range(3):
        for pg, w in ((pg_own, rest[part]), (pg_oth, rest[3 + part])):
            term = dot_nt(pg[:, H * part : H * part + H], w[...])
            total = term if total is None else total + term
    out[...] = total.astype(BF16)


def input_side(pos, pg_own, pg_oth, w_qkv):
    col = lambda part, flip: pl.BlockSpec((D, H), lambda i, s: (0, 2 * part + (s[0] ^ flip)))
    return call(
        input_body,
        (1,),
        [whole(TOK, 3 * H)] * 2 + [col(part, flip) for flip in (0, 1) for part in range(3)],
        [(whole(TOK, D), ((TOK, D), BF16))],
    )(pos, pg_own, pg_oth, *[w_qkv] * 6)[0]


def total_of(refs):
    total = refs[0].astype(F32)
    for ref in refs[1:]:
        total = total + ref.astype(F32)
    return total


def middle_body(pos, f0, f1, f2, f3, second, out):
    first = total_of([f0[...], f1[...], f2[...], f3[...]]).astype(BF16)
    i, k = iota((256, 96), 0), iota((256, 96), 1)
    row, half = i & 7, (i >> 3) & 1
    hit = (k == 6 * (i >> 4) + row) & (row < 6)
    rows = dot((hit & (half == 0)).astype(BF16), first)
    rows = rows + dot((hit & (half == 1)).astype(BF16), total_of([second[slot] for slot in range(16)]).astype(BF16))
    out[...] = rows.astype(BF16).reshape(ZN, 2, 16, H)


def middle_sum(pos, firsts, second):
    shape = (ZN, 2, 16, H)
    return call(
        middle_body, (1,), [whole(96, H)] * 4 + [whole(16, 96, H)], [(whole(*shape), (shape, BF16))]
    )(pos, *firsts, second)[0]


def z_sum_body(pos, terms, own_out, oth_out):
    for core, out in ((pos[0], own_out), (1 - pos[0], oth_out)):
        out[...] = total_of([terms[z, core] for z in range(ZN)]).astype(BF16)


def z_sum(pos, terms):
    return call(
        z_sum_body,
        (1,),
        [whole(ZN, 2, 16, H)],
        [(whole(16, H), ((16, H), BF16))] * 2,
    )(pos, terms)


def last_body(pos, own, from_dp, from_core, from_both, qkv_out, out_out, parts):
    core, dp = pos[0], pos[3]
    parts[core, dp] = own[...]
    parts[core, 1 - dp] = from_dp[...]
    parts[1 - core, dp] = from_core[...]
    parts[1 - core, 1 - dp] = from_both[...]
    for core in range(2):
        low, high = parts[core, 0].astype(F32), parts[core, 1].astype(F32)
        cols = lambda part: slice(D * part + H * core, D * part + H * core + H)
        qkv_out[:, cols(0)] = low[:6]
        qkv_out[:, cols(1)] = low[8:14]
        qkv_out[:, cols(2)] = high[8:14]
        out_out[:, cols(0)] = high[:6]


def last_rows(pos, *parts):
    return call(
        last_body,
        (1,),
        [whole(16, H)] * 4,
        [(whole(6, 3 * D), ((6, 3 * D), F32)), (whole(6, D), ((6, D), F32))],
        [pltpu.VMEM((2, 2, 16, H), BF16)],
    )(pos, *parts)


def swap(value, axis):
    return lax.ppermute(value, axis, [(0, 1), (1, 0)])


def along(value, axes, far, count=4):
    return lax.ppermute(value, axes, [(i, i ^ far) for i in range(count)])


def row_order():
    f = np.arange(D)
    source = 96 * (f // 12 % 8) + 12 * (f // 96) + f % 12
    return jnp.asarray(source[:, None] == f[None, :], BF16)


def shards(x_tokens, cotangent, w_qkv, w_out):
    x_own, ct_own = x_tokens[0], cotangent[0]
    c, z, dp = lax.axis_index("c"), lax.axis_index("z"), lax.axis_index("dp")
    j = 2 * lax.axis_index("x") + lax.axis_index("y")
    pos = jnp.stack([c, z, j, dp]).astype(jnp.int32)
    x_oth, ct_oth = swap(x_own, "c"), swap(ct_own, "c")
    perm = row_order()

    kv, n1, n2, n3, n4, zs = tree(pos, x_own, x_oth, w_qkv)
    yr = swap(n2, "y")
    wr = jnp.concatenate([along(n3, "x", 1), along(n4, "x", 2), along(n4, "x", 3)], axis=1)
    wy = swap(wr, "y")
    zr = lax.all_to_all(zs, "z", 0, 0)
    zr, yr, wy, ct_oth = lax.optimization_barrier((zr, yr, wy, ct_oth))
    xr = lax.all_to_all(plane_slots(pos, zr), ("x", "y"), 0, 0)
    q, ag, xt = project(pos, x_own, x_oth, ct_own, ct_oth, w_qkv, w_out, perm)
    att, dq, dkv, dn1, dy, dwy, dw, dx = attention(pos, q, ag, kv, n1, yr, wr, wy, xr)

    dx_r = lax.all_to_all(dx, ("x", "y"), 0, 0)
    att_oth = swap(att, "c")
    dwy = swap(dwy, "y")
    first, *firsts = output_terms(pos, att, att_oth, ct_own, ct_oth, dq, xt, perm)
    firsts = [along(firsts[far - 1], "x", far) for far in (1, 2, 3)]
    dx_r, first, firsts[0], dwy = lax.optimization_barrier((dx_r, first, firsts[0], dwy))
    dz_r = lax.all_to_all(back_slots(pos, dx_r), "z", 0, 0)
    dw, dwy, firsts = lax.optimization_barrier((dw, dwy, firsts))
    g3, g4_a, g4_b = hand_back(pos, dw, dwy)
    g3, g4_a, g4_b = along(g3, "x", 1), along(g4_a, "x", 2), along(g4_b, "x", 3)
    firsts = x_sum(pos, first, *firsts)
    firsts = list(firsts[:1]) + [along(firsts[far], ("y", "dp"), far) for far in (1, 2, 3)]
    dz_r, g3, g4_a, g4_b, firsts = lax.optimization_barrier((dz_r, g3, g4_a, g4_b, firsts))
    pg, terms = leaf_grads(pos, dz_r, dkv, dn1, swap(dy, "y"), g3, g4_a, g4_b, dq, xt)
    terms = lax.all_to_all(terms.reshape(16, 96, H), ("x", "y", "dp"), 0, 0)
    pg_own = lax.dynamic_index_in_dim(pg, c, 0, keepdims=False)
    pg_oth = swap(lax.dynamic_index_in_dim(pg, 1 - c, 0, keepdims=False), "c")
    input_grad = input_side(pos, pg_own, pg_oth, w_qkv)
    layer_out = output_side(pos, att, att_oth, w_out)
    terms, input_grad, layer_out = lax.optimization_barrier((terms, input_grad, layer_out))
    terms = lax.all_to_all(middle_sum(pos, firsts, terms), "z", 0, 0)
    own, oth = z_sum(pos, terms)
    pair = ("c", "dp")
    qkv_grad, out_grad = last_rows(pos, own, along(own, pair, 1), along(oth, pair, 2), along(oth, pair, 3))
    return (layer_out[None], input_grad[None], qkv_grad, out_grad)


def solution(mesh):
    split = Mesh(mesh.devices.reshape(ZN, XN, YN, 2, 2), ("z", "x", "y", "c", "dp"))
    seq = ("z", "x", "y", "c")
    return jax.shard_map(
        shards,
        mesh=split,
        in_specs=(P("dp", seq, None), P("dp", seq, None), P(), P()),
        out_specs=(P("dp", seq, None), P("dp", seq, None), P(seq, None), P(seq, None)),
        check_vma=False,
    )
```

```python
import jax
import jax.numpy as jnp
import numpy as np
from jax import lax
from jax.experimental import pallas as pl
from jax.experimental.pallas import tpu as pltpu
from jax.sharding import Mesh, PartitionSpec as P

D = 768
H = 384
TOK = 256
NR = 128
DH = 64
ZN, XN, YN = 8, 4, 2
ZR = 48
HALF_ROOT = 0.7071067811865476
LOG2E = 1.4426950408889634
VMEM = 56 * 1024 * 1024
F32 = jnp.float32
BF16 = jnp.bfloat16


def dot(a, b):
    return lax.dot_general(a, b, (((1,), (0,)), ((), ())), preferred_element_type=F32)


def dot_nt(a, b):
    return lax.dot_general(a, b, (((1,), (1,)), ((), ())), preferred_element_type=F32)


def dot_tn(a, b):
    return lax.dot_general(a, b, (((0,), (0,)), ((), ())), preferred_element_type=F32)


def iota(shape, axis):
    return lax.broadcasted_iota(jnp.int32, shape, axis)


def pair_matrix(rows, cols, valid):
    r, k = iota((rows, cols), 0), iota((rows, cols), 1)
    return (((k >> 1) == r) & (r < valid)).astype(BF16)


def coarsen(node, rows=None, valid=None):
    rows = node.shape[0] // 2 if rows is None else rows
    valid = rows if valid is None else valid
    return (dot(pair_matrix(rows, node.shape[0], valid), node) * HALF_ROOT).astype(BF16)


def whole(*shape):
    return pl.BlockSpec(shape, lambda *_: (0,) * len(shape))


def call(body, grid, ins, outs, scratch=()):
    return pl.pallas_call(
        body,
        grid_spec=pltpu.PrefetchScalarGridSpec(
            num_scalar_prefetch=1,
            grid=grid,
            in_specs=ins,
            out_specs=[s for s, _ in outs],
            scratch_shapes=list(scratch),
        ),
        out_shape=[jax.ShapeDtypeStruct(shape, kind) for _, (shape, kind) in outs],
        compiler_params=pltpu.CompilerParams(vmem_limit_bytes=VMEM),
    )


def tree_body(pos, x_own, x_oth, wk, wv, kv_out, n1_out, n2_out, n3_out, n4_out, zs_out):
    c, z = pos[0], pos[1]
    for e, x in ((c, x_own), (1 - c, x_oth)):
        kv_out[e, 0] = dot(x[...], wk[...]).astype(BF16)
        kv_out[e, 1] = dot(x[...], wv[...]).astype(BF16)

    def store(ref, *index):
        def put(node):
            for p in range(2):
                ref[index + (p,)] = node[:, H * p : H * p + H]

        return put

    halves = []
    for e in range(2):
        n1 = coarsen(jnp.concatenate([kv_out[e, 0], kv_out[e, 1]], axis=1))
        store(n1_out, e)(n1)
        halves.append(coarsen(n1))
    n2 = jnp.concatenate(halves, axis=0)
    store(n2_out)(n2)
    n3 = coarsen(n2)
    store(n3_out)(n3)
    n4 = coarsen(n3)
    store(n4_out)(n4)
    n5 = coarsen(n4)
    n6 = coarsen(n5, 16, 8)
    n7 = coarsen(n6, 16, 4)
    store(zs_out, z)(jnp.zeros_like(n5))
    store(zs_out, z ^ 1)(n5)
    for far in (2, 3):
        store(zs_out, z ^ far)(n6)
    for far in (4, 5, 6, 7):
        store(zs_out, z ^ far)(n7)


def tree(pos, x_own, x_oth, w_qkv):
    col = lambda part: pl.BlockSpec((D, H), lambda i, s: (0, 2 * part + s[0]))
    outs = [(2, 2, TOK, H), (2, 2, NR, H), (2, NR, H), (2, 64, H), (2, 32, H), (ZN, 2, 16, H)]
    return call(
        tree_body,
        (1,),
        [whole(TOK, D)] * 2 + [col(1), col(2)],
        [(whole(*shape), (shape, BF16)) for shape in outs],
    )(pos, x_own, x_oth, w_qkv, w_qkv)


def project_body(pos, x_own, x_oth, ct_own, ct_oth, wq, wo, perm, q_out, ag_out, xt_out):
    c = pos[0]
    for e, x, ct in ((c, x_own, ct_own), (1 - c, x_oth, ct_oth)):
        q_out[e] = dot(x[...], wq[...]).astype(BF16)
        ag_out[e] = dot_nt(ct[...], wo[...]).astype(BF16)
        xt_out[e] = dot_nt(perm[...], x[...]).astype(BF16)


def project(pos, x_own, x_oth, ct_own, ct_oth, w_qkv, w_out, perm):
    outs = [(2, TOK, H), (2, TOK, H), (2, D, TOK)]
    return call(
        project_body,
        (1,),
        [whole(TOK, D)] * 4
        + [pl.BlockSpec((D, H), lambda i, s: (0, s[0])), pl.BlockSpec((H, D), lambda i, s: (s[0], 0)), whole(D, D)],
        [(whole(*shape), (shape, BF16)) for shape in outs],
    )(pos, x_own, x_oth, ct_own, ct_oth, w_qkv, w_out, perm)


def z_source(z, rows_axis, shape):
    i = iota(shape, rows_axis)
    near = 16 * (z ^ 1) + i
    mid = 16 * (z ^ (2 + ((i - 16) >> 3))) + ((i - 16) & 7)
    far = 16 * (z ^ (4 + ((i - 32) >> 2))) + ((i - 32) & 3)
    return jnp.where(i < 16, near, jnp.where(i < 32, mid, far))


def plane_body(pos, zr, out):
    hot = (iota((ZR, 128), 1) == z_source(pos[1], 0, (ZR, 128))).astype(BF16)
    both = jnp.concatenate([zr[:, p].reshape(128, H) for p in range(2)], axis=1)
    rows = dot(hot, both).astype(BF16)
    for slot in range(8):
        for p in range(2):
            out[slot, p] = rows[:, H * p : H * p + H]


def plane_slots(pos, zr):
    return call(
        plane_body,
        (1,),
        [whole(ZN, 2, 16, H)],
        [(whole(8, 2, ZR, H), ((8, 2, ZR, H), BF16))],
    )(pos, zr)[0]


def attention_body(pos, q, ag, kv, n1, yr, wr, wy, xr, att_out, dq_out, dkv_out, dn1_out, dy_out, dwy_out, dw_out, dx_out, keys, keys_t, s_ref, dw_ref, w_ref, ds_ref, drem):
    for p in range(2):
        for e in range(2):
            keys[e, p, :256] = kv[e, p]
            keys[e, p, 256:384] = n1[1 - e, p]
            keys[e, p, 384:512] = yr[p]
            keys[e, p, 512:640] = wr[p]
            keys[e, p, 640:768] = wy[p]
            for slot in range(8):
                start = 768 + ZR * slot
                keys[e, p, start : start + ZR] = xr[slot, p]
    for p in range(2):
        for e in range(2):
            keys_t[e, p] = keys[e, p].T
    lane = iota((TOK, 128), 1)
    steps = [(e, h) for e in range(2) for h in range(2)]
    masked = {}

    def scores(step):
        e, h = steps[step]
        mine = (lane >> 6) == h
        qh = jnp.where(mine, q[e], jnp.zeros((), BF16))
        ah = jnp.where(mine, ag[e], jnp.zeros((), BF16))
        masked[step] = (qh, ah)
        s_ref[step % 2] = dot_nt(keys[e, 0], qh)
        dw_ref[step % 2] = dot_nt(keys[e, 1], ah)

    scores(0)
    for step, (e, h) in enumerate(steps):
        if step + 1 < len(steps):
            scores(step + 1)
        if h == 0:
            att_t, dq_t = [], []
            dk = dv = None
        s, dw, b = s_ref.at[step % 2], dw_ref.at[step % 2], step % 2
        qh, ah = masked[step]
        top = jnp.max(s[...], axis=0, keepdims=True)
        un = jnp.exp2((s[...] - top) * (LOG2E * DH ** -0.5))
        s[...] = un
        inverse = 1.0 / jnp.sum(un, axis=0, keepdims=True)
        delta = jnp.sum(un * dw[...], axis=0, keepdims=True) * inverse
        prob = s[...] * inverse
        w_ref[b] = prob.astype(BF16)
        ds_ref[b] = (prob * ((dw[...] - delta) * DH ** -0.5)).astype(BF16)
        att_t.append(dot(keys_t[e, 1, 64 * h : 64 * h + 64], w_ref[b]))
        dq_t.append(dot(keys_t[e, 0, 64 * h : 64 * h + 64], ds_ref[b]))
        dkh, dvh = dot(ds_ref[b], qh), dot(w_ref[b], ah)
        dk = dkh if dk is None else dk + dkh
        dv = dvh if dv is None else dv + dvh
        if h == 0:
            continue
        att_out[e] = jnp.concatenate(att_t, axis=0).T.astype(BF16)
        dq_out[e] = jnp.concatenate(dq_t, axis=0).T.astype(BF16)
        for p, grad in ((0, dk), (1, dv)):
            dkv_out[e, p] = grad[:256]
            dn1_out[1 - e, p] = grad[256:384]
            if e == 0:
                drem[p] = grad[384:]
            else:
                drem[p] = drem[p] + grad[384:]
    for p in range(2):
        rows = drem[p].astype(BF16)
        dy_out[p] = rows[:128]
        dwy_out[p] = rows[256:384]
        dw_out[p] = drem[p, 128:256]
        for slot in range(8):
            start = 384 + ZR * slot
            dx_out[slot, p] = rows[start : start + ZR]


def attention(pos, q, ag, kv, n1, yr, wr, wy, xr):
    def cut(*lead):
        return pl.BlockSpec(lead + (128,), lambda i, s: (0,) * len(lead) + (i,))

    outs = [
        ((2, TOK), BF16), ((2, TOK), BF16), ((2, 2, TOK), F32), ((2, 2, NR), F32), ((2, NR), BF16), ((2, NR), BF16),
        ((2, NR), F32), ((8, 2, ZR), BF16),
    ]
    n = 1152
    return call(
        attention_body,
        (H // 128,),
        [cut(2, TOK), cut(2, TOK), cut(2, 2, TOK), cut(2, 2, NR), cut(2, NR), cut(2, NR), cut(2, NR), cut(8, 2, ZR)],
        [(cut(*lead), (lead + (H,), kind)) for lead, kind in outs],
        [
            pltpu.VMEM((2, 2, n, 128), BF16), pltpu.VMEM((2, 2, 128, n), BF16), pltpu.VMEM((2, n, TOK), F32), pltpu.VMEM((2, n, TOK), F32),
            pltpu.VMEM((2, n, TOK), BF16), pltpu.VMEM((2, n, TOK), BF16), pltpu.VMEM((2, 768, 128), F32),
        ],
    )(pos, q, ag, kv, n1, yr, wr, wy, xr)


def output_body(pos, att_own, att_oth, w_own, w_oth, out):
    c = pos[0]
    out[...] = (dot(att_own[c], w_own[...]) + dot(att_oth[c], w_oth[...])).astype(BF16)


def output_side(pos, att_own, att_oth, w_out):
    row = lambda flip: pl.BlockSpec((H, D), lambda i, s: (s[0] ^ flip, 0))
    return call(
        output_body,
        (1,),
        [whole(2, TOK, H)] * 2 + [row(0), row(1)],
        [(whole(TOK, D), ((TOK, D), BF16))],
    )(pos, att_own, att_oth, w_out, w_out)[0]


def terms_body(pos, att_own, att_oth, ct_own, ct_oth, dq, xt, p_own, p_oth, *rest):
    c, x = pos[0], pos[2] >> 1
    slots = rest[-1]
    total = dot(xt[0], dq[0]) + dot(xt[1], dq[1])
    slots[:, :, 0] = total.astype(BF16).reshape(XN, YN, 96, H)
    total = None
    for e, ct in ((c, ct_own), (1 - c, ct_oth)):
        att_t = (dot_nt(p_own[...], att_own[e]) + dot_nt(p_oth[...], att_oth[e])).astype(BF16)
        term = dot(att_t, ct[...])
        total = term if total is None else total + term
    slots[:, :, 1] = total.astype(BF16).reshape(XN, YN, 96, H)
    for far in range(XN):
        rest[far][...] = slots[x ^ far]


def output_terms(pos, att_own, att_oth, ct_own, ct_oth, dq, xt, perm):
    col = lambda flip, rows: pl.BlockSpec((rows, H), lambda i, s: (0, s[0] ^ flip))
    slot = (YN, 2, 96, H)
    return call(
        terms_body,
        (1,),
        [whole(2, TOK, H)] * 2 + [col(0, TOK)] * 2 + [whole(2, TOK, H), whole(2, D, TOK), col(0, D), col(1, D)],
        [(whole(*slot), (slot, BF16))] * XN,
        [pltpu.VMEM((XN,) + slot, BF16)],
    )(pos, att_own, att_oth, ct_own, ct_oth, dq, xt, perm, perm)


def x_sum_body(pos, t0, t1, t2, t3, *rest):
    y, dp = pos[2] & 1, pos[3]
    slots = rest[-1]
    total = (t0[...].astype(F32) + t1[...].astype(F32)) + (t2[...].astype(F32) + t3[...].astype(F32))
    slots[...] = total.astype(BF16)
    for far in range(4):
        rest[far][...] = slots[y ^ (far >> 1), dp ^ (far & 1)]


def x_sum(pos, *terms):
    shape = (YN, 2, 96, H)
    return call(
        x_sum_body,
        (1,),
        [whole(*shape)] * 4,
        [(whole(96, H), ((96, H), BF16))] * 4,
        [pltpu.VMEM(shape, BF16)],
    )(pos, *terms)


def back_body(pos, xr, out):
    hot = (iota((128, ZR), 0) == z_source(pos[1], 1, (128, ZR))).astype(BF16)
    for p in range(2):
        total = xr[0, p].astype(F32)
        for slot in range(1, 8):
            total = total + xr[slot, p].astype(F32)
        out[:, p] = dot(hot, total.astype(BF16)).astype(BF16).reshape(8, 16, H)


def back_slots(pos, xr):
    return call(
        back_body,
        (1,),
        [whole(8, 2, ZR, H)],
        [(whole(ZN, 2, 16, H), ((ZN, 2, 16, H), BF16))],
    )(pos, xr)[0]


def hand_back_body(pos, dw, dwy, *outs):
    start = 0
    for out in outs:
        rows = out.shape[1]
        for p in range(2):
            total = dw[p, start : start + rows] + dwy[p, start : start + rows].astype(F32)
            out[p] = total.astype(BF16)
        start += rows


def hand_back(pos, dw, dwy):
    return call(
        hand_back_body,
        (1,),
        [whole(2, NR, H)] * 2,
        [(whole(2, rows, H), ((2, rows, H), BF16)) for rows in (64, 32, 32)],
    )(pos, dw, dwy)


def leaf_body(pos, zr, dkv, dn1, dy, g3, g4_a, g4_b, dq, xt, pg_out, grad_out):
    def split(grad):
        high = grad.astype(BF16)
        return [high, (grad - high.astype(F32)).astype(BF16)]

    def hot(hit, scale):
        return jnp.where(hit, scale, 0.0).astype(BF16)

    def wide(ref):
        return jnp.concatenate([ref[0], ref[1]], axis=1)

    zs = jnp.concatenate([zr[:, p].reshape(128, H) for p in range(2)], axis=1)
    ws = jnp.concatenate([wide(g3), wide(g4_a), wide(g4_b)], axis=0)
    ys = wide(dy)
    for e in range(2):
        t, k = iota((TOK, 128), 0), iota((TOK, 128), 1)
        far, row, chip = (k >> 4) ^ pos[1], k & 15, t + TOK * e
        first = hot(t >> 1 == k, 1.0)
        third = hot(chip >> 3 == k, 0.5)
        odd = hot((far == 1) & (row == chip >> 5), 0.25) + hot((far >= 4) & (row == chip >> 7), 0.125)
        second = hot(chip >> 2 == k, 0.5)
        fourth = hot((k >= 64) & (chip >> 4 == k & 31), 0.25)
        even = hot((far >> 1 == 1) & (row == chip >> 6), 0.125)
        up = dot(jnp.concatenate([first, first, third, odd], axis=1), jnp.concatenate(split(wide(dn1.at[e])) + [ws, zs], axis=0))
        up = up * HALF_ROOT + dot(jnp.concatenate([second, fourth, even], axis=1), jnp.concatenate([ys, ws, zs], axis=0))
        for p in range(2):
            pg_out[e, :, H * (1 + p) : H * (2 + p)] = (dkv[e, p] + up[:, H * p : H * p + H]).astype(BF16)
        pg_out[e, :, :H] = dq[e]
    for p in range(2):
        cols = slice(H * (1 + p), H * (2 + p))
        total = dot(xt[0], pg_out[0, :, cols]) + dot(xt[1], pg_out[1, :, cols])
        grad_out[:, p] = total.astype(BF16).reshape(8, 96, H)


def leaf_grads(pos, zr, dkv, dn1, dy, g3, g4_a, g4_b, dq, xt):
    return call(
        leaf_body,
        (1,),
        [
            whole(ZN, 2, 16, H), whole(2, 2, TOK, H), whole(2, 2, NR, H), whole(2, NR, H), whole(2, 64, H), whole(2, 32, H),
            whole(2, 32, H), whole(2, TOK, H), whole(2, D, TOK),
        ],
        [(whole(2, TOK, 3 * H), ((2, TOK, 3 * H), BF16)), (whole(8, 2, 96, H), ((8, 2, 96, H), BF16))],
    )(pos, zr, dkv, dn1, dy, g3, g4_a, g4_b, dq, xt)


def input_body(pos, pg_own, pg_oth, *rest):
    out = rest[-1]
    total = None
    for part in range(3):
        for pg, w in ((pg_own, rest[part]), (pg_oth, rest[3 + part])):
            term = dot_nt(pg[:, H * part : H * part + H], w[...])
            total = term if total is None else total + term
    out[...] = total.astype(BF16)


def input_side(pos, pg_own, pg_oth, w_qkv):
    col = lambda part, flip: pl.BlockSpec((D, H), lambda i, s: (0, 2 * part + (s[0] ^ flip)))
    return call(
        input_body,
        (1,),
        [whole(TOK, 3 * H)] * 2 + [col(part, flip) for flip in (0, 1) for part in range(3)],
        [(whole(TOK, D), ((TOK, D), BF16))],
    )(pos, pg_own, pg_oth, *[w_qkv] * 6)[0]


def total_of(refs):
    total = refs[0].astype(F32)
    for ref in refs[1:]:
        total = total + ref.astype(F32)
    return total


def middle_body(pos, f0, f1, f2, f3, second, out):
    first = total_of([f0[...], f1[...], f2[...], f3[...]]).astype(BF16)
    i, k = iota((256, 96), 0), iota((256, 96), 1)
    row, half = i & 7, (i >> 3) & 1
    hit = (k == 6 * (i >> 4) + row) & (row < 6)
    rows = dot((hit & (half == 0)).astype(BF16), first)
    rows = rows + dot((hit & (half == 1)).astype(BF16), total_of([second[slot] for slot in range(16)]).astype(BF16))
    out[...] = rows.astype(BF16).reshape(ZN, 2, 16, H)


def middle_sum(pos, firsts, second):
    shape = (ZN, 2, 16, H)
    return call(
        middle_body, (1,), [whole(96, H)] * 4 + [whole(16, 96, H)], [(whole(*shape), (shape, BF16))]
    )(pos, *firsts, second)[0]


def z_sum_body(pos, terms, own_out, oth_out):
    for core, out in ((pos[0], own_out), (1 - pos[0], oth_out)):
        out[...] = total_of([terms[z, core] for z in range(ZN)]).astype(BF16)


def z_sum(pos, terms):
    return call(
        z_sum_body,
        (1,),
        [whole(ZN, 2, 16, H)],
        [(whole(16, H), ((16, H), BF16))] * 2,
    )(pos, terms)


def last_body(pos, own, from_dp, from_core, from_both, qkv_out, out_out, parts):
    core, dp = pos[0], pos[3]
    parts[core, dp] = own[...]
    parts[core, 1 - dp] = from_dp[...]
    parts[1 - core, dp] = from_core[...]
    parts[1 - core, 1 - dp] = from_both[...]
    for core in range(2):
        low, high = parts[core, 0].astype(F32), parts[core, 1].astype(F32)
        cols = lambda part: slice(D * part + H * core, D * part + H * core + H)
        qkv_out[:, cols(0)] = low[:6]
        qkv_out[:, cols(1)] = low[8:14]
        qkv_out[:, cols(2)] = high[8:14]
        out_out[:, cols(0)] = high[:6]


def last_rows(pos, *parts):
    return call(
        last_body,
        (1,),
        [whole(16, H)] * 4,
        [(whole(6, 3 * D), ((6, 3 * D), F32)), (whole(6, D), ((6, D), F32))],
        [pltpu.VMEM((2, 2, 16, H), BF16)],
    )(pos, *parts)


def swap(value, axis):
    return lax.ppermute(value, axis, [(0, 1), (1, 0)])


def along(value, axes, far, count=4):
    return lax.ppermute(value, axes, [(i, i ^ far) for i in range(count)])


def row_order():
    f = np.arange(D)
    source = 96 * (f // 12 % 8) + 12 * (f // 96) + f % 12
    return jnp.asarray(source[:, None] == f[None, :], BF16)


def shards(x_tokens, cotangent, w_qkv, w_out):
    x_own, ct_own = x_tokens[0], cotangent[0]
    c, z, dp = lax.axis_index("c"), lax.axis_index("z"), lax.axis_index("dp")
    j = 2 * lax.axis_index("x") + lax.axis_index("y")
    pos = jnp.stack([c, z, j, dp]).astype(jnp.int32)
    x_oth, ct_oth = swap(x_own, "c"), swap(ct_own, "c")
    perm = row_order()

    kv, n1, n2, n3, n4, zs = tree(pos, x_own, x_oth, w_qkv)
    yr = swap(n2, "y")
    wr = jnp.concatenate([along(n3, "x", 1), along(n4, "x", 2), along(n4, "x", 3)], axis=1)
    wy = swap(wr, "y")
    zr = lax.all_to_all(zs, "z", 0, 0)
    zr, yr, wy, ct_oth = lax.optimization_barrier((zr, yr, wy, ct_oth))
    xr = lax.all_to_all(plane_slots(pos, zr), ("x", "y"), 0, 0)
    q, ag, xt = project(pos, x_own, x_oth, ct_own, ct_oth, w_qkv, w_out, perm)
    att, dq, dkv, dn1, dy, dwy, dw, dx = attention(pos, q, ag, kv, n1, yr, wr, wy, xr)

    dx_r = lax.all_to_all(dx, ("x", "y"), 0, 0)
    att_oth = swap(att, "c")
    dwy = swap(dwy, "y")
    first, *firsts = output_terms(pos, att, att_oth, ct_own, ct_oth, dq, xt, perm)
    firsts = [along(firsts[far - 1], "x", far) for far in (1, 2, 3)]
    g3, g4_a, g4_b = hand_back(pos, dw, dwy)
    dx_r, first, firsts[0], g3, g4_a, g4_b = lax.optimization_barrier((dx_r, first, firsts[0], g3, g4_a, g4_b))
    dz_r = lax.all_to_all(back_slots(pos, dx_r), "z", 0, 0)
    g3, g4_a, g4_b = along(g3, "x", 1), along(g4_a, "x", 2), along(g4_b, "x", 3)
    firsts = x_sum(pos, first, *firsts)
    dz_r, g3, g4_a, g4_b, firsts = lax.optimization_barrier((dz_r, g3, g4_a, g4_b, firsts))
    firsts = list(firsts[:1]) + [along(firsts[far], ("y", "dp"), far) for far in (1, 2, 3)]
    pg, terms = leaf_grads(pos, dz_r, dkv, dn1, swap(dy, "y"), g3, g4_a, g4_b, dq, xt)
    terms, firsts = lax.optimization_barrier((terms, firsts))
    terms = lax.all_to_all(terms.reshape(16, 96, H), ("x", "y", "dp"), 0, 0)
    pg_own = lax.dynamic_index_in_dim(pg, c, 0, keepdims=False)
    pg_oth = swap(lax.dynamic_index_in_dim(pg, 1 - c, 0, keepdims=False), "c")
    input_grad = input_side(pos, pg_own, pg_oth, w_qkv)
    layer_out = output_side(pos, att, att_oth, w_out)
    terms, input_grad, layer_out = lax.optimization_barrier((terms, input_grad, layer_out))
    terms = lax.all_to_all(middle_sum(pos, firsts, terms), "z", 0, 0)
    own, oth = z_sum(pos, terms)
    pair = ("c", "dp")
    qkv_grad, out_grad = last_rows(pos, own, along(own, pair, 1), along(oth, pair, 2), along(oth, pair, 3))
    return (layer_out[None], input_grad[None], qkv_grad, out_grad)


def solution(mesh):
    split = Mesh(mesh.devices.reshape(ZN, XN, YN, 2, 2), ("z", "x", "y", "c", "dp"))
    seq = ("z", "x", "y", "c")
    return jax.shard_map(
        shards,
        mesh=split,
        in_specs=(P("dp", seq, None), P("dp", seq, None), P(), P()),
        out_specs=(P("dp", seq, None), P("dp", seq, None), P(seq, None), P(seq, None)),
        check_vma=False,
    )
```

```python
import jax
import jax.numpy as jnp
import numpy as np
from jax import lax
from jax.experimental import pallas as pl
from jax.experimental.pallas import tpu as pltpu
from jax.sharding import Mesh, PartitionSpec as P

D = 768
H = 384
TOK = 256
NR = 128
DH = 64
ZN, XN, YN = 8, 4, 2
ZR = 48
HALF_ROOT = 0.7071067811865476
LOG2E = 1.4426950408889634
VMEM = 56 * 1024 * 1024
F32 = jnp.float32
BF16 = jnp.bfloat16


def dot(a, b):
    return lax.dot_general(a, b, (((1,), (0,)), ((), ())), preferred_element_type=F32)


def dot_nt(a, b):
    return lax.dot_general(a, b, (((1,), (1,)), ((), ())), preferred_element_type=F32)


def dot_tn(a, b):
    return lax.dot_general(a, b, (((0,), (0,)), ((), ())), preferred_element_type=F32)


def iota(shape, axis):
    return lax.broadcasted_iota(jnp.int32, shape, axis)


def pair_matrix(rows, cols, valid):
    r, k = iota((rows, cols), 0), iota((rows, cols), 1)
    return (((k >> 1) == r) & (r < valid)).astype(BF16)


def coarsen(node, rows=None, valid=None):
    rows = node.shape[0] // 2 if rows is None else rows
    valid = rows if valid is None else valid
    return (dot(pair_matrix(rows, node.shape[0], valid), node) * HALF_ROOT).astype(BF16)


def whole(*shape):
    return pl.BlockSpec(shape, lambda *_: (0,) * len(shape))


def call(body, grid, ins, outs, scratch=()):
    return pl.pallas_call(
        body,
        grid_spec=pltpu.PrefetchScalarGridSpec(
            num_scalar_prefetch=1,
            grid=grid,
            in_specs=ins,
            out_specs=[s for s, _ in outs],
            scratch_shapes=list(scratch),
        ),
        out_shape=[jax.ShapeDtypeStruct(shape, kind) for _, (shape, kind) in outs],
        compiler_params=pltpu.CompilerParams(vmem_limit_bytes=VMEM),
    )


def tree_body(pos, x_own, x_oth, wk, wv, kv_out, n1_out, n2_out, n3_out, n4_out, zs_out):
    c, z = pos[0], pos[1]
    for e, x in ((c, x_own), (1 - c, x_oth)):
        kv_out[e, 0] = dot(x[...], wk[...]).astype(BF16)
        kv_out[e, 1] = dot(x[...], wv[...]).astype(BF16)

    def store(ref, *index):
        def put(node):
            for p in range(2):
                ref[index + (p,)] = node[:, H * p : H * p + H]

        return put

    halves = []
    for e in range(2):
        n1 = coarsen(jnp.concatenate([kv_out[e, 0], kv_out[e, 1]], axis=1))
        store(n1_out, e)(n1)
        halves.append(coarsen(n1))
    n2 = jnp.concatenate(halves, axis=0)
    store(n2_out)(n2)
    n3 = coarsen(n2)
    store(n3_out)(n3)
    n4 = coarsen(n3)
    store(n4_out)(n4)
    n5 = coarsen(n4)
    n6 = coarsen(n5, 16, 8)
    n7 = coarsen(n6, 16, 4)
    store(zs_out, z)(jnp.zeros_like(n5))
    store(zs_out, z ^ 1)(n5)
    for far in (2, 3):
        store(zs_out, z ^ far)(n6)
    for far in (4, 5, 6, 7):
        store(zs_out, z ^ far)(n7)


def tree(pos, x_own, x_oth, w_qkv):
    col = lambda part: pl.BlockSpec((D, H), lambda i, s: (0, 2 * part + s[0]))
    outs = [(2, 2, TOK, H), (2, 2, NR, H), (2, NR, H), (2, 64, H), (2, 32, H), (ZN, 2, 16, H)]
    return call(
        tree_body,
        (1,),
        [whole(TOK, D)] * 2 + [col(1), col(2)],
        [(whole(*shape), (shape, BF16)) for shape in outs],
    )(pos, x_own, x_oth, w_qkv, w_qkv)


def project_body(pos, x_own, x_oth, ct_own, ct_oth, wq, wo, perm, q_out, ag_out, xt_out):
    c = pos[0]
    for e, x, ct in ((c, x_own, ct_own), (1 - c, x_oth, ct_oth)):
        q_out[e] = dot(x[...], wq[...]).astype(BF16)
        ag_out[e] = dot_nt(ct[...], wo[...]).astype(BF16)
        xt_out[e] = dot_nt(perm[...], x[...]).astype(BF16)


def project(pos, x_own, x_oth, ct_own, ct_oth, w_qkv, w_out, perm):
    outs = [(2, TOK, H), (2, TOK, H), (2, D, TOK)]
    return call(
        project_body,
        (1,),
        [whole(TOK, D)] * 4
        + [pl.BlockSpec((D, H), lambda i, s: (0, s[0])), pl.BlockSpec((H, D), lambda i, s: (s[0], 0)), whole(D, D)],
        [(whole(*shape), (shape, BF16)) for shape in outs],
    )(pos, x_own, x_oth, ct_own, ct_oth, w_qkv, w_out, perm)


def z_source(z, rows_axis, shape):
    i = iota(shape, rows_axis)
    near = 16 * (z ^ 1) + i
    mid = 16 * (z ^ (2 + ((i - 16) >> 3))) + ((i - 16) & 7)
    far = 16 * (z ^ (4 + ((i - 32) >> 2))) + ((i - 32) & 3)
    return jnp.where(i < 16, near, jnp.where(i < 32, mid, far))


def plane_body(pos, zr, out):
    hot = (iota((ZR, 128), 1) == z_source(pos[1], 0, (ZR, 128))).astype(BF16)
    both = jnp.concatenate([zr[:, p].reshape(128, H) for p in range(2)], axis=1)
    rows = dot(hot, both).astype(BF16)
    for slot in range(8):
        for p in range(2):
            out[slot, p] = rows[:, H * p : H * p + H]


def plane_slots(pos, zr):
    return call(
        plane_body,
        (1,),
        [whole(ZN, 2, 16, H)],
        [(whole(8, 2, ZR, H), ((8, 2, ZR, H), BF16))],
    )(pos, zr)[0]


def attention_body(pos, q, ag, kv, n1, yr, wr, wy, xr, att_out, dq_out, dkv_out, dn1_out, dy_out, dwy_out, dw_out, dx_out, keys, keys_t, s_ref, dw_ref, w_ref, ds_ref, drem):
    for p in range(2):
        for e in range(2):
            keys[e, p, :256] = kv[e, p]
            keys[e, p, 256:384] = n1[1 - e, p]
            keys[e, p, 384:512] = yr[p]
            keys[e, p, 512:640] = wr[p]
            keys[e, p, 640:768] = wy[p]
            for slot in range(8):
                start = 768 + ZR * slot
                keys[e, p, start : start + ZR] = xr[slot, p]
    for p in range(2):
        for e in range(2):
            keys_t[e, p] = keys[e, p].T
    lane = iota((TOK, 128), 1)
    steps = [(e, h) for e in range(2) for h in range(2)]
    masked = {}

    def scores(step):
        e, h = steps[step]
        mine = (lane >> 6) == h
        qh = jnp.where(mine, q[e], jnp.zeros((), BF16))
        ah = jnp.where(mine, ag[e], jnp.zeros((), BF16))
        masked[step] = (qh, ah)
        s_ref[step % 2] = dot_nt(keys[e, 0], qh)
        dw_ref[step % 2] = dot_nt(keys[e, 1], ah * jnp.asarray(DH ** -0.5, BF16))

    scores(0)
    for step, (e, h) in enumerate(steps):
        if step + 1 < len(steps):
            scores(step + 1)
        if h == 0:
            att_t, dq_t = [], []
        s, dw, b = s_ref.at[step % 2], dw_ref.at[step % 2], step % 2
        qh, ah = masked[step]
        top = jnp.max(s[...], axis=0, keepdims=True)
        un = jnp.exp2((s[...] - top) * (LOG2E * DH ** -0.5))
        s[...] = un
        inverse = 1.0 / jnp.sum(un, axis=0, keepdims=True)
        delta = jnp.sum(un * dw[...], axis=0, keepdims=True) * inverse
        prob = s[...] * inverse
        cols = slice(TOK * h, TOK * h + TOK)
        w_ref[e, :, cols] = prob.astype(BF16)
        ds_ref[e, :, cols] = (prob * (dw[...] - delta)).astype(BF16)
        att_t.append(dot(keys_t[e, 1, 64 * h : 64 * h + 64], w_ref[e, :, cols]))
        dq_t.append(dot(keys_t[e, 0, 64 * h : 64 * h + 64], ds_ref[e, :, cols]))
        if h == 0:
            continue
        dk = dot(ds_ref[e], jnp.concatenate([masked[step - 1][0], qh], axis=0))
        dv = dot(w_ref[e], jnp.concatenate([masked[step - 1][1], ah], axis=0))
        att_out[e] = jnp.concatenate(att_t, axis=0).T.astype(BF16)
        dq_out[e] = jnp.concatenate(dq_t, axis=0).T.astype(BF16)
        for p, grad in ((0, dk), (1, dv)):
            dkv_out[e, p] = grad[:256]
            dn1_out[1 - e, p] = grad[256:384]
            if e == 0:
                drem[p] = grad[384:]
            else:
                drem[p] = drem[p] + grad[384:]
    for p in range(2):
        rows = drem[p].astype(BF16)
        dy_out[p] = rows[:128]
        dwy_out[p] = rows[256:384]
        dw_out[p] = drem[p, 128:256]
        for slot in range(8):
            start = 384 + ZR * slot
            dx_out[slot, p] = rows[start : start + ZR]


def attention(pos, q, ag, kv, n1, yr, wr, wy, xr):
    def cut(*lead):
        return pl.BlockSpec(lead + (128,), lambda i, s: (0,) * len(lead) + (i,))

    outs = [
        ((2, TOK), BF16), ((2, TOK), BF16), ((2, 2, TOK), F32), ((2, 2, NR), F32), ((2, NR), BF16), ((2, NR), BF16),
        ((2, NR), F32), ((8, 2, ZR), BF16),
    ]
    n = 1152
    return call(
        attention_body,
        (H // 128,),
        [cut(2, TOK), cut(2, TOK), cut(2, 2, TOK), cut(2, 2, NR), cut(2, NR), cut(2, NR), cut(2, NR), cut(8, 2, ZR)],
        [(cut(*lead), (lead + (H,), kind)) for lead, kind in outs],
        [
            pltpu.VMEM((2, 2, n, 128), BF16), pltpu.VMEM((2, 2, 128, n), BF16), pltpu.VMEM((2, n, TOK), F32), pltpu.VMEM((2, n, TOK), F32),
            pltpu.VMEM((2, n, 2 * TOK), BF16), pltpu.VMEM((2, n, 2 * TOK), BF16), pltpu.VMEM((2, 768, 128), F32),
        ],
    )(pos, q, ag, kv, n1, yr, wr, wy, xr)


def output_body(pos, att_own, att_oth, w_own, w_oth, out):
    c = pos[0]
    out[...] = (dot(att_own[c], w_own[...]) + dot(att_oth[c], w_oth[...])).astype(BF16)


def output_side(pos, att_own, att_oth, w_out):
    row = lambda flip: pl.BlockSpec((H, D), lambda i, s: (s[0] ^ flip, 0))
    return call(
        output_body,
        (1,),
        [whole(2, TOK, H)] * 2 + [row(0), row(1)],
        [(whole(TOK, D), ((TOK, D), BF16))],
    )(pos, att_own, att_oth, w_out, w_out)[0]


def terms_body(pos, att_own, att_oth, ct_own, ct_oth, dq, xt, p_own, p_oth, *rest):
    c, x = pos[0], pos[2] >> 1
    slots = rest[-1]
    total = dot(xt[0], dq[0]) + dot(xt[1], dq[1])
    slots[:, :, 0] = total.astype(BF16).reshape(XN, YN, 96, H)
    total = None
    for e, ct in ((c, ct_own), (1 - c, ct_oth)):
        att_t = (dot_nt(p_own[...], att_own[e]) + dot_nt(p_oth[...], att_oth[e])).astype(BF16)
        term = dot(att_t, ct[...])
        total = term if total is None else total + term
    slots[:, :, 1] = total.astype(BF16).reshape(XN, YN, 96, H)
    for far in range(XN):
        rest[far][...] = slots[x ^ far]


def output_terms(pos, att_own, att_oth, ct_own, ct_oth, dq, xt, perm):
    col = lambda flip, rows: pl.BlockSpec((rows, H), lambda i, s: (0, s[0] ^ flip))
    slot = (YN, 2, 96, H)
    return call(
        terms_body,
        (1,),
        [whole(2, TOK, H)] * 2 + [col(0, TOK)] * 2 + [whole(2, TOK, H), whole(2, D, TOK), col(0, D), col(1, D)],
        [(whole(*slot), (slot, BF16))] * XN,
        [pltpu.VMEM((XN,) + slot, BF16)],
    )(pos, att_own, att_oth, ct_own, ct_oth, dq, xt, perm, perm)


def x_sum_body(pos, t0, t1, t2, t3, *rest):
    y, dp = pos[2] & 1, pos[3]
    slots = rest[-1]
    total = (t0[...].astype(F32) + t1[...].astype(F32)) + (t2[...].astype(F32) + t3[...].astype(F32))
    slots[...] = total.astype(BF16)
    for far in range(4):
        rest[far][...] = slots[y ^ (far >> 1), dp ^ (far & 1)]


def x_sum(pos, *terms):
    shape = (YN, 2, 96, H)
    return call(
        x_sum_body,
        (1,),
        [whole(*shape)] * 4,
        [(whole(96, H), ((96, H), BF16))] * 4,
        [pltpu.VMEM(shape, BF16)],
    )(pos, *terms)


def back_body(pos, xr, out):
    hot = (iota((128, ZR), 0) == z_source(pos[1], 1, (128, ZR))).astype(BF16)
    for p in range(2):
        total = xr[0, p].astype(F32)
        for slot in range(1, 8):
            total = total + xr[slot, p].astype(F32)
        out[:, p] = dot(hot, total.astype(BF16)).astype(BF16).reshape(8, 16, H)


def back_slots(pos, xr):
    return call(
        back_body,
        (1,),
        [whole(8, 2, ZR, H)],
        [(whole(ZN, 2, 16, H), ((ZN, 2, 16, H), BF16))],
    )(pos, xr)[0]


def hand_back_body(pos, dw, dwy, *outs):
    start = 0
    for out in outs:
        rows = out.shape[1]
        for p in range(2):
            total = dw[p, start : start + rows] + dwy[p, start : start + rows].astype(F32)
            out[p] = total.astype(BF16)
        start += rows


def hand_back(pos, dw, dwy):
    return call(
        hand_back_body,
        (1,),
        [whole(2, NR, H)] * 2,
        [(whole(2, rows, H), ((2, rows, H), BF16)) for rows in (64, 32, 32)],
    )(pos, dw, dwy)


def leaf_body(pos, zr, dkv, dn1, dy, g3, g4_a, g4_b, dq, xt, pg_out, grad_out):
    def split(grad):
        high = grad.astype(BF16)
        return [high, (grad - high.astype(F32)).astype(BF16)]

    def hot(hit, scale):
        return jnp.where(hit, scale, 0.0).astype(BF16)

    def wide(ref):
        return jnp.concatenate([ref[0], ref[1]], axis=1)

    zs = jnp.concatenate([zr[:, p].reshape(128, H) for p in range(2)], axis=1)
    ws = jnp.concatenate([wide(g3), wide(g4_a), wide(g4_b)], axis=0)
    ys = wide(dy)
    for e in range(2):
        t, k = iota((TOK, 128), 0), iota((TOK, 128), 1)
        far, row, chip = (k >> 4) ^ pos[1], k & 15, t + TOK * e
        first = hot(t >> 1 == k, 1.0)
        third = hot(chip >> 3 == k, 0.5)
        odd = hot((far == 1) & (row == chip >> 5), 0.25) + hot((far >= 4) & (row == chip >> 7), 0.125)
        second = hot(chip >> 2 == k, 0.5)
        fourth = hot((k >= 64) & (chip >> 4 == k & 31), 0.25)
        even = hot((far >> 1 == 1) & (row == chip >> 6), 0.125)
        up = dot(jnp.concatenate([first, first, third, odd], axis=1), jnp.concatenate(split(wide(dn1.at[e])) + [ws, zs], axis=0))
        up = up * HALF_ROOT + dot(jnp.concatenate([second, fourth, even], axis=1), jnp.concatenate([ys, ws, zs], axis=0))
        for p in range(2):
            pg_out[e, :, H * (1 + p) : H * (2 + p)] = (dkv[e, p] + up[:, H * p : H * p + H]).astype(BF16)
        pg_out[e, :, :H] = dq[e]
    for p in range(2):
        cols = slice(H * (1 + p), H * (2 + p))
        total = dot(xt[0], pg_out[0, :, cols]) + dot(xt[1], pg_out[1, :, cols])
        grad_out[:, p] = total.astype(BF16).reshape(8, 96, H)


def leaf_grads(pos, zr, dkv, dn1, dy, g3, g4_a, g4_b, dq, xt):
    return call(
        leaf_body,
        (1,),
        [
            whole(ZN, 2, 16, H), whole(2, 2, TOK, H), whole(2, 2, NR, H), whole(2, NR, H), whole(2, 64, H), whole(2, 32, H),
            whole(2, 32, H), whole(2, TOK, H), whole(2, D, TOK),
        ],
        [(whole(2, TOK, 3 * H), ((2, TOK, 3 * H), BF16)), (whole(8, 2, 96, H), ((8, 2, 96, H), BF16))],
    )(pos, zr, dkv, dn1, dy, g3, g4_a, g4_b, dq, xt)


def input_body(pos, pg_own, pg_oth, *rest):
    out = rest[-1]
    total = None
    for part in range(3):
        for pg, w in ((pg_own, rest[part]), (pg_oth, rest[3 + part])):
            term = dot_nt(pg[:, H * part : H * part + H], w[...])
            total = term if total is None else total + term
    out[...] = total.astype(BF16)


def input_side(pos, pg_own, pg_oth, w_qkv):
    col = lambda part, flip: pl.BlockSpec((D, H), lambda i, s: (0, 2 * part + (s[0] ^ flip)))
    return call(
        input_body,
        (1,),
        [whole(TOK, 3 * H)] * 2 + [col(part, flip) for flip in (0, 1) for part in range(3)],
        [(whole(TOK, D), ((TOK, D), BF16))],
    )(pos, pg_own, pg_oth, *[w_qkv] * 6)[0]


def total_of(refs):
    total = refs[0].astype(F32)
    for ref in refs[1:]:
        total = total + ref.astype(F32)
    return total


def middle_body(pos, f0, f1, f2, f3, second, out):
    first = total_of([f0[...], f1[...], f2[...], f3[...]]).astype(BF16)
    i, k = iota((256, 96), 0), iota((256, 96), 1)
    row, half = i & 7, (i >> 3) & 1
    hit = (k == 6 * (i >> 4) + row) & (row < 6)
    rows = dot((hit & (half == 0)).astype(BF16), first)
    rows = rows + dot((hit & (half == 1)).astype(BF16), total_of([second[slot] for slot in range(16)]).astype(BF16))
    rows = rows.astype(BF16).reshape(ZN, 2, 16, H)
    for core in range(2):
        out[:, core ^ pos[0]] = rows[:, core]


def middle_sum(pos, firsts, second):
    shape = (ZN, 2, 16, H)
    return call(
        middle_body, (1,), [whole(96, H)] * 4 + [whole(16, 96, H)], [(whole(*shape), (shape, BF16))]
    )(pos, *firsts, second)[0]


def last_body(pos, own, from_dp, from_core, from_both, qkv_out, out_out, parts):
    core, dp = pos[0], pos[3]
    parts[core, dp] = own[...]
    parts[core, 1 - dp] = from_dp[...]
    parts[1 - core, dp] = from_core[...]
    parts[1 - core, 1 - dp] = from_both[...]
    for core in range(2):
        low, high = parts[core, 0].astype(F32), parts[core, 1].astype(F32)
        cols = lambda part: slice(D * part + H * core, D * part + H * core + H)
        qkv_out[:, cols(0)] = low[:6]
        qkv_out[:, cols(1)] = low[8:14]
        qkv_out[:, cols(2)] = high[8:14]
        out_out[:, cols(0)] = high[:6]


def last_rows(pos, *parts):
    return call(
        last_body,
        (1,),
        [whole(16, H)] * 4,
        [(whole(6, 3 * D), ((6, 3 * D), F32)), (whole(6, D), ((6, D), F32))],
        [pltpu.VMEM((2, 2, 16, H), BF16)],
    )(pos, *parts)


def swap(value, axis):
    return lax.ppermute(value, axis, [(0, 1), (1, 0)])


def along(value, axes, far, count=4):
    return lax.ppermute(value, axes, [(i, i ^ far) for i in range(count)])


def row_order():
    f = np.arange(D)
    source = 96 * (f // 12 % 8) + 12 * (f // 96) + f % 12
    return jnp.asarray(source[:, None] == f[None, :], BF16)


def shards(x_tokens, cotangent, w_qkv, w_out):
    x_own, ct_own = x_tokens[0], cotangent[0]
    c, z, dp = lax.axis_index("c"), lax.axis_index("z"), lax.axis_index("dp")
    j = 2 * lax.axis_index("x") + lax.axis_index("y")
    pos = jnp.stack([c, z, j, dp]).astype(jnp.int32)
    x_oth, ct_oth = swap(x_own, "c"), swap(ct_own, "c")
    perm = row_order()

    kv, n1, n2, n3, n4, zs = tree(pos, x_own, x_oth, w_qkv)
    yr = swap(n2, "y")
    wr = jnp.concatenate([along(n3, "x", 1), along(n4, "x", 2), along(n4, "x", 3)], axis=1)
    wy = swap(wr, "y")
    zr = lax.all_to_all(zs, "z", 0, 0)
    zr, yr, wy, ct_oth = lax.optimization_barrier((zr, yr, wy, ct_oth))
    xr = lax.all_to_all(plane_slots(pos, zr), ("x", "y"), 0, 0)
    q, ag, xt = project(pos, x_own, x_oth, ct_own, ct_oth, w_qkv, w_out, perm)
    att, dq, dkv, dn1, dy, dwy, dw, dx = attention(pos, q, ag, kv, n1, yr, wr, wy, xr)

    dx_r = lax.all_to_all(dx, ("x", "y"), 0, 0)
    att_oth = swap(att, "c")
    dwy = swap(dwy, "y")
    first, *firsts = output_terms(pos, att, att_oth, ct_own, ct_oth, dq, xt, perm)
    firsts = [along(firsts[far - 1], "x", far) for far in (1, 2, 3)]
    dx_r, first, firsts[0], dwy = lax.optimization_barrier((dx_r, first, firsts[0], dwy))
    dz_r = lax.all_to_all(back_slots(pos, dx_r), "z", 0, 0)
    g3, g4_a, g4_b = hand_back(pos, dw, dwy)
    g3, g4_a, g4_b, firsts = lax.optimization_barrier((g3, g4_a, g4_b, firsts))
    g3, g4_a, g4_b = along(g3, "x", 1), along(g4_a, "x", 2), along(g4_b, "x", 3)
    firsts = x_sum(pos, first, *firsts)
    dz_r, g3, g4_a, g4_b, first = lax.optimization_barrier((dz_r, g3, g4_a, g4_b, firsts[0]))
    firsts = [first] + [along(firsts[far], ("y", "dp"), far) for far in (1, 2, 3)]
    pg, terms = leaf_grads(pos, dz_r, dkv, dn1, swap(dy, "y"), g3, g4_a, g4_b, dq, xt)
    terms, firsts = lax.optimization_barrier((terms, firsts))
    terms = lax.all_to_all(terms.reshape(16, 96, H), ("x", "y", "dp"), 0, 0)
    pg_own = lax.dynamic_index_in_dim(pg, c, 0, keepdims=False)
    pg_oth = swap(lax.dynamic_index_in_dim(pg, 1 - c, 0, keepdims=False), "c")
    input_grad = input_side(pos, pg_own, pg_oth, w_qkv)
    layer_out = output_side(pos, att, att_oth, w_out)
    terms, input_grad, layer_out = lax.optimization_barrier((terms, input_grad, layer_out))
    terms = lax.all_to_all(middle_sum(pos, firsts, terms), "z", 0, 0)
    own, oth = (jnp.sum(terms[:, core].astype(F32), axis=0).astype(BF16) for core in range(2))
    pair = ("c", "dp")
    qkv_grad, out_grad = last_rows(pos, own, along(own, pair, 1), along(oth, pair, 2), along(oth, pair, 3))
    return (layer_out[None], input_grad[None], qkv_grad, out_grad)


def solution(mesh):
    split = Mesh(mesh.devices.reshape(ZN, XN, YN, 2, 2), ("z", "x", "y", "c", "dp"))
    seq = ("z", "x", "y", "c")
    return jax.shard_map(
        shards,
        mesh=split,
        in_specs=(P("dp", seq, None), P("dp", seq, None), P(), P()),
        out_specs=(P("dp", seq, None), P("dp", seq, None), P(seq, None), P(seq, None)),
        check_vma=False,
    )
```

```python
import jax
import jax.numpy as jnp
import numpy as np
from jax import lax
from jax.experimental import pallas as pl
from jax.experimental.pallas import tpu as pltpu
from jax.sharding import Mesh, PartitionSpec as P

D = 768
H = 384
TOK = 256
NR = 128
DH = 64
ZN, XN, YN = 8, 4, 2
ZR = 48
HALF_ROOT = 0.7071067811865476
LOG2E = 1.4426950408889634
VMEM = 56 * 1024 * 1024
F32 = jnp.float32
BF16 = jnp.bfloat16


def dot(a, b):
    return lax.dot_general(a, b, (((1,), (0,)), ((), ())), preferred_element_type=F32)


def dot_nt(a, b):
    return lax.dot_general(a, b, (((1,), (1,)), ((), ())), preferred_element_type=F32)


def dot_tn(a, b):
    return lax.dot_general(a, b, (((0,), (0,)), ((), ())), preferred_element_type=F32)


def iota(shape, axis):
    return lax.broadcasted_iota(jnp.int32, shape, axis)


def pair_matrix(rows, cols, valid):
    r, k = iota((rows, cols), 0), iota((rows, cols), 1)
    return (((k >> 1) == r) & (r < valid)).astype(BF16)


def coarsen(node, rows=None, valid=None):
    rows = node.shape[0] // 2 if rows is None else rows
    valid = rows if valid is None else valid
    return (dot(pair_matrix(rows, node.shape[0], valid), node) * HALF_ROOT).astype(BF16)


def whole(*shape):
    return pl.BlockSpec(shape, lambda *_: (0,) * len(shape))


def call(body, grid, ins, outs, scratch=()):
    return pl.pallas_call(
        body,
        grid_spec=pltpu.PrefetchScalarGridSpec(
            num_scalar_prefetch=1,
            grid=grid,
            in_specs=ins,
            out_specs=[s for s, _ in outs],
            scratch_shapes=list(scratch),
        ),
        out_shape=[jax.ShapeDtypeStruct(shape, kind) for _, (shape, kind) in outs],
        compiler_params=pltpu.CompilerParams(vmem_limit_bytes=VMEM),
    )


def tree_body(pos, x_own, x_oth, wk, wv, kv_out, n1_out, n2_out, n3_out, n4_out, zs_out):
    c, z = pos[0], pos[1]
    for e, x in ((c, x_own), (1 - c, x_oth)):
        kv_out[e, 0] = dot(x[...], wk[...]).astype(BF16)
        kv_out[e, 1] = dot(x[...], wv[...]).astype(BF16)

    def store(ref, *index):
        def put(node):
            for p in range(2):
                ref[index + (p,)] = node[:, H * p : H * p + H]

        return put

    halves = []
    for e in range(2):
        n1 = coarsen(jnp.concatenate([kv_out[e, 0], kv_out[e, 1]], axis=1))
        store(n1_out, e)(n1)
        halves.append(coarsen(n1))
    n2 = jnp.concatenate(halves, axis=0)
    store(n2_out)(n2)
    n3 = coarsen(n2)
    store(n3_out)(n3)
    n4 = coarsen(n3)
    store(n4_out)(n4)
    n5 = coarsen(n4)
    n6 = coarsen(n5, 16, 8)
    n7 = coarsen(n6, 16, 4)
    store(zs_out, z)(jnp.zeros_like(n5))
    store(zs_out, z ^ 1)(n5)
    for far in (2, 3):
        store(zs_out, z ^ far)(n6)
    for far in (4, 5, 6, 7):
        store(zs_out, z ^ far)(n7)


def tree(pos, x_own, x_oth, w_qkv):
    col = lambda part: pl.BlockSpec((D, H), lambda i, s: (0, 2 * part + s[0]))
    outs = [(2, 2, TOK, H), (2, 2, NR, H), (2, NR, H), (2, 64, H), (2, 32, H), (ZN, 2, 16, H)]
    return call(
        tree_body,
        (1,),
        [whole(TOK, D)] * 2 + [col(1), col(2)],
        [(whole(*shape), (shape, BF16)) for shape in outs],
    )(pos, x_own, x_oth, w_qkv, w_qkv)


def project_body(pos, x_own, x_oth, ct_own, ct_oth, wq, wo, perm, q_out, ag_out, xt_out):
    c = pos[0]
    for e, x, ct in ((c, x_own, ct_own), (1 - c, x_oth, ct_oth)):
        q_out[e] = dot(x[...], wq[...]).astype(BF16)
        ag_out[e] = dot_nt(ct[...], wo[...]).astype(BF16)
        xt_out[e] = dot_nt(perm[...], x[...]).astype(BF16)


def project(pos, x_own, x_oth, ct_own, ct_oth, w_qkv, w_out, perm):
    outs = [(2, TOK, H), (2, TOK, H), (2, D, TOK)]
    return call(
        project_body,
        (1,),
        [whole(TOK, D)] * 4
        + [pl.BlockSpec((D, H), lambda i, s: (0, s[0])), pl.BlockSpec((H, D), lambda i, s: (s[0], 0)), whole(D, D)],
        [(whole(*shape), (shape, BF16)) for shape in outs],
    )(pos, x_own, x_oth, ct_own, ct_oth, w_qkv, w_out, perm)


def z_source(z, rows_axis, shape):
    i = iota(shape, rows_axis)
    near = 16 * (z ^ 1) + i
    mid = 16 * (z ^ (2 + ((i - 16) >> 3))) + ((i - 16) & 7)
    far = 16 * (z ^ (4 + ((i - 32) >> 2))) + ((i - 32) & 3)
    return jnp.where(i < 16, near, jnp.where(i < 32, mid, far))


def plane_body(pos, zr, out):
    hot = (iota((ZR, 128), 1) == z_source(pos[1], 0, (ZR, 128))).astype(BF16)
    both = jnp.concatenate([zr[:, p].reshape(128, H) for p in range(2)], axis=1)
    rows = dot(hot, both).astype(BF16)
    for slot in range(8):
        for p in range(2):
            out[slot, p] = rows[:, H * p : H * p + H]


def plane_slots(pos, zr):
    return call(
        plane_body,
        (1,),
        [whole(ZN, 2, 16, H)],
        [(whole(8, 2, ZR, H), ((8, 2, ZR, H), BF16))],
    )(pos, zr)[0]


def attention_body(pos, q, ag, kv, n1, yr, wr, wy, xr, att_out, dq_out, dkv_out, dn1_out, dy_out, dwy_out, dw_out, dx_out, keys, keys_t, s_ref, dw_ref, w_ref, ds_ref, drem):
    for p in range(2):
        for e in range(2):
            keys[e, p, :256] = kv[e, p]
            keys[e, p, 256:384] = n1[1 - e, p]
            keys[e, p, 384:512] = yr[p]
            keys[e, p, 512:640] = wr[p]
            keys[e, p, 640:768] = wy[p]
            for slot in range(8):
                start = 768 + ZR * slot
                keys[e, p, start : start + ZR] = xr[slot, p]
    for p in range(2):
        for e in range(2):
            keys_t[e, p] = keys[e, p].T
    lane = iota((TOK, 128), 1)
    steps = [(e, h) for e in range(2) for h in range(2)]
    masked = {}

    def scores(step):
        e, h = steps[step]
        mine = (lane >> 6) == h
        qh = jnp.where(mine, q[e], jnp.zeros((), BF16))
        ah = jnp.where(mine, ag[e], jnp.zeros((), BF16))
        masked[step] = (qh, ah)
        s_ref[step % 2] = dot_nt(keys[e, 0], qh)
        dw_ref[step % 2] = dot_nt(keys[e, 1], ah * jnp.asarray(DH ** -0.5, BF16))

    scores(0)
    for step, (e, h) in enumerate(steps):
        if step + 1 < len(steps):
            scores(step + 1)
        if h == 0:
            att_t, dq_t = [], []
        s, dw, b = s_ref.at[step % 2], dw_ref.at[step % 2], step % 2
        qh, ah = masked[step]
        top = jnp.max(s[...], axis=0, keepdims=True)
        un = jnp.exp2((s[...] - top) * (LOG2E * DH ** -0.5))
        s[...] = un
        inverse = 1.0 / jnp.sum(un, axis=0, keepdims=True)
        delta = jnp.sum(un * dw[...], axis=0, keepdims=True) * inverse
        prob = s[...] * inverse
        cols = slice(TOK * h, TOK * h + TOK)
        w_ref[e, :, cols] = prob.astype(BF16)
        ds_ref[e, :, cols] = (prob * (dw[...] - delta)).astype(BF16)
        att_t.append(dot(keys_t[e, 1, 64 * h : 64 * h + 64], w_ref[e, :, cols]))
        dq_t.append(dot(keys_t[e, 0, 64 * h : 64 * h + 64], ds_ref[e, :, cols]))
        if h == 0:
            continue
        dk = dot(ds_ref[e], jnp.concatenate([masked[step - 1][0], qh], axis=0))
        dv = dot(w_ref[e], jnp.concatenate([masked[step - 1][1], ah], axis=0))
        att_out[e] = jnp.concatenate(att_t, axis=0).T.astype(BF16)
        dq_out[e] = jnp.concatenate(dq_t, axis=0).T.astype(BF16)
        for p, grad in ((0, dk), (1, dv)):
            dkv_out[e, p] = grad[:256]
            dn1_out[1 - e, p] = grad[256:384]
            if e == 0:
                drem[p] = grad[384:]
            else:
                drem[p] = drem[p] + grad[384:]
    for p in range(2):
        rows = drem[p].astype(BF16)
        dy_out[p] = rows[:128]
        dwy_out[p] = rows[256:384]
        dw_out[p] = drem[p, 128:256]
        for slot in range(8):
            start = 384 + ZR * slot
            dx_out[slot, p] = rows[start : start + ZR]


def attention(pos, q, ag, kv, n1, yr, wr, wy, xr):
    def cut(*lead):
        return pl.BlockSpec(lead + (128,), lambda i, s: (0,) * len(lead) + (i,))

    outs = [
        ((2, TOK), BF16), ((2, TOK), BF16), ((2, 2, TOK), F32), ((2, 2, NR), F32), ((2, NR), BF16), ((2, NR), BF16),
        ((2, NR), F32), ((8, 2, ZR), BF16),
    ]
    n = 1152
    return call(
        attention_body,
        (H // 128,),
        [cut(2, TOK), cut(2, TOK), cut(2, 2, TOK), cut(2, 2, NR), cut(2, NR), cut(2, NR), cut(2, NR), cut(8, 2, ZR)],
        [(cut(*lead), (lead + (H,), kind)) for lead, kind in outs],
        [
            pltpu.VMEM((2, 2, n, 128), BF16), pltpu.VMEM((2, 2, 128, n), BF16), pltpu.VMEM((2, n, TOK), F32), pltpu.VMEM((2, n, TOK), F32),
            pltpu.VMEM((2, n, 2 * TOK), BF16), pltpu.VMEM((2, n, 2 * TOK), BF16), pltpu.VMEM((2, 768, 128), F32),
        ],
    )(pos, q, ag, kv, n1, yr, wr, wy, xr)


def output_body(pos, att_own, att_oth, w_own, w_oth, out):
    c = pos[0]
    out[...] = (dot(att_own[c], w_own[...]) + dot(att_oth[c], w_oth[...])).astype(BF16)


def output_side(pos, att_own, att_oth, w_out):
    row = lambda flip: pl.BlockSpec((H, D), lambda i, s: (s[0] ^ flip, 0))
    return call(
        output_body,
        (1,),
        [whole(2, TOK, H)] * 2 + [row(0), row(1)],
        [(whole(TOK, D), ((TOK, D), BF16))],
    )(pos, att_own, att_oth, w_out, w_out)[0]


def terms_body(pos, att_own, att_oth, ct_own, ct_oth, dq, xt, p_own, p_oth, *rest):
    c, x = pos[0], pos[2] >> 1
    slots = rest[-1]
    total = dot(xt[0], dq[0]) + dot(xt[1], dq[1])
    slots[:, :, 0] = total.astype(BF16).reshape(XN, YN, 96, H)
    total = None
    for e, ct in ((c, ct_own), (1 - c, ct_oth)):
        att_t = (dot_nt(p_own[...], att_own[e]) + dot_nt(p_oth[...], att_oth[e])).astype(BF16)
        term = dot(att_t, ct[...])
        total = term if total is None else total + term
    slots[:, :, 1] = total.astype(BF16).reshape(XN, YN, 96, H)
    for far in range(XN):
        rest[far][...] = slots[x ^ far]


def output_terms(pos, att_own, att_oth, ct_own, ct_oth, dq, xt, perm):
    col = lambda flip, rows: pl.BlockSpec((rows, H), lambda i, s: (0, s[0] ^ flip))
    slot = (YN, 2, 96, H)
    return call(
        terms_body,
        (1,),
        [whole(2, TOK, H)] * 2 + [col(0, TOK)] * 2 + [whole(2, TOK, H), whole(2, D, TOK), col(0, D), col(1, D)],
        [(whole(*slot), (slot, BF16))] * XN,
        [pltpu.VMEM((XN,) + slot, BF16)],
    )(pos, att_own, att_oth, ct_own, ct_oth, dq, xt, perm, perm)


def x_sum_body(pos, t0, t1, t2, t3, *rest):
    y, dp = pos[2] & 1, pos[3]
    slots = rest[-1]
    total = (t0[...].astype(F32) + t1[...].astype(F32)) + (t2[...].astype(F32) + t3[...].astype(F32))
    slots[...] = total.astype(BF16)
    for far in range(4):
        rest[far][...] = slots[y ^ (far >> 1), dp ^ (far & 1)]


def x_sum(pos, *terms):
    shape = (YN, 2, 96, H)
    return call(
        x_sum_body,
        (1,),
        [whole(*shape)] * 4,
        [(whole(96, H), ((96, H), BF16))] * 4,
        [pltpu.VMEM(shape, BF16)],
    )(pos, *terms)


def back_body(pos, xr, dw, dwy, out, *tiers):
    hot = (iota((128, ZR), 0) == z_source(pos[1], 1, (128, ZR))).astype(BF16)
    for p in range(2):
        total = xr[0, p].astype(F32)
        for slot in range(1, 8):
            total = total + xr[slot, p].astype(F32)
        out[:, p] = dot(hot, total.astype(BF16)).astype(BF16).reshape(8, 16, H)
        start = 0
        for tier in tiers:
            rows = tier.shape[1]
            total = dw[p, start : start + rows] + dwy[p, start : start + rows].astype(F32)
            tier[p] = total.astype(BF16)
            start += rows


def back_slots(pos, xr, dw, dwy):
    outs = [(ZN, 2, 16, H), (2, 64, H), (2, 32, H), (2, 32, H)]
    return call(
        back_body,
        (1,),
        [whole(8, 2, ZR, H), whole(2, NR, H), whole(2, NR, H)],
        [(whole(*shape), (shape, BF16)) for shape in outs],
    )(pos, xr, dw, dwy)


def leaf_body(pos, zr, dkv, dn1, dy, g3, g4_a, g4_b, dq, xt, pg_out, grad_out):
    def split(grad):
        high = grad.astype(BF16)
        return [high, (grad - high.astype(F32)).astype(BF16)]

    def hot(hit, scale):
        return jnp.where(hit, scale, 0.0).astype(BF16)

    def wide(ref):
        return jnp.concatenate([ref[0], ref[1]], axis=1)

    zs = jnp.concatenate([zr[:, p].reshape(128, H) for p in range(2)], axis=1)
    ws = jnp.concatenate([wide(g3), wide(g4_a), wide(g4_b)], axis=0)
    ys = wide(dy)
    for e in range(2):
        t, k = iota((TOK, 128), 0), iota((TOK, 128), 1)
        far, row, chip = (k >> 4) ^ pos[1], k & 15, t + TOK * e
        first = hot(t >> 1 == k, 1.0)
        third = hot(chip >> 3 == k, 0.5)
        odd = hot((far == 1) & (row == chip >> 5), 0.25) + hot((far >= 4) & (row == chip >> 7), 0.125)
        second = hot(chip >> 2 == k, 0.5)
        fourth = hot((k >= 64) & (chip >> 4 == k & 31), 0.25)
        even = hot((far >> 1 == 1) & (row == chip >> 6), 0.125)
        up = dot(jnp.concatenate([first, first, third, odd], axis=1), jnp.concatenate(split(wide(dn1.at[e])) + [ws, zs], axis=0))
        up = up * HALF_ROOT + dot(jnp.concatenate([second, fourth, even], axis=1), jnp.concatenate([ys, ws, zs], axis=0))
        for p in range(2):
            pg_out[e, :, H * (1 + p) : H * (2 + p)] = (dkv[e, p] + up[:, H * p : H * p + H]).astype(BF16)
        pg_out[e, :, :H] = dq[e]
    for p in range(2):
        cols = slice(H * (1 + p), H * (2 + p))
        total = dot(xt[0], pg_out[0, :, cols]) + dot(xt[1], pg_out[1, :, cols])
        grad_out[:, p] = total.astype(BF16).reshape(8, 96, H)


def leaf_grads(pos, zr, dkv, dn1, dy, g3, g4_a, g4_b, dq, xt):
    return call(
        leaf_body,
        (1,),
        [
            whole(ZN, 2, 16, H), whole(2, 2, TOK, H), whole(2, 2, NR, H), whole(2, NR, H), whole(2, 64, H), whole(2, 32, H),
            whole(2, 32, H), whole(2, TOK, H), whole(2, D, TOK),
        ],
        [(whole(2, TOK, 3 * H), ((2, TOK, 3 * H), BF16)), (whole(8, 2, 96, H), ((8, 2, 96, H), BF16))],
    )(pos, zr, dkv, dn1, dy, g3, g4_a, g4_b, dq, xt)


def input_body(pos, pg_own, pg_oth, *rest):
    out = rest[-1]
    total = None
    for part in range(3):
        for pg, w in ((pg_own, rest[part]), (pg_oth, rest[3 + part])):
            term = dot_nt(pg[:, H * part : H * part + H], w[...])
            total = term if total is None else total + term
    out[...] = total.astype(BF16)


def input_side(pos, pg_own, pg_oth, w_qkv):
    col = lambda part, flip: pl.BlockSpec((D, H), lambda i, s: (0, 2 * part + (s[0] ^ flip)))
    return call(
        input_body,
        (1,),
        [whole(TOK, 3 * H)] * 2 + [col(part, flip) for flip in (0, 1) for part in range(3)],
        [(whole(TOK, D), ((TOK, D), BF16))],
    )(pos, pg_own, pg_oth, *[w_qkv] * 6)[0]


def total_of(refs):
    total = refs[0].astype(F32)
    for ref in refs[1:]:
        total = total + ref.astype(F32)
    return total


def middle_body(pos, f0, f1, f2, f3, second, out):
    first = total_of([f0[...], f1[...], f2[...], f3[...]]).astype(BF16)
    i, k = iota((256, 96), 0), iota((256, 96), 1)
    row, half = i & 7, (i >> 3) & 1
    hit = (k == 6 * (i >> 4) + row) & (row < 6)
    rows = dot((hit & (half == 0)).astype(BF16), first)
    rows = rows + dot((hit & (half == 1)).astype(BF16), total_of([second[slot] for slot in range(16)]).astype(BF16))
    rows = rows.astype(BF16).reshape(ZN, 2, 16, H)
    for core in range(2):
        out[:, core ^ pos[0]] = rows[:, core]


def middle_sum(pos, firsts, second):
    shape = (ZN, 2, 16, H)
    return call(
        middle_body, (1,), [whole(96, H)] * 4 + [whole(16, 96, H)], [(whole(*shape), (shape, BF16))]
    )(pos, *firsts, second)[0]


def last_body(pos, own, from_dp, from_core, from_both, qkv_out, out_out, parts):
    core, dp = pos[0], pos[3]
    parts[core, dp] = own[...]
    parts[core, 1 - dp] = from_dp[...]
    parts[1 - core, dp] = from_core[...]
    parts[1 - core, 1 - dp] = from_both[...]
    for core in range(2):
        low, high = parts[core, 0].astype(F32), parts[core, 1].astype(F32)
        cols = lambda part: slice(D * part + H * core, D * part + H * core + H)
        qkv_out[:, cols(0)] = low[:6]
        qkv_out[:, cols(1)] = low[8:14]
        qkv_out[:, cols(2)] = high[8:14]
        out_out[:, cols(0)] = high[:6]


def last_rows(pos, *parts):
    return call(
        last_body,
        (1,),
        [whole(16, H)] * 4,
        [(whole(6, 3 * D), ((6, 3 * D), F32)), (whole(6, D), ((6, D), F32))],
        [pltpu.VMEM((2, 2, 16, H), BF16)],
    )(pos, *parts)


def swap(value, axis):
    return lax.ppermute(value, axis, [(0, 1), (1, 0)])


def along(value, axes, far, count=4):
    return lax.ppermute(value, axes, [(i, i ^ far) for i in range(count)])


def row_order():
    f = np.arange(D)
    source = 96 * (f // 12 % 8) + 12 * (f // 96) + f % 12
    return jnp.asarray(source[:, None] == f[None, :], BF16)


def shards(x_tokens, cotangent, w_qkv, w_out):
    x_own, ct_own = x_tokens[0], cotangent[0]
    c, z, dp = lax.axis_index("c"), lax.axis_index("z"), lax.axis_index("dp")
    j = 2 * lax.axis_index("x") + lax.axis_index("y")
    pos = jnp.stack([c, z, j, dp]).astype(jnp.int32)
    x_oth, ct_oth = swap(x_own, "c"), swap(ct_own, "c")
    perm = row_order()

    kv, n1, n2, n3, n4, zs = tree(pos, x_own, x_oth, w_qkv)
    yr = swap(n2, "y")
    wr = jnp.concatenate([along(n3, "x", 1), along(n4, "x", 2), along(n4, "x", 3)], axis=1)
    zr = lax.all_to_all(zs, "z", 0, 0)
    zr, yr, wr, ct_oth = lax.optimization_barrier((zr, yr, wr, ct_oth))
    wy = swap(wr, "y")
    xr = lax.all_to_all(plane_slots(pos, zr), ("x", "y"), 0, 0)
    q, ag, xt = project(pos, x_own, x_oth, ct_own, ct_oth, w_qkv, w_out, perm)
    att, dq, dkv, dn1, dy, dwy, dw, dx = attention(pos, q, ag, kv, n1, yr, wr, wy, xr)

    dx_r = lax.all_to_all(dx, ("x", "y"), 0, 0)
    att_oth = swap(att, "c")
    dwy = swap(dwy, "y")
    first, *firsts = output_terms(pos, att, att_oth, ct_own, ct_oth, dq, xt, perm)
    firsts = [along(firsts[far - 1], "x", far) for far in (1, 2, 3)]
    dx_r, first, firsts[0], dwy = lax.optimization_barrier((dx_r, first, firsts[0], dwy))
    dz, g3, g4_a, g4_b = back_slots(pos, dx_r, dw, dwy)
    dz_r = lax.all_to_all(dz, "z", 0, 0)
    g3, g4_a, g4_b, firsts = lax.optimization_barrier((g3, g4_a, g4_b, firsts))
    g3, g4_a, g4_b = along(g3, "x", 1), along(g4_a, "x", 2), along(g4_b, "x", 3)
    firsts = x_sum(pos, first, *firsts)
    dz_r, g3, g4_a, g4_b, first = lax.optimization_barrier((dz_r, g3, g4_a, g4_b, firsts[0]))
    firsts = [first] + [along(firsts[far], ("y", "dp"), far) for far in (1, 2, 3)]
    pg, terms = leaf_grads(pos, dz_r, dkv, dn1, swap(dy, "y"), g3, g4_a, g4_b, dq, xt)
    terms, firsts = lax.optimization_barrier((terms, firsts))
    terms = lax.all_to_all(terms.reshape(16, 96, H), ("x", "y", "dp"), 0, 0)
    pg_own = lax.dynamic_index_in_dim(pg, c, 0, keepdims=False)
    pg_oth = swap(lax.dynamic_index_in_dim(pg, 1 - c, 0, keepdims=False), "c")
    input_grad = input_side(pos, pg_own, pg_oth, w_qkv)
    layer_out = output_side(pos, att, att_oth, w_out)
    terms, input_grad, layer_out = lax.optimization_barrier((terms, input_grad, layer_out))
    terms = lax.all_to_all(middle_sum(pos, firsts, terms), "z", 0, 0)
    own, oth = (jnp.sum(terms[:, core].astype(F32), axis=0).astype(BF16) for core in range(2))
    pair = ("c", "dp")
    qkv_grad, out_grad = last_rows(pos, own, along(own, pair, 1), along(oth, pair, 2), along(oth, pair, 3))
    return (layer_out[None], input_grad[None], qkv_grad, out_grad)


def solution(mesh):
    split = Mesh(mesh.devices.reshape(ZN, XN, YN, 2, 2), ("z", "x", "y", "c", "dp"))
    seq = ("z", "x", "y", "c")
    return jax.shard_map(
        shards,
        mesh=split,
        in_specs=(P("dp", seq, None), P("dp", seq, None), P(), P()),
        out_specs=(P("dp", seq, None), P("dp", seq, None), P(seq, None), P(seq, None)),
        check_vma=False,
    )
```

```python
import jax
import jax.numpy as jnp
import numpy as np
from jax import lax
from jax.experimental import pallas as pl
from jax.experimental.pallas import tpu as pltpu
from jax.sharding import Mesh, PartitionSpec as P

D = 768
H = 384
TOK = 256
NR = 128
DH = 64
ZN, XN, YN = 8, 4, 2
ZR = 48
HALF_ROOT = 0.7071067811865476
LOG2E = 1.4426950408889634
VMEM = 56 * 1024 * 1024
F32 = jnp.float32
BF16 = jnp.bfloat16


def dot(a, b):
    return lax.dot_general(a, b, (((1,), (0,)), ((), ())), preferred_element_type=F32)


def dot_nt(a, b):
    return lax.dot_general(a, b, (((1,), (1,)), ((), ())), preferred_element_type=F32)


def dot_tn(a, b):
    return lax.dot_general(a, b, (((0,), (0,)), ((), ())), preferred_element_type=F32)


def iota(shape, axis):
    return lax.broadcasted_iota(jnp.int32, shape, axis)


def pair_matrix(rows, cols, valid):
    r, k = iota((rows, cols), 0), iota((rows, cols), 1)
    return (((k >> 1) == r) & (r < valid)).astype(BF16)


def coarsen(node, rows=None, valid=None):
    rows = node.shape[0] // 2 if rows is None else rows
    valid = rows if valid is None else valid
    return (dot(pair_matrix(rows, node.shape[0], valid), node) * HALF_ROOT).astype(BF16)


def whole(*shape):
    return pl.BlockSpec(shape, lambda *_: (0,) * len(shape))


def call(body, grid, ins, outs, scratch=()):
    return pl.pallas_call(
        body,
        grid_spec=pltpu.PrefetchScalarGridSpec(
            num_scalar_prefetch=1,
            grid=grid,
            in_specs=ins,
            out_specs=[s for s, _ in outs],
            scratch_shapes=list(scratch),
        ),
        out_shape=[jax.ShapeDtypeStruct(shape, kind) for _, (shape, kind) in outs],
        compiler_params=pltpu.CompilerParams(vmem_limit_bytes=VMEM),
    )


def tree_body(pos, x_own, x_oth, wk, wv, kv_out, n1_out, n2_out, n3_out, n4_out, zs_out):
    c, z = pos[0], pos[1]
    for e, x in ((c, x_own), (1 - c, x_oth)):
        kv_out[e, 0] = dot(x[...], wk[...]).astype(BF16)
        kv_out[e, 1] = dot(x[...], wv[...]).astype(BF16)

    def store(ref, *index):
        def put(node):
            for p in range(2):
                ref[index + (p,)] = node[:, H * p : H * p + H]

        return put

    halves = []
    for e in range(2):
        n1 = coarsen(jnp.concatenate([kv_out[e, 0], kv_out[e, 1]], axis=1))
        store(n1_out, e)(n1)
        halves.append(coarsen(n1))
    n2 = jnp.concatenate(halves, axis=0)
    store(n2_out)(n2)
    n3 = coarsen(n2)
    store(n3_out)(n3)
    n4 = coarsen(n3)
    store(n4_out)(n4)
    n5 = coarsen(n4)
    n6 = coarsen(n5, 16, 8)
    n7 = coarsen(n6, 16, 4)
    store(zs_out, z)(jnp.zeros_like(n5))
    store(zs_out, z ^ 1)(n5)
    for far in (2, 3):
        store(zs_out, z ^ far)(n6)
    for far in (4, 5, 6, 7):
        store(zs_out, z ^ far)(n7)


def tree(pos, x_own, x_oth, w_qkv):
    col = lambda part: pl.BlockSpec((D, H), lambda i, s: (0, 2 * part + s[0]))
    outs = [(2, 2, TOK, H), (2, 2, NR, H), (2, NR, H), (2, 64, H), (2, 32, H), (ZN, 2, 16, H)]
    return call(
        tree_body,
        (1,),
        [whole(TOK, D)] * 2 + [col(1), col(2)],
        [(whole(*shape), (shape, BF16)) for shape in outs],
    )(pos, x_own, x_oth, w_qkv, w_qkv)


def project_body(pos, x_own, x_oth, ct_own, ct_oth, wq, wo, perm, q_out, ag_out, xt_out):
    c = pos[0]
    for e, x, ct in ((c, x_own, ct_own), (1 - c, x_oth, ct_oth)):
        q_out[e] = dot(x[...], wq[...]).astype(BF16)
        ag_out[e] = dot_nt(ct[...], wo[...]).astype(BF16)
        xt_out[e] = dot_nt(perm[...], x[...]).astype(BF16)


def project(pos, x_own, x_oth, ct_own, ct_oth, w_qkv, w_out, perm):
    outs = [(2, TOK, H), (2, TOK, H), (2, D, TOK)]
    return call(
        project_body,
        (1,),
        [whole(TOK, D)] * 4
        + [pl.BlockSpec((D, H), lambda i, s: (0, s[0])), pl.BlockSpec((H, D), lambda i, s: (s[0], 0)), whole(D, D)],
        [(whole(*shape), (shape, BF16)) for shape in outs],
    )(pos, x_own, x_oth, ct_own, ct_oth, w_qkv, w_out, perm)


def z_source(z, rows_axis, shape):
    i = iota(shape, rows_axis)
    near = 16 * (z ^ 1) + i
    mid = 16 * (z ^ (2 + ((i - 16) >> 3))) + ((i - 16) & 7)
    far = 16 * (z ^ (4 + ((i - 32) >> 2))) + ((i - 32) & 3)
    return jnp.where(i < 16, near, jnp.where(i < 32, mid, far))


def plane_body(pos, zr, out):
    hot = (iota((ZR, 128), 1) == z_source(pos[1], 0, (ZR, 128))).astype(BF16)
    both = jnp.concatenate([zr[:, p].reshape(128, H) for p in range(2)], axis=1)
    rows = dot(hot, both).astype(BF16)
    for slot in range(8):
        for p in range(2):
            out[slot, p] = rows[:, H * p : H * p + H]


def plane_slots(pos, zr):
    return call(
        plane_body,
        (1,),
        [whole(ZN, 2, 16, H)],
        [(whole(8, 2, ZR, H), ((8, 2, ZR, H), BF16))],
    )(pos, zr)[0]


def attention_body(pos, q, ag, kv, n1, yr, wr, wy, xr, att_out, dq_out, dkv_out, dn1_out, dy_out, dwy_out, dw_out, dx_out, keys, keys_t, s_ref, dw_ref, w_ref, ds_ref, drem):
    for p in range(2):
        for e in range(2):
            keys[e, p, :256] = kv[e, p]
            keys[e, p, 256:384] = n1[1 - e, p]
            keys[e, p, 384:512] = yr[p]
            keys[e, p, 512:640] = wr[p]
            keys[e, p, 640:768] = wy[p]
            for slot in range(8):
                start = 768 + ZR * slot
                keys[e, p, start : start + ZR] = xr[slot, p]
    for p in range(2):
        for e in range(2):
            keys_t[e, p] = keys[e, p].T
    lane = iota((TOK, 128), 1)
    steps = [(e, h) for e in range(2) for h in range(2)]
    masked = {}

    def scores(step):
        e, h = steps[step]
        mine = (lane >> 6) == h
        qh = jnp.where(mine, q[e], jnp.zeros((), BF16))
        ah = jnp.where(mine, ag[e], jnp.zeros((), BF16))
        masked[step] = (qh, ah)
        s_ref[step % 2] = dot_nt(keys[e, 0], qh)
        dw_ref[step % 2] = dot_nt(keys[e, 1], ah * jnp.asarray(DH ** -0.5, BF16))

    scores(0)
    for step, (e, h) in enumerate(steps):
        if step + 1 < len(steps):
            scores(step + 1)
        if h == 0:
            att_t, dq_t = [], []
        s, dw, b = s_ref.at[step % 2], dw_ref.at[step % 2], step % 2
        qh, ah = masked[step]
        top = jnp.max(s[...], axis=0, keepdims=True)
        un = jnp.exp2((s[...] - top) * (LOG2E * DH ** -0.5))
        s[...] = un
        inverse = 1.0 / jnp.sum(un, axis=0, keepdims=True)
        delta = jnp.sum(un * dw[...], axis=0, keepdims=True) * inverse
        prob = s[...] * inverse
        cols = slice(TOK * h, TOK * h + TOK)
        w_ref[e, :, cols] = prob.astype(BF16)
        ds_ref[e, :, cols] = (prob * (dw[...] - delta)).astype(BF16)
        att_t.append(dot(keys_t[e, 1, 64 * h : 64 * h + 64], w_ref[e, :, cols]))
        dq_t.append(dot(keys_t[e, 0, 64 * h : 64 * h + 64], ds_ref[e, :, cols]))
        if h == 0:
            continue
        dk = dot(ds_ref[e], jnp.concatenate([masked[step - 1][0], qh], axis=0))
        dv = dot(w_ref[e], jnp.concatenate([masked[step - 1][1], ah], axis=0))
        att_out[e] = jnp.concatenate(att_t, axis=0).T.astype(BF16)
        dq_out[e] = jnp.concatenate(dq_t, axis=0).T.astype(BF16)
        for p, grad in ((0, dk), (1, dv)):
            dkv_out[e, p] = grad[:256]
            dn1_out[1 - e, p] = grad[256:384]
            if e == 0:
                drem[p] = grad[384:]
            else:
                drem[p] = drem[p] + grad[384:]
    for p in range(2):
        rows = drem[p].astype(BF16)
        dy_out[p] = rows[:128]
        dwy_out[p] = rows[256:384]
        dw_out[p] = drem[p, 128:256]
        for slot in range(8):
            start = 384 + ZR * slot
            dx_out[slot, p] = rows[start : start + ZR]


def attention(pos, q, ag, kv, n1, yr, wr, wy, xr):
    def cut(*lead):
        return pl.BlockSpec(lead + (128,), lambda i, s: (0,) * len(lead) + (i,))

    outs = [
        ((2, TOK), BF16), ((2, TOK), BF16), ((2, 2, TOK), F32), ((2, 2, NR), F32), ((2, NR), BF16), ((2, NR), BF16),
        ((2, NR), F32), ((8, 2, ZR), BF16),
    ]
    n = 1152
    return call(
        attention_body,
        (H // 128,),
        [cut(2, TOK), cut(2, TOK), cut(2, 2, TOK), cut(2, 2, NR), cut(2, NR), cut(2, NR), cut(2, NR), cut(8, 2, ZR)],
        [(cut(*lead), (lead + (H,), kind)) for lead, kind in outs],
        [
            pltpu.VMEM((2, 2, n, 128), BF16), pltpu.VMEM((2, 2, 128, n), BF16), pltpu.VMEM((2, n, TOK), F32), pltpu.VMEM((2, n, TOK), F32),
            pltpu.VMEM((2, n, 2 * TOK), BF16), pltpu.VMEM((2, n, 2 * TOK), BF16), pltpu.VMEM((2, 768, 128), F32),
        ],
    )(pos, q, ag, kv, n1, yr, wr, wy, xr)


def output_body(pos, att_own, att_oth, w_own, w_oth, out):
    c = pos[0]
    out[...] = (dot(att_own[c], w_own[...]) + dot(att_oth[c], w_oth[...])).astype(BF16)


def output_side(pos, att_own, att_oth, w_out):
    row = lambda flip: pl.BlockSpec((H, D), lambda i, s: (s[0] ^ flip, 0))
    return call(
        output_body,
        (1,),
        [whole(2, TOK, H)] * 2 + [row(0), row(1)],
        [(whole(TOK, D), ((TOK, D), BF16))],
    )(pos, att_own, att_oth, w_out, w_out)[0]


def terms_body(pos, att_own, att_oth, ct_own, ct_oth, dq, xt, p_own, p_oth, *rest):
    c, x = pos[0], pos[2] >> 1
    slots = rest[-1]
    total = dot(xt[0], dq[0]) + dot(xt[1], dq[1])
    slots[:, :, 0] = total.astype(BF16).reshape(XN, YN, 96, H)
    total = None
    for e, ct in ((c, ct_own), (1 - c, ct_oth)):
        att_t = (dot_nt(p_own[...], att_own[e]) + dot_nt(p_oth[...], att_oth[e])).astype(BF16)
        term = dot(att_t, ct[...])
        total = term if total is None else total + term
    slots[:, :, 1] = total.astype(BF16).reshape(XN, YN, 96, H)
    for far in range(XN):
        rest[far][...] = slots[x ^ far]


def output_terms(pos, att_own, att_oth, ct_own, ct_oth, dq, xt, perm):
    col = lambda flip, rows: pl.BlockSpec((rows, H), lambda i, s: (0, s[0] ^ flip))
    slot = (YN, 2, 96, H)
    return call(
        terms_body,
        (1,),
        [whole(2, TOK, H)] * 2 + [col(0, TOK)] * 2 + [whole(2, TOK, H), whole(2, D, TOK), col(0, D), col(1, D)],
        [(whole(*slot), (slot, BF16))] * XN,
        [pltpu.VMEM((XN,) + slot, BF16)],
    )(pos, att_own, att_oth, ct_own, ct_oth, dq, xt, perm, perm)


def x_sum_body(pos, t0, t1, t2, t3, *rest):
    y, dp = pos[2] & 1, pos[3]
    slots = rest[-1]
    total = (t0[...].astype(F32) + t1[...].astype(F32)) + (t2[...].astype(F32) + t3[...].astype(F32))
    slots[...] = total.astype(BF16)
    for far in range(4):
        rest[far][...] = slots[y ^ (far >> 1), dp ^ (far & 1)]


def x_sum(pos, *terms):
    shape = (YN, 2, 96, H)
    return call(
        x_sum_body,
        (1,),
        [whole(*shape)] * 4,
        [(whole(96, H), ((96, H), BF16))] * 4,
        [pltpu.VMEM(shape, BF16)],
    )(pos, *terms)


def back_body(pos, xr, dw, dwy, out, *tiers):
    hot = (iota((128, ZR), 0) == z_source(pos[1], 1, (128, ZR))).astype(BF16)
    for p in range(2):
        total = xr[0, p].astype(F32)
        for slot in range(1, 8):
            total = total + xr[slot, p].astype(F32)
        out[:, p] = dot(hot, total.astype(BF16)).astype(BF16).reshape(8, 16, H)
        start = 0
        for tier in tiers:
            rows = tier.shape[1]
            total = dw[p, start : start + rows] + dwy[p, start : start + rows].astype(F32)
            tier[p] = total.astype(BF16)
            start += rows


def back_slots(pos, xr, dw, dwy):
    outs = [(ZN, 2, 16, H), (2, 64, H), (2, 32, H), (2, 32, H)]
    return call(
        back_body,
        (1,),
        [whole(8, 2, ZR, H), whole(2, NR, H), whole(2, NR, H)],
        [(whole(*shape), (shape, BF16)) for shape in outs],
    )(pos, xr, dw, dwy)


def leaf_body(pos, zr, dkv, dn1, dy, g3, g4_a, g4_b, dq, xt, pg_out, grad_out):
    def split(grad):
        high = grad.astype(BF16)
        return [high, (grad - high.astype(F32)).astype(BF16)]

    def hot(hit, scale):
        return jnp.where(hit, scale, 0.0).astype(BF16)

    def wide(ref):
        return jnp.concatenate([ref[0], ref[1]], axis=1)

    zs = jnp.concatenate([zr[:, p].reshape(128, H) for p in range(2)], axis=1)
    ws = jnp.concatenate([wide(g3), wide(g4_a), wide(g4_b)], axis=0)
    ys = wide(dy)
    for e in range(2):
        t, k = iota((TOK, 128), 0), iota((TOK, 128), 1)
        far, row, chip = (k >> 4) ^ pos[1], k & 15, t + TOK * e
        first = hot(t >> 1 == k, 1.0)
        third = hot(chip >> 3 == k, 0.5)
        odd = hot((far == 1) & (row == chip >> 5), 0.25) + hot((far >= 4) & (row == chip >> 7), 0.125)
        second = hot(chip >> 2 == k, 0.5)
        fourth = hot((k >= 64) & (chip >> 4 == k & 31), 0.25)
        even = hot((far >> 1 == 1) & (row == chip >> 6), 0.125)
        up = dot(jnp.concatenate([first, first, third, odd], axis=1), jnp.concatenate(split(wide(dn1.at[e])) + [ws, zs], axis=0))
        up = up * HALF_ROOT + dot(jnp.concatenate([second, fourth, even], axis=1), jnp.concatenate([ys, ws, zs], axis=0))
        for p in range(2):
            pg_out[e, :, H * (1 + p) : H * (2 + p)] = (dkv[e, p] + up[:, H * p : H * p + H]).astype(BF16)
        pg_out[e, :, :H] = dq[e]
    for p in range(2):
        cols = slice(H * (1 + p), H * (2 + p))
        total = dot(xt[0], pg_out[0, :, cols]) + dot(xt[1], pg_out[1, :, cols])
        grad_out[:, p] = total.astype(BF16).reshape(8, 96, H)


def leaf_grads(pos, zr, dkv, dn1, dy, g3, g4_a, g4_b, dq, xt):
    return call(
        leaf_body,
        (1,),
        [
            whole(ZN, 2, 16, H), whole(2, 2, TOK, H), whole(2, 2, NR, H), whole(2, NR, H), whole(2, 64, H), whole(2, 32, H),
            whole(2, 32, H), whole(2, TOK, H), whole(2, D, TOK),
        ],
        [(whole(2, TOK, 3 * H), ((2, TOK, 3 * H), BF16)), (whole(8, 2, 96, H), ((8, 2, 96, H), BF16))],
    )(pos, zr, dkv, dn1, dy, g3, g4_a, g4_b, dq, xt)


def input_body(pos, pg_own, pg_oth, *rest):
    out = rest[-1]
    total = None
    for part in range(3):
        for pg, w in ((pg_own, rest[part]), (pg_oth, rest[3 + part])):
            term = dot_nt(pg[:, H * part : H * part + H], w[...])
            total = term if total is None else total + term
    out[...] = total.astype(BF16)


def input_side(pos, pg_own, pg_oth, w_qkv):
    col = lambda part, flip: pl.BlockSpec((D, H), lambda i, s: (0, 2 * part + (s[0] ^ flip)))
    return call(
        input_body,
        (1,),
        [whole(TOK, 3 * H)] * 2 + [col(part, flip) for flip in (0, 1) for part in range(3)],
        [(whole(TOK, D), ((TOK, D), BF16))],
    )(pos, pg_own, pg_oth, *[w_qkv] * 6)[0]


def total_of(refs):
    total = refs[0].astype(F32)
    for ref in refs[1:]:
        total = total + ref.astype(F32)
    return total


def middle_body(pos, f0, f1, f2, f3, second, out):
    first = total_of([f0[...], f1[...], f2[...], f3[...]]).astype(BF16)
    i, k = iota((256, 96), 0), iota((256, 96), 1)
    row, half = i & 7, (i >> 3) & 1
    hit = (k == 6 * (i >> 4) + row) & (row < 6)
    rows = dot((hit & (half == 0)).astype(BF16), first)
    rows = rows + dot((hit & (half == 1)).astype(BF16), total_of([second[slot] for slot in range(16)]).astype(BF16))
    rows = rows.astype(BF16).reshape(ZN, 2, 16, H)
    for core in range(2):
        out[:, core ^ pos[0]] = rows[:, core]


def middle_sum(pos, firsts, second):
    shape = (ZN, 2, 16, H)
    return call(
        middle_body, (1,), [whole(96, H)] * 4 + [whole(16, 96, H)], [(whole(*shape), (shape, BF16))]
    )(pos, *firsts, second)[0]


def last_body(pos, own, from_dp, from_core, from_both, qkv_out, out_out, parts):
    core, dp = pos[0], pos[3]
    parts[core, dp] = own[...]
    parts[core, 1 - dp] = from_dp[...]
    parts[1 - core, dp] = from_core[...]
    parts[1 - core, 1 - dp] = from_both[...]
    for core in range(2):
        low, high = parts[core, 0].astype(F32), parts[core, 1].astype(F32)
        cols = lambda part: slice(D * part + H * core, D * part + H * core + H)
        qkv_out[:, cols(0)] = low[:6]
        qkv_out[:, cols(1)] = low[8:14]
        qkv_out[:, cols(2)] = high[8:14]
        out_out[:, cols(0)] = high[:6]


def last_rows(pos, *parts):
    return call(
        last_body,
        (1,),
        [whole(16, H)] * 4,
        [(whole(6, 3 * D), ((6, 3 * D), F32)), (whole(6, D), ((6, D), F32))],
        [pltpu.VMEM((2, 2, 16, H), BF16)],
    )(pos, *parts)


def swap(value, axis):
    return lax.ppermute(value, axis, [(0, 1), (1, 0)])


def along(value, axes, far, count=4):
    return lax.ppermute(value, axes, [(i, i ^ far) for i in range(count)])


def row_order():
    f = np.arange(D)
    source = 96 * (f // 12 % 8) + 12 * (f // 96) + f % 12
    return jnp.asarray(source[:, None] == f[None, :], BF16)


def shards(x_tokens, cotangent, w_qkv, w_out):
    x_own, ct_own = x_tokens[0], cotangent[0]
    c, z, dp = lax.axis_index("c"), lax.axis_index("z"), lax.axis_index("dp")
    j = 2 * lax.axis_index("x") + lax.axis_index("y")
    pos = jnp.stack([c, z, j, dp]).astype(jnp.int32)
    x_oth, ct_oth = swap(x_own, "c"), swap(ct_own, "c")
    perm = row_order()

    kv, n1, n2, n3, n4, zs = tree(pos, x_own, x_oth, w_qkv)
    yr = swap(n2, "y")
    wr = jnp.concatenate([along(n3, "x", 1), along(n4, "x", 2), along(n4, "x", 3)], axis=1)
    zr = lax.all_to_all(zs, "z", 0, 0)
    zr, yr, wr, ct_oth = lax.optimization_barrier((zr, yr, wr, ct_oth))
    wy = swap(wr, "y")
    xs, wy = lax.optimization_barrier((plane_slots(pos, zr), wy))
    xr = lax.all_to_all(xs, ("x", "y"), 0, 0)
    q, ag, xt = project(pos, x_own, x_oth, ct_own, ct_oth, w_qkv, w_out, perm)
    att, dq, dkv, dn1, dy, dwy, dw, dx = attention(pos, q, ag, kv, n1, yr, wr, wy, xr)

    dx_r = lax.all_to_all(dx, ("x", "y"), 0, 0)
    att_oth = swap(att, "c")
    dwy = swap(dwy, "y")
    first, *firsts = output_terms(pos, att, att_oth, ct_own, ct_oth, dq, xt, perm)
    firsts = [along(firsts[far - 1], "x", far) for far in (1, 2, 3)]
    dx_r, first, firsts[0], dwy = lax.optimization_barrier((dx_r, first, firsts[0], dwy))
    dz, g3, g4_a, g4_b = back_slots(pos, dx_r, dw, dwy)
    dz_r = lax.all_to_all(dz, "z", 0, 0)
    g3, g4_a, g4_b, firsts = lax.optimization_barrier((g3, g4_a, g4_b, firsts))
    g3, g4_a, g4_b = along(g3, "x", 1), along(g4_a, "x", 2), along(g4_b, "x", 3)
    pg, terms = leaf_grads(pos, dz_r, dkv, dn1, swap(dy, "y"), g3, g4_a, g4_b, dq, xt)
    terms, first, firsts = lax.optimization_barrier((terms, first, firsts))
    firsts = x_sum(pos, first, *firsts)
    firsts = list(firsts[:1]) + [along(firsts[far], ("y", "dp"), far) for far in (1, 2, 3)]
    terms = lax.all_to_all(terms.reshape(16, 96, H), ("x", "y", "dp"), 0, 0)
    pg_own = lax.dynamic_index_in_dim(pg, c, 0, keepdims=False)
    pg_oth = swap(lax.dynamic_index_in_dim(pg, 1 - c, 0, keepdims=False), "c")
    input_grad = input_side(pos, pg_own, pg_oth, w_qkv)
    terms, input_grad = lax.optimization_barrier((terms, input_grad))
    terms, att, att_oth = lax.optimization_barrier((middle_sum(pos, firsts, terms), att, att_oth))
    terms = lax.all_to_all(terms, "z", 0, 0)
    terms, layer_out = lax.optimization_barrier((terms, output_side(pos, att, att_oth, w_out)))
    own, oth = (jnp.sum(terms[:, core].astype(F32), axis=0).astype(BF16) for core in range(2))
    pair = ("c", "dp")
    qkv_grad, out_grad = last_rows(pos, own, along(own, pair, 1), along(oth, pair, 2), along(oth, pair, 3))
    return (layer_out[None], input_grad[None], qkv_grad, out_grad)


def solution(mesh):
    split = Mesh(mesh.devices.reshape(ZN, XN, YN, 2, 2), ("z", "x", "y", "c", "dp"))
    seq = ("z", "x", "y", "c")
    return jax.shard_map(
        shards,
        mesh=split,
        in_specs=(P("dp", seq, None), P("dp", seq, None), P(), P()),
        out_specs=(P("dp", seq, None), P("dp", seq, None), P(seq, None), P(seq, None)),
        check_vma=False,
    )
```

```python
import jax
import jax.numpy as jnp
import numpy as np
from jax import lax
from jax.experimental import pallas as pl
from jax.experimental.pallas import tpu as pltpu
from jax.sharding import Mesh, PartitionSpec as P

D = 768
H = 384
TOK = 256
NR = 128
DH = 64
ZN, XN, YN = 8, 4, 2
ZR = 48
HALF_ROOT = 0.7071067811865476
LOG2E = 1.4426950408889634
VMEM = 56 * 1024 * 1024
F32 = jnp.float32
BF16 = jnp.bfloat16


def dot(a, b):
    return lax.dot_general(a, b, (((1,), (0,)), ((), ())), preferred_element_type=F32)


def dot_nt(a, b):
    return lax.dot_general(a, b, (((1,), (1,)), ((), ())), preferred_element_type=F32)


def dot_tn(a, b):
    return lax.dot_general(a, b, (((0,), (0,)), ((), ())), preferred_element_type=F32)


def iota(shape, axis):
    return lax.broadcasted_iota(jnp.int32, shape, axis)


def pair_matrix(rows, cols, valid):
    r, k = iota((rows, cols), 0), iota((rows, cols), 1)
    return (((k >> 1) == r) & (r < valid)).astype(BF16)


def coarsen(node, rows=None, valid=None):
    rows = node.shape[0] // 2 if rows is None else rows
    valid = rows if valid is None else valid
    return (dot(pair_matrix(rows, node.shape[0], valid), node) * HALF_ROOT).astype(BF16)


def whole(*shape):
    return pl.BlockSpec(shape, lambda *_: (0,) * len(shape))


def call(body, grid, ins, outs, scratch=()):
    return pl.pallas_call(
        body,
        grid_spec=pltpu.PrefetchScalarGridSpec(
            num_scalar_prefetch=1,
            grid=grid,
            in_specs=ins,
            out_specs=[s for s, _ in outs],
            scratch_shapes=list(scratch),
        ),
        out_shape=[jax.ShapeDtypeStruct(shape, kind) for _, (shape, kind) in outs],
        compiler_params=pltpu.CompilerParams(vmem_limit_bytes=VMEM),
    )


def tree_body(pos, x_own, x_oth, wk, wv, kv_out, n1_out, n2_out, n3_out, n4_out, zs_out, rows, pad):
    c, z = pos[0], pos[1]
    for e, x in ((c, x_own), (1 - c, x_oth)):
        for p, w in ((0, wk), (1, wv)):
            part = dot(x[...], w[...]).astype(BF16)
            kv_out[e, p] = part
            for n in range(3):
                rows[e, 3 * p + n] = part[:, 128 * n : 128 * n + 128].astype(F32)

    def coarser(ref, n):
        node = ((ref[pl.ds(0, n, stride=2), :] + ref[pl.ds(1, n, stride=2), :]) * HALF_ROOT).astype(BF16)
        return node, node.astype(F32)

    for p in range(2):
        for n in range(3):
            cols, block = slice(128 * n, 128 * n + 128), 3 * p + n
            top = pad.at[block]
            for e in range(2):
                ref = rows.at[e, block]
                n1_out[e, p, :, cols], wide = coarser(ref, NR)
                ref[:NR] = wide
                n2_out[p, 64 * e : 64 * e + 64, cols], wide = coarser(ref, 64)
                top[64 * e : 64 * e + 64] = wide
            n3_out[p, :, cols], wide = coarser(top, 64)
            top[:64] = wide
            n4_out[p, :, cols], wide = coarser(top, 32)
            top[:32] = wide
            n5, wide = coarser(top, 16)
            top[:16] = wide
            top[16:48] = jnp.zeros((32, 128), F32)
            top[16:24] = coarser(top, 8)[1]
            top[32:36] = coarser(top.at[pl.ds(16, 8)], 4)[1]
            n6, n7 = top[16:32].astype(BF16), top[32:48].astype(BF16)
            zs_out[z, p, :, cols] = jnp.zeros_like(n5)
            zs_out[z ^ 1, p, :, cols] = n5
            for far in (2, 3):
                zs_out[z ^ far, p, :, cols] = n6
            for far in (4, 5, 6, 7):
                zs_out[z ^ far, p, :, cols] = n7


def tree(pos, x_own, x_oth, w_qkv):
    col = lambda part: pl.BlockSpec((D, H), lambda i, s: (0, 2 * part + s[0]))
    outs = [(2, 2, TOK, H), (2, 2, NR, H), (2, NR, H), (2, 64, H), (2, 32, H), (ZN, 2, 16, H)]
    return call(
        tree_body,
        (1,),
        [whole(TOK, D)] * 2 + [col(1), col(2)],
        [(whole(*shape), (shape, BF16)) for shape in outs],
        [pltpu.VMEM((2, 6, TOK, 128), F32), pltpu.VMEM((6, NR, 128), F32)],
    )(pos, x_own, x_oth, w_qkv, w_qkv)


def project_body(pos, x_own, x_oth, ct_own, ct_oth, wq, wo, perm, q_out, ag_out, xt_out):
    c = pos[0]
    for e, x, ct in ((c, x_own, ct_own), (1 - c, x_oth, ct_oth)):
        q_out[e] = dot(x[...], wq[...]).astype(BF16)
        ag_out[e] = dot_nt(ct[...], wo[...]).astype(BF16)
        xt_out[e] = dot_nt(perm[...], x[...]).astype(BF16)


def project(pos, x_own, x_oth, ct_own, ct_oth, w_qkv, w_out, perm):
    outs = [(2, TOK, H), (2, TOK, H), (2, D, TOK)]
    return call(
        project_body,
        (1,),
        [whole(TOK, D)] * 4
        + [pl.BlockSpec((D, H), lambda i, s: (0, s[0])), pl.BlockSpec((H, D), lambda i, s: (s[0], 0)), whole(D, D)],
        [(whole(*shape), (shape, BF16)) for shape in outs],
    )(pos, x_own, x_oth, ct_own, ct_oth, w_qkv, w_out, perm)


def z_source(z, rows_axis, shape):
    i = iota(shape, rows_axis)
    near = 16 * (z ^ 1) + i
    mid = 16 * (z ^ (2 + ((i - 16) >> 3))) + ((i - 16) & 7)
    far = 16 * (z ^ (4 + ((i - 32) >> 2))) + ((i - 32) & 3)
    return jnp.where(i < 16, near, jnp.where(i < 32, mid, far))


def plane_body(pos, zr, out):
    hot = (iota((ZR, 128), 1) == z_source(pos[1], 0, (ZR, 128))).astype(BF16)
    both = jnp.concatenate([zr[:, p].reshape(128, H) for p in range(2)], axis=1)
    rows = dot(hot, both).astype(BF16)
    for slot in range(8):
        for p in range(2):
            out[slot, p] = rows[:, H * p : H * p + H]


def plane_slots(pos, zr):
    return call(
        plane_body,
        (1,),
        [whole(ZN, 2, 16, H)],
        [(whole(8, 2, ZR, H), ((8, 2, ZR, H), BF16))],
    )(pos, zr)[0]


def attention_body(pos, q, ag, kv, n1, yr, wr, wy, xr, att_out, dq_out, dkv_out, dn1_out, dy_out, dwy_out, dw_out, dx_out, near, near_t, shared, shared_t, s_ref, dw_ref, w_ref, ds_ref, drem):
    for p in range(2):
        for e in range(2):
            near[e, p, :256] = kv[e, p]
            near[e, p, 256:] = n1[1 - e, p]
            near_t[e, p] = near[e, p].T
        shared[p, :128] = yr[p]
        shared[p, 128:256] = wr[p]
        shared[p, 256:384] = wy[p]
        for slot in range(8):
            start = 384 + ZR * slot
            shared[p, start : start + ZR] = xr[slot, p]
        shared_t[p] = shared[p].T
    lane = iota((TOK, 128), 1)
    steps = [(e, h) for e in range(2) for h in range(2)]
    masked = {}

    def scores(step):
        e, h = steps[step]
        mine = (lane >> 6) == h
        qh = jnp.where(mine, q[e], jnp.zeros((), BF16))
        ah = jnp.where(mine, ag[e], jnp.zeros((), BF16))
        masked[step] = (qh, ah)
        for ref, p, token in ((s_ref, 0, qh), (dw_ref, 1, ah * jnp.asarray(DH ** -0.5, BF16))):
            ref[step % 2, :384] = dot_nt(near[e, p], token)
            ref[step % 2, 384:] = dot_nt(shared[p], token)

    scores(0)
    for step, (e, h) in enumerate(steps):
        if step + 1 < len(steps):
            scores(step + 1)
        if h == 0:
            att_t, dq_t = [], []
        s, dw, b = s_ref.at[step % 2], dw_ref.at[step % 2], step % 2
        qh, ah = masked[step]
        top = jnp.max(s[...], axis=0, keepdims=True)
        un = jnp.exp2((s[...] - top) * (LOG2E * DH ** -0.5))
        s[...] = un
        inverse = 1.0 / jnp.sum(un, axis=0, keepdims=True)
        delta = jnp.sum(un * dw[...], axis=0, keepdims=True) * inverse
        prob = s[...] * inverse
        cols = slice(TOK * h, TOK * h + TOK)
        w_ref[e, :, cols] = prob.astype(BF16)
        ds_ref[e, :, cols] = (prob * (dw[...] - delta)).astype(BF16)
        head = slice(64 * h, 64 * h + 64)
        for out, p, ref in ((att_t, 1, w_ref), (dq_t, 0, ds_ref)):
            out.append(dot(near_t[e, p, head], ref[e, :384, cols]) + dot(shared_t[p, head], ref[e, 384:, cols]))
        if h == 0:
            continue
        dk = dot(ds_ref[e], jnp.concatenate([masked[step - 1][0], qh], axis=0))
        dv = dot(w_ref[e], jnp.concatenate([masked[step - 1][1], ah], axis=0))
        att_out[e] = jnp.concatenate(att_t, axis=0).T.astype(BF16)
        dq_out[e] = jnp.concatenate(dq_t, axis=0).T.astype(BF16)
        for p, grad in ((0, dk), (1, dv)):
            dkv_out[e, p] = grad[:256]
            dn1_out[1 - e, p] = grad[256:384]
            if e == 0:
                drem[p] = grad[384:]
            else:
                drem[p] = drem[p] + grad[384:]
    for p in range(2):
        rows = drem[p].astype(BF16)
        dy_out[p] = rows[:128]
        dwy_out[p] = rows[256:384]
        dw_out[p] = drem[p, 128:256]
        for slot in range(8):
            start = 384 + ZR * slot
            dx_out[slot, p] = rows[start : start + ZR]


def attention(pos, q, ag, kv, n1, yr, wr, wy, xr):
    def cut(*lead):
        return pl.BlockSpec(lead + (128,), lambda i, s: (0,) * len(lead) + (i,))

    outs = [
        ((2, TOK), BF16), ((2, TOK), BF16), ((2, 2, TOK), F32), ((2, 2, NR), F32), ((2, NR), BF16), ((2, NR), BF16),
        ((2, NR), F32), ((8, 2, ZR), BF16),
    ]
    n = 1152
    return call(
        attention_body,
        (H // 128,),
        [cut(2, TOK), cut(2, TOK), cut(2, 2, TOK), cut(2, 2, NR), cut(2, NR), cut(2, NR), cut(2, NR), cut(8, 2, ZR)],
        [(cut(*lead), (lead + (H,), kind)) for lead, kind in outs],
        [
            pltpu.VMEM((2, 2, 384, 128), BF16), pltpu.VMEM((2, 2, 128, 384), BF16),
            pltpu.VMEM((2, 768, 128), BF16), pltpu.VMEM((2, 128, 768), BF16), pltpu.VMEM((2, n, TOK), F32), pltpu.VMEM((2, n, TOK), F32),
            pltpu.VMEM((2, n, 2 * TOK), BF16), pltpu.VMEM((2, n, 2 * TOK), BF16), pltpu.VMEM((2, 768, 128), F32),
        ],
    )(pos, q, ag, kv, n1, yr, wr, wy, xr)


def output_body(pos, att_own, att_oth, w_own, w_oth, out):
    c = pos[0]
    out[...] = (dot(att_own[c], w_own[...]) + dot(att_oth[c], w_oth[...])).astype(BF16)


def output_side(pos, att_own, att_oth, w_out):
    row = lambda flip: pl.BlockSpec((H, D), lambda i, s: (s[0] ^ flip, 0))
    return call(
        output_body,
        (1,),
        [whole(2, TOK, H)] * 2 + [row(0), row(1)],
        [(whole(TOK, D), ((TOK, D), BF16))],
    )(pos, att_own, att_oth, w_out, w_out)[0]


def terms_body(pos, att_own, att_oth, ct_own, ct_oth, dq, xt, p_own, p_oth, *rest):
    c, x = pos[0], pos[2] >> 1
    slots = rest[-1]
    total = dot(xt[0], dq[0]) + dot(xt[1], dq[1])
    slots[:, :, 0] = total.astype(BF16).reshape(XN, YN, 96, H)
    total = None
    for e, ct in ((c, ct_own), (1 - c, ct_oth)):
        att_t = (dot_nt(p_own[...], att_own[e]) + dot_nt(p_oth[...], att_oth[e])).astype(BF16)
        term = dot(att_t, ct[...])
        total = term if total is None else total + term
    slots[:, :, 1] = total.astype(BF16).reshape(XN, YN, 96, H)
    for far in range(XN):
        rest[far][...] = slots[x ^ far]


def output_terms(pos, att_own, att_oth, ct_own, ct_oth, dq, xt, perm):
    col = lambda flip, rows: pl.BlockSpec((rows, H), lambda i, s: (0, s[0] ^ flip))
    slot = (YN, 2, 96, H)
    return call(
        terms_body,
        (1,),
        [whole(2, TOK, H)] * 2 + [col(0, TOK)] * 2 + [whole(2, TOK, H), whole(2, D, TOK), col(0, D), col(1, D)],
        [(whole(*slot), (slot, BF16))] * XN,
        [pltpu.VMEM((XN,) + slot, BF16)],
    )(pos, att_own, att_oth, ct_own, ct_oth, dq, xt, perm, perm)


def x_sum_body(pos, t0, t1, t2, t3, *rest):
    y, dp = pos[2] & 1, pos[3]
    slots = rest[-1]
    total = (t0[...].astype(F32) + t1[...].astype(F32)) + (t2[...].astype(F32) + t3[...].astype(F32))
    slots[...] = total.astype(BF16)
    for far in range(4):
        rest[far][...] = slots[y ^ (far >> 1), dp ^ (far & 1)]


def x_sum(pos, *terms):
    shape = (YN, 2, 96, H)
    return call(
        x_sum_body,
        (1,),
        [whole(*shape)] * 4,
        [(whole(96, H), ((96, H), BF16))] * 4,
        [pltpu.VMEM(shape, BF16)],
    )(pos, *terms)


def back_body(pos, xr, dw, dwy, out, *tiers):
    hot = (iota((128, ZR), 0) == z_source(pos[1], 1, (128, ZR))).astype(BF16)
    for p in range(2):
        total = xr[0, p].astype(F32)
        for slot in range(1, 8):
            total = total + xr[slot, p].astype(F32)
        out[:, p] = dot(hot, total.astype(BF16)).astype(BF16).reshape(8, 16, H)
        start = 0
        for tier in tiers:
            rows = tier.shape[1]
            total = dw[p, start : start + rows] + dwy[p, start : start + rows].astype(F32)
            tier[p] = total.astype(BF16)
            start += rows


def back_slots(pos, xr, dw, dwy):
    outs = [(ZN, 2, 16, H), (2, 64, H), (2, 32, H), (2, 32, H)]
    return call(
        back_body,
        (1,),
        [whole(8, 2, ZR, H), whole(2, NR, H), whole(2, NR, H)],
        [(whole(*shape), (shape, BF16)) for shape in outs],
    )(pos, xr, dw, dwy)


def leaf_body(pos, zr, dkv, dn1, dy, g3, g4_a, g4_b, dq, xt, own_out, oth_out, grad_out):
    def split(grad):
        high = grad.astype(BF16)
        return [high, (grad - high.astype(F32)).astype(BF16)]

    def hot(hit, scale):
        return jnp.where(hit, scale, 0.0).astype(BF16)

    def wide(ref):
        return jnp.concatenate([ref[0], ref[1]], axis=1)

    zs = jnp.concatenate([zr[:, p].reshape(128, H) for p in range(2)], axis=1)
    ws = jnp.concatenate([wide(g3), wide(g4_a), wide(g4_b)], axis=0)
    ys = wide(dy)
    sides = ((pos[0], own_out), (1 - pos[0], oth_out))
    for e, pg_out in sides:
        t, k = iota((TOK, 128), 0), iota((TOK, 128), 1)
        far, row, chip = (k >> 4) ^ pos[1], k & 15, t + TOK * e
        first = hot(t >> 1 == k, 1.0)
        third = hot(chip >> 3 == k, 0.5)
        odd = hot((far == 1) & (row == chip >> 5), 0.25) + hot((far >= 4) & (row == chip >> 7), 0.125)
        second = hot(chip >> 2 == k, 0.5)
        fourth = hot((k >= 64) & (chip >> 4 == k & 31), 0.25)
        even = hot((far >> 1 == 1) & (row == chip >> 6), 0.125)
        up = dot(jnp.concatenate([first, first, third, odd], axis=1), jnp.concatenate(split(wide(dn1.at[e])) + [ws, zs], axis=0))
        up = up * HALF_ROOT + dot(jnp.concatenate([second, fourth, even], axis=1), jnp.concatenate([ys, ws, zs], axis=0))
        for p in range(2):
            pg_out[:, H * (1 + p) : H * (2 + p)] = (dkv[e, p] + up[:, H * p : H * p + H]).astype(BF16)
        pg_out[:, :H] = dq[e]
    for p in range(2):
        cols = slice(H * (1 + p), H * (2 + p))
        first, second = (dot(xt[e], pg_out[:, cols]) for e, pg_out in sides)
        total = first + second
        grad_out[:, p] = total.astype(BF16).reshape(8, 96, H)


def leaf_grads(pos, zr, dkv, dn1, dy, g3, g4_a, g4_b, dq, xt):
    return call(
        leaf_body,
        (1,),
        [
            whole(ZN, 2, 16, H), whole(2, 2, TOK, H), whole(2, 2, NR, H), whole(2, NR, H), whole(2, 64, H), whole(2, 32, H),
            whole(2, 32, H), whole(2, TOK, H), whole(2, D, TOK),
        ],
        [(whole(TOK, 3 * H), ((TOK, 3 * H), BF16))] * 2 + [(whole(8, 2, 96, H), ((8, 2, 96, H), BF16))],
    )(pos, zr, dkv, dn1, dy, g3, g4_a, g4_b, dq, xt)


def input_body(pos, pg_own, pg_oth, *rest):
    out = rest[-1]
    total = None
    for part in range(3):
        for pg, w in ((pg_own, rest[part]), (pg_oth, rest[3 + part])):
            term = dot_nt(pg[:, H * part : H * part + H], w[...])
            total = term if total is None else total + term
    out[...] = total.astype(BF16)


def input_side(pos, pg_own, pg_oth, w_qkv):
    col = lambda part, flip: pl.BlockSpec((D, H), lambda i, s: (0, 2 * part + (s[0] ^ flip)))
    return call(
        input_body,
        (1,),
        [whole(TOK, 3 * H)] * 2 + [col(part, flip) for flip in (0, 1) for part in range(3)],
        [(whole(TOK, D), ((TOK, D), BF16))],
    )(pos, pg_own, pg_oth, *[w_qkv] * 6)[0]


def total_of(refs):
    total = refs[0].astype(F32)
    for ref in refs[1:]:
        total = total + ref.astype(F32)
    return total


def middle_body(pos, f0, f1, f2, f3, second, out):
    first = total_of([f0[...], f1[...], f2[...], f3[...]]).astype(BF16)
    i, k = iota((256, 96), 0), iota((256, 96), 1)
    row, half = i & 7, (i >> 3) & 1
    hit = (k == 6 * (i >> 4) + row) & (row < 6)
    rows = dot((hit & (half == 0)).astype(BF16), first)
    rows = rows + dot((hit & (half == 1)).astype(BF16), total_of([second[slot] for slot in range(16)]).astype(BF16))
    rows = rows.astype(BF16).reshape(ZN, 2, 16, H)
    for core in range(2):
        out[:, core ^ pos[0]] = rows[:, core]


def middle_sum(pos, firsts, second):
    shape = (ZN, 2, 16, H)
    return call(
        middle_body, (1,), [whole(96, H)] * 4 + [whole(16, 96, H)], [(whole(*shape), (shape, BF16))]
    )(pos, *firsts, second)[0]


def last_body(pos, own, from_dp, from_core, from_both, qkv_out, out_out, parts):
    core, dp = pos[0], pos[3]
    parts[core, dp] = own[...]
    parts[core, 1 - dp] = from_dp[...]
    parts[1 - core, dp] = from_core[...]
    parts[1 - core, 1 - dp] = from_both[...]
    for core in range(2):
        low, high = parts[core, 0].astype(F32), parts[core, 1].astype(F32)
        cols = lambda part: slice(D * part + H * core, D * part + H * core + H)
        qkv_out[:, cols(0)] = low[:6]
        qkv_out[:, cols(1)] = low[8:14]
        qkv_out[:, cols(2)] = high[8:14]
        out_out[:, cols(0)] = high[:6]


def last_rows(pos, *parts):
    return call(
        last_body,
        (1,),
        [whole(16, H)] * 4,
        [(whole(6, 3 * D), ((6, 3 * D), F32)), (whole(6, D), ((6, D), F32))],
        [pltpu.VMEM((2, 2, 16, H), BF16)],
    )(pos, *parts)


def swap(value, axis):
    return lax.ppermute(value, axis, [(0, 1), (1, 0)])


def along(value, axes, far, count=4):
    return lax.ppermute(value, axes, [(i, i ^ far) for i in range(count)])


def row_order():
    f = np.arange(D)
    source = 96 * (f // 12 % 8) + 12 * (f // 96) + f % 12
    return jnp.asarray(source[:, None] == f[None, :], BF16)


def shards(x_tokens, cotangent, w_qkv, w_out):
    x_own, ct_own = x_tokens[0], cotangent[0]
    c, z, dp = lax.axis_index("c"), lax.axis_index("z"), lax.axis_index("dp")
    j = 2 * lax.axis_index("x") + lax.axis_index("y")
    pos = jnp.stack([c, z, j, dp]).astype(jnp.int32)
    x_oth, ct_oth = swap(x_own, "c"), swap(ct_own, "c")
    perm = row_order()

    kv, n1, n2, n3, n4, zs = tree(pos, x_own, x_oth, w_qkv)
    yr = swap(n2, "y")
    wr = jnp.concatenate([along(n3, "x", 1), along(n4, "x", 2), along(n4, "x", 3)], axis=1)
    zr = lax.all_to_all(zs, "z", 0, 0)
    zr, yr, wr, ct_oth = lax.optimization_barrier((zr, yr, wr, ct_oth))
    wy = swap(wr, "y")
    xs, wy = lax.optimization_barrier((plane_slots(pos, zr), wy))
    xr = lax.all_to_all(xs, ("x", "y"), 0, 0)
    q, ag, xt = project(pos, x_own, x_oth, ct_own, ct_oth, w_qkv, w_out, perm)
    att, dq, dkv, dn1, dy, dwy, dw, dx = attention(pos, q, ag, kv, n1, yr, wr, wy, xr)

    dx_r = lax.all_to_all(dx, ("x", "y"), 0, 0)
    att_oth = swap(att, "c")
    dwy = swap(dwy, "y")
    first, *firsts = output_terms(pos, att, att_oth, ct_own, ct_oth, dq, xt, perm)
    firsts = [along(firsts[far - 1], "x", far) for far in (1, 2, 3)]
    dx_r, first, firsts[0], dwy = lax.optimization_barrier((dx_r, first, firsts[0], dwy))
    dz, g3, g4_a, g4_b = back_slots(pos, dx_r, dw, dwy)
    dz_r = lax.all_to_all(dz, "z", 0, 0)
    g3, g4_a, g4_b, firsts = lax.optimization_barrier((g3, g4_a, g4_b, firsts))
    g3, g4_a, g4_b = along(g3, "x", 1), along(g4_a, "x", 2), along(g4_b, "x", 3)
    pg_own, pg_oth, terms = leaf_grads(pos, dz_r, dkv, dn1, swap(dy, "y"), g3, g4_a, g4_b, dq, xt)
    terms, first, firsts = lax.optimization_barrier((terms, first, firsts))
    firsts = x_sum(pos, first, *firsts)
    firsts = list(firsts[:1]) + [along(firsts[far], ("y", "dp"), far) for far in (1, 2, 3)]
    terms = lax.all_to_all(terms.reshape(16, 96, H), ("x", "y", "dp"), 0, 0)
    input_grad = input_side(pos, pg_own, swap(pg_oth, "c"), w_qkv)
    terms, input_grad = lax.optimization_barrier((terms, input_grad))
    terms, att, att_oth = lax.optimization_barrier((middle_sum(pos, firsts, terms), att, att_oth))
    terms = lax.all_to_all(terms, "z", 0, 0)
    terms, layer_out = lax.optimization_barrier((terms, output_side(pos, att, att_oth, w_out)))
    own, oth = (jnp.sum(terms[:, core].astype(F32), axis=0).astype(BF16) for core in range(2))
    pair = ("c", "dp")
    qkv_grad, out_grad = last_rows(pos, own, along(own, pair, 1), along(oth, pair, 2), along(oth, pair, 3))
    return (layer_out[None], input_grad[None], qkv_grad, out_grad)


def solution(mesh):
    split = Mesh(mesh.devices.reshape(ZN, XN, YN, 2, 2), ("z", "x", "y", "c", "dp"))
    seq = ("z", "x", "y", "c")
    return jax.shard_map(
        shards,
        mesh=split,
        in_specs=(P("dp", seq, None), P("dp", seq, None), P(), P()),
        out_specs=(P("dp", seq, None), P("dp", seq, None), P(seq, None), P(seq, None)),
        check_vma=False,
    )
```

```python
import jax
import jax.numpy as jnp
import numpy as np
from jax import lax
from jax.experimental import pallas as pl
from jax.experimental.pallas import tpu as pltpu
from jax.sharding import Mesh, PartitionSpec as P

D = 768
H = 384
TOK = 256
NR = 128
DH = 64
ZN, XN, YN = 8, 4, 2
ZR = 48
HALF_ROOT = 0.7071067811865476
LOG2E = 1.4426950408889634
VMEM = 56 * 1024 * 1024
F32 = jnp.float32
BF16 = jnp.bfloat16


def dot(a, b):
    return lax.dot_general(a, b, (((1,), (0,)), ((), ())), preferred_element_type=F32)


def dot_nt(a, b):
    return lax.dot_general(a, b, (((1,), (1,)), ((), ())), preferred_element_type=F32)


def dot_tn(a, b):
    return lax.dot_general(a, b, (((0,), (0,)), ((), ())), preferred_element_type=F32)


def iota(shape, axis):
    return lax.broadcasted_iota(jnp.int32, shape, axis)


def pair_matrix(rows, cols, valid):
    r, k = iota((rows, cols), 0), iota((rows, cols), 1)
    return (((k >> 1) == r) & (r < valid)).astype(BF16)


def coarsen(node, rows=None, valid=None):
    rows = node.shape[0] // 2 if rows is None else rows
    valid = rows if valid is None else valid
    return (dot(pair_matrix(rows, node.shape[0], valid), node) * HALF_ROOT).astype(BF16)


def whole(*shape):
    return pl.BlockSpec(shape, lambda *_: (0,) * len(shape))


def call(body, grid, ins, outs, scratch=()):
    return pl.pallas_call(
        body,
        grid_spec=pltpu.PrefetchScalarGridSpec(
            num_scalar_prefetch=1,
            grid=grid,
            in_specs=ins,
            out_specs=[s for s, _ in outs],
            scratch_shapes=list(scratch),
        ),
        out_shape=[jax.ShapeDtypeStruct(shape, kind) for _, (shape, kind) in outs],
        compiler_params=pltpu.CompilerParams(vmem_limit_bytes=VMEM),
    )


def tree_body(pos, x_own, x_oth, wk, wv, kv_out, n1_out, n2_out, n3_out, n4_out, zs_out, rows, pad):
    c, z = pos[0], pos[1]
    for e, x in ((c, x_own), (1 - c, x_oth)):
        for p, w in ((0, wk), (1, wv)):
            part = dot(x[...], w[...]).astype(BF16)
            kv_out[e, p] = part
            for n in range(3):
                rows[e, 3 * p + n] = part[:, 128 * n : 128 * n + 128].astype(F32)

    def coarser(ref, n):
        node = ((ref[pl.ds(0, n, stride=2), :] + ref[pl.ds(1, n, stride=2), :]) * HALF_ROOT).astype(BF16)
        return node, node.astype(F32)

    for p in range(2):
        for n in range(3):
            cols, block = slice(128 * n, 128 * n + 128), 3 * p + n
            top = pad.at[block]
            for e in range(2):
                ref = rows.at[e, block]
                n1_out[e, p, :, cols], wide = coarser(ref, NR)
                ref[:NR] = wide
                n2_out[p, 64 * e : 64 * e + 64, cols], wide = coarser(ref, 64)
                top[64 * e : 64 * e + 64] = wide
            n3_out[p, :, cols], wide = coarser(top, 64)
            top[:64] = wide
            n4_out[p, :, cols], wide = coarser(top, 32)
            top[:32] = wide
            n5, wide = coarser(top, 16)
            top[:16] = wide
            top[16:48] = jnp.zeros((32, 128), F32)
            top[16:24] = coarser(top, 8)[1]
            top[32:36] = coarser(top.at[pl.ds(16, 8)], 4)[1]
            n6, n7 = top[16:32].astype(BF16), top[32:48].astype(BF16)
            zs_out[z, p, :, cols] = jnp.zeros_like(n5)
            zs_out[z ^ 1, p, :, cols] = n5
            for far in (2, 3):
                zs_out[z ^ far, p, :, cols] = n6
            for far in (4, 5, 6, 7):
                zs_out[z ^ far, p, :, cols] = n7


def tree(pos, x_own, x_oth, w_qkv):
    col = lambda part: pl.BlockSpec((D, H), lambda i, s: (0, 2 * part + s[0]))
    outs = [(2, 2, TOK, H), (2, 2, NR, H), (2, NR, H), (2, 64, H), (2, 32, H), (ZN, 2, 16, H)]
    return call(
        tree_body,
        (1,),
        [whole(TOK, D)] * 2 + [col(1), col(2)],
        [(whole(*shape), (shape, BF16)) for shape in outs],
        [pltpu.VMEM((2, 6, TOK, 128), F32), pltpu.VMEM((6, NR, 128), F32)],
    )(pos, x_own, x_oth, w_qkv, w_qkv)


def project_body(pos, x_own, x_oth, ct_own, ct_oth, wq, wo, perm, q_out, ag_out, xt_out):
    c = pos[0]
    for e, x, ct in ((c, x_own, ct_own), (1 - c, x_oth, ct_oth)):
        q_out[e] = dot(x[...], wq[...]).astype(BF16)
        ag_out[e] = dot_nt(ct[...], wo[...]).astype(BF16)
        xt_out[e] = dot_nt(perm[...], x[...]).astype(BF16)


def project(pos, x_own, x_oth, ct_own, ct_oth, w_qkv, w_out, perm):
    outs = [(2, TOK, H), (2, TOK, H), (2, D, TOK)]
    return call(
        project_body,
        (1,),
        [whole(TOK, D)] * 4
        + [pl.BlockSpec((D, H), lambda i, s: (0, s[0])), pl.BlockSpec((H, D), lambda i, s: (s[0], 0)), whole(D, D)],
        [(whole(*shape), (shape, BF16)) for shape in outs],
    )(pos, x_own, x_oth, ct_own, ct_oth, w_qkv, w_out, perm)


def z_source(z, rows_axis, shape):
    i = iota(shape, rows_axis)
    near = 16 * (z ^ 1) + i
    mid = 16 * (z ^ (2 + ((i - 16) >> 3))) + ((i - 16) & 7)
    far = 16 * (z ^ (4 + ((i - 32) >> 2))) + ((i - 32) & 3)
    return jnp.where(i < 16, near, jnp.where(i < 32, mid, far))


def plane_body(pos, zr, out):
    hot = (iota((ZR, 128), 1) == z_source(pos[1], 0, (ZR, 128))).astype(BF16)
    both = jnp.concatenate([zr[:, p].reshape(128, H) for p in range(2)], axis=1)
    rows = dot(hot, both).astype(BF16)
    for slot in range(8):
        for p in range(2):
            out[slot, p] = rows[:, H * p : H * p + H]


def plane_slots(pos, zr):
    return call(
        plane_body,
        (1,),
        [whole(ZN, 2, 16, H)],
        [(whole(8, 2, ZR, H), ((8, 2, ZR, H), BF16))],
    )(pos, zr)[0]


def attention_body(pos, q, ag, kv, n1, yr, wr, wy, xr, att_out, dq_out, dkv_out, dn1_out, dy_out, dwy_out, dw_out, dx_out, near, near_t, shared, shared_t, s_ref, dw_ref, w_ref, ds_ref, drem):
    for p in range(2):
        for e in range(2):
            near[e, p, :256] = kv[e, p]
            near[e, p, 256:] = n1[1 - e, p]
            near_t[e, p] = near[e, p].T
        shared[p, :128] = yr[p]
        shared[p, 128:256] = wr[p]
        shared[p, 256:384] = wy[p]
        for slot in range(8):
            start = 384 + ZR * slot
            shared[p, start : start + ZR] = xr[slot, p]
        shared_t[p] = shared[p].T
    lane = iota((TOK, 128), 1)
    steps = [(e, h) for e in range(2) for h in range(2)]
    masked = {}

    def scores(step):
        e, h = steps[step]
        mine = (lane >> 6) == h
        qh = jnp.where(mine, q[e], jnp.zeros((), BF16))
        ah = jnp.where(mine, ag[e], jnp.zeros((), BF16))
        masked[step] = (qh, ah)
        for ref, p, token in ((s_ref, 0, qh), (dw_ref, 1, ah * jnp.asarray(DH ** -0.5, BF16))):
            ref[step % 2, :384] = dot_nt(near[e, p], token)
            ref[step % 2, 384:] = dot_nt(shared[p], token)

    scores(0)
    for step, (e, h) in enumerate(steps):
        if step + 1 < len(steps):
            scores(step + 1)
        if h == 0:
            att_t, dq_t = [], []
        s, dw, b = s_ref.at[step % 2], dw_ref.at[step % 2], step % 2
        qh, ah = masked[step]
        top = jnp.max(s[...], axis=0, keepdims=True)
        un = jnp.exp2((s[...] - top) * (LOG2E * DH ** -0.5))
        s[...] = un
        inverse = 1.0 / jnp.sum(un, axis=0, keepdims=True)
        delta = jnp.sum(un * dw[...], axis=0, keepdims=True) * inverse
        prob = s[...] * inverse
        cols = slice(TOK * h, TOK * h + TOK)
        w_ref[e, :, cols] = prob.astype(BF16)
        ds_ref[e, :, cols] = (prob * (dw[...] - delta)).astype(BF16)
        head = slice(64 * h, 64 * h + 64)
        for out, p, ref in ((att_t, 1, w_ref), (dq_t, 0, ds_ref)):
            out.append(dot(near_t[e, p, head], ref[e, :384, cols]) + dot(shared_t[p, head], ref[e, 384:, cols]))
        if h == 0:
            continue
        dk = dot(ds_ref[e], jnp.concatenate([masked[step - 1][0], qh], axis=0))
        dv = dot(w_ref[e], jnp.concatenate([masked[step - 1][1], ah], axis=0))
        att_out[e] = jnp.concatenate(att_t, axis=0).T.astype(BF16)
        dq_out[e] = jnp.concatenate(dq_t, axis=0).T.astype(BF16)
        for p, grad in ((0, dk), (1, dv)):
            dkv_out[e, p] = grad[:256]
            dn1_out[1 - e, p] = grad[256:384]
            if e == 0:
                drem[p] = grad[384:]
            else:
                drem[p] = drem[p] + grad[384:]
    for p in range(2):
        rows = drem[p].astype(BF16)
        dy_out[p] = rows[:128]
        dwy_out[p] = rows[256:384]
        dw_out[p] = drem[p, 128:256]
        for slot in range(8):
            start = 384 + ZR * slot
            dx_out[slot, p] = rows[start : start + ZR]


def attention(pos, q, ag, kv, n1, yr, wr, wy, xr):
    def cut(*lead):
        return pl.BlockSpec(lead + (128,), lambda i, s: (0,) * len(lead) + (i,))

    outs = [
        ((2, TOK), BF16), ((2, TOK), BF16), ((2, 2, TOK), F32), ((2, 2, NR), F32), ((2, NR), BF16), ((2, NR), BF16),
        ((2, NR), F32), ((8, 2, ZR), BF16),
    ]
    n = 1152
    return call(
        attention_body,
        (H // 128,),
        [cut(2, TOK), cut(2, TOK), cut(2, 2, TOK), cut(2, 2, NR), cut(2, NR), cut(2, NR), cut(2, NR), cut(8, 2, ZR)],
        [(cut(*lead), (lead + (H,), kind)) for lead, kind in outs],
        [
            pltpu.VMEM((2, 2, 384, 128), BF16), pltpu.VMEM((2, 2, 128, 384), BF16),
            pltpu.VMEM((2, 768, 128), BF16), pltpu.VMEM((2, 128, 768), BF16), pltpu.VMEM((2, n, TOK), F32), pltpu.VMEM((2, n, TOK), F32),
            pltpu.VMEM((2, n, 2 * TOK), BF16), pltpu.VMEM((2, n, 2 * TOK), BF16), pltpu.VMEM((2, 768, 128), F32),
        ],
    )(pos, q, ag, kv, n1, yr, wr, wy, xr)


def output_body(pos, att_own, att_oth, w_own, w_oth, out):
    c = pos[0]
    out[...] = (dot(att_own[c], w_own[...]) + dot(att_oth[c], w_oth[...])).astype(BF16)


def output_side(pos, att_own, att_oth, w_out):
    row = lambda flip: pl.BlockSpec((H, D), lambda i, s: (s[0] ^ flip, 0))
    return call(
        output_body,
        (1,),
        [whole(2, TOK, H)] * 2 + [row(0), row(1)],
        [(whole(TOK, D), ((TOK, D), BF16))],
    )(pos, att_own, att_oth, w_out, w_out)[0]


def terms_body(pos, att_own, att_oth, ct_own, ct_oth, dq, xt, p_own, p_oth, *rest):
    c, x = pos[0], pos[2] >> 1
    slots = rest[-1]
    total = dot(xt[0], dq[0]) + dot(xt[1], dq[1])
    slots[:, :, 0] = total.astype(BF16).reshape(XN, YN, 96, H)
    total = None
    for e, ct in ((c, ct_own), (1 - c, ct_oth)):
        att_t = (dot_nt(p_own[...], att_own[e]) + dot_nt(p_oth[...], att_oth[e])).astype(BF16)
        term = dot(att_t, ct[...])
        total = term if total is None else total + term
    slots[:, :, 1] = total.astype(BF16).reshape(XN, YN, 96, H)
    for far in range(XN):
        rest[far][...] = slots[x ^ far]


def output_terms(pos, att_own, att_oth, ct_own, ct_oth, dq, xt, perm):
    col = lambda flip, rows: pl.BlockSpec((rows, H), lambda i, s: (0, s[0] ^ flip))
    slot = (YN, 2, 96, H)
    return call(
        terms_body,
        (1,),
        [whole(2, TOK, H)] * 2 + [col(0, TOK)] * 2 + [whole(2, TOK, H), whole(2, D, TOK), col(0, D), col(1, D)],
        [(whole(*slot), (slot, BF16))] * XN,
        [pltpu.VMEM((XN,) + slot, BF16)],
    )(pos, att_own, att_oth, ct_own, ct_oth, dq, xt, perm, perm)


def x_sum_body(pos, t0, t1, t2, t3, *rest):
    y, dp = pos[2] & 1, pos[3]
    slots = rest[-1]
    total = (t0[...].astype(F32) + t1[...].astype(F32)) + (t2[...].astype(F32) + t3[...].astype(F32))
    slots[...] = total.astype(BF16)
    for far in range(4):
        rest[far][...] = slots[y ^ (far >> 1), dp ^ (far & 1)]


def x_sum(pos, *terms):
    shape = (YN, 2, 96, H)
    return call(
        x_sum_body,
        (1,),
        [whole(*shape)] * 4,
        [(whole(96, H), ((96, H), BF16))] * 4,
        [pltpu.VMEM(shape, BF16)],
    )(pos, *terms)


def back_body(pos, xr, dw, dwy, out, *tiers):
    hot = (iota((128, ZR), 0) == z_source(pos[1], 1, (128, ZR))).astype(BF16)
    for p in range(2):
        total = xr[0, p].astype(F32)
        for slot in range(1, 8):
            total = total + xr[slot, p].astype(F32)
        out[:, p] = dot(hot, total.astype(BF16)).astype(BF16).reshape(8, 16, H)
        start = 0
        for tier in tiers:
            rows = tier.shape[1]
            total = dw[p, start : start + rows] + dwy[p, start : start + rows].astype(F32)
            tier[p] = total.astype(BF16)
            start += rows


def back_slots(pos, xr, dw, dwy):
    outs = [(ZN, 2, 16, H), (2, 64, H), (2, 32, H), (2, 32, H)]
    return call(
        back_body,
        (1,),
        [whole(8, 2, ZR, H), whole(2, NR, H), whole(2, NR, H)],
        [(whole(*shape), (shape, BF16)) for shape in outs],
    )(pos, xr, dw, dwy)


def leaf_body(pos, zr, dkv, dn1, dy, g3, g4_a, g4_b, dq, xt, own_out, oth_out, grad_out):
    def split(grad):
        high = grad.astype(BF16)
        return [high, (grad - high.astype(F32)).astype(BF16)]

    def hot(hit, scale):
        return jnp.where(hit, scale, 0.0).astype(BF16)

    def wide(ref):
        return jnp.concatenate([ref[0], ref[1]], axis=1)

    zs = jnp.concatenate([zr[:, p].reshape(128, H) for p in range(2)], axis=1)
    ws = jnp.concatenate([wide(g3), wide(g4_a), wide(g4_b)], axis=0)
    ys = wide(dy)
    sides = ((pos[0], own_out), (1 - pos[0], oth_out))
    for e, pg_out in sides:
        t, k = iota((TOK, 128), 0), iota((TOK, 128), 1)
        far, row, chip = (k >> 4) ^ pos[1], k & 15, t + TOK * e
        first = hot(t >> 1 == k, 1.0)
        third = hot(chip >> 3 == k, 0.5)
        odd = hot((far == 1) & (row == chip >> 5), 0.25) + hot((far >= 4) & (row == chip >> 7), 0.125)
        second = hot(chip >> 2 == k, 0.5)
        fourth = hot((k >= 64) & (chip >> 4 == k & 31), 0.25)
        even = hot((far >> 1 == 1) & (row == chip >> 6), 0.125)
        up = dot(jnp.concatenate([first, first, third, odd], axis=1), jnp.concatenate(split(wide(dn1.at[e])) + [ws, zs], axis=0))
        up = up * HALF_ROOT + dot(jnp.concatenate([second, fourth, even], axis=1), jnp.concatenate([ys, ws, zs], axis=0))
        for p in range(2):
            pg_out[:, H * (1 + p) : H * (2 + p)] = (dkv[e, p] + up[:, H * p : H * p + H]).astype(BF16)
        pg_out[:, :H] = dq[e]
    for p in range(2):
        cols = slice(H * (1 + p), H * (2 + p))
        first, second = (dot(xt[e], pg_out[:, cols]) for e, pg_out in sides)
        total = first + second
        grad_out[:, p] = total.astype(BF16).reshape(8, 96, H)


def leaf_grads(pos, zr, dkv, dn1, dy, g3, g4_a, g4_b, dq, xt):
    return call(
        leaf_body,
        (1,),
        [
            whole(ZN, 2, 16, H), whole(2, 2, TOK, H), whole(2, 2, NR, H), whole(2, NR, H), whole(2, 64, H), whole(2, 32, H),
            whole(2, 32, H), whole(2, TOK, H), whole(2, D, TOK),
        ],
        [(whole(TOK, 3 * H), ((TOK, 3 * H), BF16))] * 2 + [(whole(8, 2, 96, H), ((8, 2, 96, H), BF16))],
    )(pos, zr, dkv, dn1, dy, g3, g4_a, g4_b, dq, xt)


def input_body(pos, pg_own, pg_oth, *rest):
    out = rest[-1]
    total = None
    for part in range(3):
        for pg, w in ((pg_own, rest[part]), (pg_oth, rest[3 + part])):
            term = dot_nt(pg[:, H * part : H * part + H], w[...])
            total = term if total is None else total + term
    out[...] = total.astype(BF16)


def input_side(pos, pg_own, pg_oth, w_qkv):
    col = lambda part, flip: pl.BlockSpec((D, H), lambda i, s: (0, 2 * part + (s[0] ^ flip)))
    return call(
        input_body,
        (1,),
        [whole(TOK, 3 * H)] * 2 + [col(part, flip) for flip in (0, 1) for part in range(3)],
        [(whole(TOK, D), ((TOK, D), BF16))],
    )(pos, pg_own, pg_oth, *[w_qkv] * 6)[0]


def total_of(refs):
    total = refs[0].astype(F32)
    for ref in refs[1:]:
        total = total + ref.astype(F32)
    return total


def middle_body(pos, f0, f1, f2, f3, second, out):
    first = total_of([f0[...], f1[...], f2[...], f3[...]]).astype(BF16)
    i, k = iota((256, 96), 0), iota((256, 96), 1)
    row, half = i & 7, (i >> 3) & 1
    hit = (k == 6 * (i >> 4) + row) & (row < 6)
    rows = dot((hit & (half == 0)).astype(BF16), first)
    rows = rows + dot((hit & (half == 1)).astype(BF16), total_of([second[slot] for slot in range(16)]).astype(BF16))
    rows = rows.astype(BF16).reshape(ZN, 2, 16, H)
    for core in range(2):
        out[:, core ^ pos[0]] = rows[:, core]


def middle_sum(pos, firsts, second):
    shape = (ZN, 2, 16, H)
    return call(
        middle_body, (1,), [whole(96, H)] * 4 + [whole(16, 96, H)], [(whole(*shape), (shape, BF16))]
    )(pos, *firsts, second)[0]


def last_body(pos, own, from_dp, from_core, from_both, qkv_out, out_out, parts):
    core, dp = pos[0], pos[3]
    parts[core, dp] = own[...]
    parts[core, 1 - dp] = from_dp[...]
    parts[1 - core, dp] = from_core[...]
    parts[1 - core, 1 - dp] = from_both[...]
    for core in range(2):
        low, high = parts[core, 0].astype(F32), parts[core, 1].astype(F32)
        cols = lambda part: slice(D * part + H * core, D * part + H * core + H)
        qkv_out[:, cols(0)] = low[:6]
        qkv_out[:, cols(1)] = low[8:14]
        qkv_out[:, cols(2)] = high[8:14]
        out_out[:, cols(0)] = high[:6]


def last_rows(pos, *parts):
    return call(
        last_body,
        (1,),
        [whole(16, H)] * 4,
        [(whole(6, 3 * D), ((6, 3 * D), F32)), (whole(6, D), ((6, D), F32))],
        [pltpu.VMEM((2, 2, 16, H), BF16)],
    )(pos, *parts)


def swap(value, axis):
    return lax.ppermute(value, axis, [(0, 1), (1, 0)])


def along(value, axes, far, count=4):
    return lax.ppermute(value, axes, [(i, i ^ far) for i in range(count)])


def row_order():
    f = np.arange(D)
    source = 96 * (f // 12 % 8) + 12 * (f // 96) + f % 12
    return jnp.asarray(source[:, None] == f[None, :], BF16)


def shards(x_tokens, cotangent, w_qkv, w_out):
    x_own, ct_own = x_tokens[0], cotangent[0]
    c, z, dp = lax.axis_index("c"), lax.axis_index("z"), lax.axis_index("dp")
    j = 2 * lax.axis_index("x") + lax.axis_index("y")
    pos = jnp.stack([c, z, j, dp]).astype(jnp.int32)
    x_oth, ct_oth = swap(x_own, "c"), swap(ct_own, "c")
    perm = row_order()

    kv, n1, n2, n3, n4, zs = tree(pos, x_own, x_oth, w_qkv)
    yr = swap(n2, "y")
    wr = jnp.concatenate([along(n3, "x", 1), along(n4, "x", 2), along(n4, "x", 3)], axis=1)
    zr = lax.all_to_all(zs, "z", 0, 0)
    zr, yr, wr, ct_oth = lax.optimization_barrier((zr, yr, wr, ct_oth))
    wy = swap(wr, "y")
    xs, wy = lax.optimization_barrier((plane_slots(pos, zr), wy))
    xr = lax.all_to_all(xs, ("x", "y"), 0, 0)
    q, ag, xt = project(pos, x_own, x_oth, ct_own, ct_oth, w_qkv, w_out, perm)
    att, dq, dkv, dn1, dy, dwy, dw, dx = attention(pos, q, ag, kv, n1, yr, wr, wy, xr)

    dx_r = lax.all_to_all(dx, ("x", "y"), 0, 0)
    att_oth = swap(att, "c")
    dwy = swap(dwy, "y")
    first, *firsts = output_terms(pos, att, att_oth, ct_own, ct_oth, dq, xt, perm)
    firsts = [along(firsts[far - 1], "x", far) for far in (1, 2, 3)]
    dx_r, first, dwy = lax.optimization_barrier((dx_r, first, dwy))
    dz, g3, g4_a, g4_b = back_slots(pos, dx_r, dw, dwy)
    dz_r = lax.all_to_all(dz, "z", 0, 0)
    g3, g4_a, g4_b, firsts = lax.optimization_barrier((g3, g4_a, g4_b, firsts))
    g3, g4_a, g4_b = along(g3, "x", 1), along(g4_a, "x", 2), along(g4_b, "x", 3)
    pg_own, pg_oth, terms = leaf_grads(pos, dz_r, dkv, dn1, swap(dy, "y"), g3, g4_a, g4_b, dq, xt)
    terms, first, firsts = lax.optimization_barrier((terms, first, firsts))
    firsts = x_sum(pos, first, *firsts)
    firsts = list(firsts[:1]) + [along(firsts[far], ("y", "dp"), far) for far in (1, 2, 3)]
    terms = lax.all_to_all(terms.reshape(16, 96, H), ("x", "y", "dp"), 0, 0)
    input_grad = input_side(pos, pg_own, swap(pg_oth, "c"), w_qkv)
    terms, input_grad = lax.optimization_barrier((terms, input_grad))
    terms, att, att_oth = lax.optimization_barrier((middle_sum(pos, firsts, terms), att, att_oth))
    terms = lax.all_to_all(terms, "z", 0, 0)
    terms, layer_out = lax.optimization_barrier((terms, output_side(pos, att, att_oth, w_out)))
    own, oth = (jnp.sum(terms[:, core].astype(F32), axis=0).astype(BF16) for core in range(2))
    pair = ("c", "dp")
    qkv_grad, out_grad = last_rows(pos, own, along(own, pair, 1), along(oth, pair, 2), along(oth, pair, 3))
    return (layer_out[None], input_grad[None], qkv_grad, out_grad)


def solution(mesh):
    split = Mesh(mesh.devices.reshape(ZN, XN, YN, 2, 2), ("z", "x", "y", "c", "dp"))
    seq = ("z", "x", "y", "c")
    return jax.shard_map(
        shards,
        mesh=split,
        in_specs=(P("dp", seq, None), P("dp", seq, None), P(), P()),
        out_specs=(P("dp", seq, None), P("dp", seq, None), P(seq, None), P(seq, None)),
        check_vma=False,
    )
```

```python
import jax
import jax.numpy as jnp
import numpy as np
from jax import lax
from jax.experimental import pallas as pl
from jax.experimental.pallas import tpu as pltpu
from jax.sharding import Mesh, PartitionSpec as P

D = 768
H = 384
TOK = 256
NR = 128
DH = 64
ZN, XN, YN = 8, 4, 2
ZR = 48
HALF_ROOT = 0.7071067811865476
LOG2E = 1.4426950408889634
VMEM = 56 * 1024 * 1024
F32 = jnp.float32
BF16 = jnp.bfloat16


def dot(a, b):
    return lax.dot_general(a, b, (((1,), (0,)), ((), ())), preferred_element_type=F32)


def dot_nt(a, b):
    return lax.dot_general(a, b, (((1,), (1,)), ((), ())), preferred_element_type=F32)


def dot_tn(a, b):
    return lax.dot_general(a, b, (((0,), (0,)), ((), ())), preferred_element_type=F32)


def iota(shape, axis):
    return lax.broadcasted_iota(jnp.int32, shape, axis)


def pair_matrix(rows, cols, valid):
    r, k = iota((rows, cols), 0), iota((rows, cols), 1)
    return (((k >> 1) == r) & (r < valid)).astype(BF16)


def coarsen(node, rows=None, valid=None):
    rows = node.shape[0] // 2 if rows is None else rows
    valid = rows if valid is None else valid
    return (dot(pair_matrix(rows, node.shape[0], valid), node) * HALF_ROOT).astype(BF16)


def whole(*shape):
    return pl.BlockSpec(shape, lambda *_: (0,) * len(shape))


def call(body, grid, ins, outs, scratch=()):
    return pl.pallas_call(
        body,
        grid_spec=pltpu.PrefetchScalarGridSpec(
            num_scalar_prefetch=1,
            grid=grid,
            in_specs=ins,
            out_specs=[s for s, _ in outs],
            scratch_shapes=list(scratch),
        ),
        out_shape=[jax.ShapeDtypeStruct(shape, kind) for _, (shape, kind) in outs],
        compiler_params=pltpu.CompilerParams(vmem_limit_bytes=VMEM),
    )


def tree_body(pos, x_own, x_oth, wk, wv, kv_out, n1_out, n2_out, n3_out, n4_out, zs_out, rows, pad):
    c, z = pos[0], pos[1]
    for e, x in ((c, x_own), (1 - c, x_oth)):
        for p, w in ((0, wk), (1, wv)):
            part = dot(x[...], w[...]).astype(BF16)
            kv_out[e, p] = part
            for n in range(3):
                rows[e, 3 * p + n] = part[:, 128 * n : 128 * n + 128].astype(F32)

    def coarser(ref, n):
        node = ((ref[pl.ds(0, n, stride=2), :] + ref[pl.ds(1, n, stride=2), :]) * HALF_ROOT).astype(BF16)
        return node, node.astype(F32)

    for p in range(2):
        for n in range(3):
            cols, block = slice(128 * n, 128 * n + 128), 3 * p + n
            top = pad.at[block]
            for e in range(2):
                ref = rows.at[e, block]
                n1_out[e, p, :, cols], wide = coarser(ref, NR)
                ref[:NR] = wide
                n2_out[p, 64 * e : 64 * e + 64, cols], wide = coarser(ref, 64)
                top[64 * e : 64 * e + 64] = wide
            n3_out[p, :, cols], wide = coarser(top, 64)
            top[:64] = wide
            n4_out[p, :, cols], wide = coarser(top, 32)
            top[:32] = wide
            n5, wide = coarser(top, 16)
            top[:16] = wide
            top[16:48] = jnp.zeros((32, 128), F32)
            top[16:24] = coarser(top, 8)[1]
            top[32:36] = coarser(top.at[pl.ds(16, 8)], 4)[1]
            n6, n7 = top[16:32].astype(BF16), top[32:48].astype(BF16)
            zs_out[z, p, :, cols] = jnp.zeros_like(n5)
            zs_out[z ^ 1, p, :, cols] = n5
            for far in (2, 3):
                zs_out[z ^ far, p, :, cols] = n6
            for far in (4, 5, 6, 7):
                zs_out[z ^ far, p, :, cols] = n7


def tree(pos, x_own, x_oth, w_qkv):
    col = lambda part: pl.BlockSpec((D, H), lambda i, s: (0, 2 * part + s[0]))
    outs = [(2, 2, TOK, H), (2, 2, NR, H), (2, NR, H), (2, 64, H), (2, 32, H), (ZN, 2, 16, H)]
    return call(
        tree_body,
        (1,),
        [whole(TOK, D)] * 2 + [col(1), col(2)],
        [(whole(*shape), (shape, BF16)) for shape in outs],
        [pltpu.VMEM((2, 6, TOK, 128), F32), pltpu.VMEM((6, NR, 128), F32)],
    )(pos, x_own, x_oth, w_qkv, w_qkv)


def project_body(pos, x_own, x_oth, ct_own, ct_oth, wq, wo, perm, q_out, ag_out, xt_out):
    c = pos[0]
    for e, x, ct in ((c, x_own, ct_own), (1 - c, x_oth, ct_oth)):
        q_out[e] = dot(x[...], wq[...]).astype(BF16)
        ag_out[e] = dot_nt(ct[...], wo[...]).astype(BF16)
        xt_out[e] = dot_nt(perm[...], x[...]).astype(BF16)


def project(pos, x_own, x_oth, ct_own, ct_oth, w_qkv, w_out, perm):
    outs = [(2, TOK, H), (2, TOK, H), (2, D, TOK)]
    return call(
        project_body,
        (1,),
        [whole(TOK, D)] * 4
        + [pl.BlockSpec((D, H), lambda i, s: (0, s[0])), pl.BlockSpec((H, D), lambda i, s: (s[0], 0)), whole(D, D)],
        [(whole(*shape), (shape, BF16)) for shape in outs],
    )(pos, x_own, x_oth, ct_own, ct_oth, w_qkv, w_out, perm)


def z_source(z, rows_axis, shape):
    i = iota(shape, rows_axis)
    near = 16 * (z ^ 1) + i
    mid = 16 * (z ^ (2 + ((i - 16) >> 3))) + ((i - 16) & 7)
    far = 16 * (z ^ (4 + ((i - 32) >> 2))) + ((i - 32) & 3)
    return jnp.where(i < 16, near, jnp.where(i < 32, mid, far))


def plane_body(pos, zr, out):
    hot = (iota((ZR, 128), 1) == z_source(pos[1], 0, (ZR, 128))).astype(BF16)
    both = jnp.concatenate([zr[:, p].reshape(128, H) for p in range(2)], axis=1)
    rows = dot(hot, both).astype(BF16)
    for slot in range(8):
        for p in range(2):
            out[slot, p] = rows[:, H * p : H * p + H]


def plane_slots(pos, zr):
    return call(
        plane_body,
        (1,),
        [whole(ZN, 2, 16, H)],
        [(whole(8, 2, ZR, H), ((8, 2, ZR, H), BF16))],
    )(pos, zr)[0]


def attention_body(pos, q, ag, kv, n1, yr, wr, wy, xr, att_out, dq_out, dkv_out, dn1_out, dy_out, dwy_out, dw_out, dx_out, near, near_t, shared, shared_t, s_ref, dw_ref, w_ref, ds_ref, drem):
    for p in range(2):
        for e in range(2):
            near[e, p, :256] = kv[e, p]
            near[e, p, 256:] = n1[1 - e, p]
            near_t[e, p] = near[e, p].T
        shared[p, :128] = yr[p]
        shared[p, 128:256] = wr[p]
        shared[p, 256:384] = wy[p]
        for slot in range(8):
            start = 384 + ZR * slot
            shared[p, start : start + ZR] = xr[slot, p]
        shared_t[p] = shared[p].T
    lane = iota((TOK, 128), 1)
    steps = [(e, h) for e in range(2) for h in range(2)]
    masked = {}

    def scores(step):
        e, h = steps[step]
        mine = (lane >> 6) == h
        qh = jnp.where(mine, q[e], jnp.zeros((), BF16))
        ah = jnp.where(mine, ag[e], jnp.zeros((), BF16))
        masked[step] = (qh, ah)
        for ref, p, token in ((s_ref, 0, qh), (dw_ref, 1, ah * jnp.asarray(DH ** -0.5, BF16))):
            ref[step % 2, :384] = dot_nt(near[e, p], token)
            ref[step % 2, 384:] = dot_nt(shared[p], token)

    scores(0)
    for step, (e, h) in enumerate(steps):
        if step + 1 < len(steps):
            scores(step + 1)
        if h == 0:
            att_t, dq_t = [], []
        s, dw, b = s_ref.at[step % 2], dw_ref.at[step % 2], step % 2
        qh, ah = masked[step]
        top = jnp.max(s[...], axis=0, keepdims=True)
        un = jnp.exp2((s[...] - top) * (LOG2E * DH ** -0.5))
        s[...] = un
        inverse = 1.0 / jnp.sum(un, axis=0, keepdims=True)
        delta = jnp.sum(un * dw[...], axis=0, keepdims=True) * inverse
        prob = s[...] * inverse
        cols = slice(TOK * h, TOK * h + TOK)
        w_ref[e, :, cols] = prob.astype(BF16)
        ds_ref[e, :, cols] = (prob * (dw[...] - delta)).astype(BF16)
        head = slice(64 * h, 64 * h + 64)
        for out, p, ref in ((att_t, 1, w_ref), (dq_t, 0, ds_ref)):
            out.append(dot(near_t[e, p, head], ref[e, :384, cols]) + dot(shared_t[p, head], ref[e, 384:, cols]))
        if h == 0:
            continue
        dk = dot(ds_ref[e], jnp.concatenate([masked[step - 1][0], qh], axis=0))
        dv = dot(w_ref[e], jnp.concatenate([masked[step - 1][1], ah], axis=0))
        att_out[e] = jnp.concatenate(att_t, axis=0).T.astype(BF16)
        dq_out[e] = jnp.concatenate(dq_t, axis=0).T.astype(BF16)
        for p, grad in ((0, dk), (1, dv)):
            dkv_out[e, p] = grad[:256]
            dn1_out[1 - e, p] = grad[256:384]
            if e == 0:
                drem[p] = grad[384:]
            else:
                drem[p] = drem[p] + grad[384:]
    for p in range(2):
        rows = drem[p].astype(BF16)
        dy_out[p] = rows[:128]
        dwy_out[p] = rows[256:384]
        dw_out[p] = drem[p, 128:256]
        for slot in range(8):
            start = 384 + ZR * slot
            dx_out[slot, p] = rows[start : start + ZR]


def attention(pos, q, ag, kv, n1, yr, wr, wy, xr):
    def cut(*lead):
        return pl.BlockSpec(lead + (128,), lambda i, s: (0,) * len(lead) + (i,))

    outs = [
        ((2, TOK), BF16), ((2, TOK), BF16), ((2, 2, TOK), F32), ((2, 2, NR), F32), ((2, NR), BF16), ((2, NR), BF16),
        ((2, NR), F32), ((8, 2, ZR), BF16),
    ]
    n = 1152
    return call(
        attention_body,
        (H // 128,),
        [cut(2, TOK), cut(2, TOK), cut(2, 2, TOK), cut(2, 2, NR), cut(2, NR), cut(2, NR), cut(2, NR), cut(8, 2, ZR)],
        [(cut(*lead), (lead + (H,), kind)) for lead, kind in outs],
        [
            pltpu.VMEM((2, 2, 384, 128), BF16), pltpu.VMEM((2, 2, 128, 384), BF16),
            pltpu.VMEM((2, 768, 128), BF16), pltpu.VMEM((2, 128, 768), BF16), pltpu.VMEM((2, n, TOK), F32), pltpu.VMEM((2, n, TOK), F32),
            pltpu.VMEM((2, n, 2 * TOK), BF16), pltpu.VMEM((2, n, 2 * TOK), BF16), pltpu.VMEM((2, 768, 128), F32),
        ],
    )(pos, q, ag, kv, n1, yr, wr, wy, xr)


def output_body(pos, att_own, att_oth, w_own, w_oth, out):
    c = pos[0]
    out[...] = (dot(att_own[c], w_own[...]) + dot(att_oth[c], w_oth[...])).astype(BF16)


def output_side(pos, att_own, att_oth, w_out):
    row = lambda flip: pl.BlockSpec((H, D), lambda i, s: (s[0] ^ flip, 0))
    return call(
        output_body,
        (1,),
        [whole(2, TOK, H)] * 2 + [row(0), row(1)],
        [(whole(TOK, D), ((TOK, D), BF16))],
    )(pos, att_own, att_oth, w_out, w_out)[0]


def terms_body(pos, att_own, att_oth, ct_own, ct_oth, dq, xt, p_own, p_oth, *rest):
    c, y, dp = pos[0], pos[2] & 1, pos[3]
    slots = rest[-1]
    total = dot(xt[0], dq[0]) + dot(xt[1], dq[1])
    slots[:, :, 0] = total.astype(BF16).reshape(XN, YN, 96, H)
    total = None
    for e, ct in ((c, ct_own), (1 - c, ct_oth)):
        att_t = (dot_nt(p_own[...], att_own[e]) + dot_nt(p_oth[...], att_oth[e])).astype(BF16)
        term = dot(att_t, ct[...])
        total = term if total is None else total + term
    slots[:, :, 1] = total.astype(BF16).reshape(XN, YN, 96, H)
    for far in range(4):
        rest[far][...] = slots[:, y ^ (far >> 1), dp ^ (far & 1)]


def output_terms(pos, att_own, att_oth, ct_own, ct_oth, dq, xt, perm):
    col = lambda flip, rows: pl.BlockSpec((rows, H), lambda i, s: (0, s[0] ^ flip))
    slot = (XN, 96, H)
    return call(
        terms_body,
        (1,),
        [whole(2, TOK, H)] * 2 + [col(0, TOK)] * 2 + [whole(2, TOK, H), whole(2, D, TOK), col(0, D), col(1, D)],
        [(whole(*slot), (slot, BF16))] * 4,
        [pltpu.VMEM((XN, YN, 2, 96, H), BF16)],
    )(pos, att_own, att_oth, ct_own, ct_oth, dq, xt, perm, perm)


def x_sum_body(pos, t0, t1, t2, t3, *rest):
    x = pos[2] >> 1
    slots = rest[-1]
    total = (t0[...].astype(F32) + t1[...].astype(F32)) + (t2[...].astype(F32) + t3[...].astype(F32))
    slots[...] = total.astype(BF16)
    for far in range(XN):
        rest[far][...] = slots[x ^ far]


def x_sum(pos, *terms):
    shape = (XN, 96, H)
    return call(
        x_sum_body,
        (1,),
        [whole(*shape)] * 4,
        [(whole(96, H), ((96, H), BF16))] * 4,
        [pltpu.VMEM(shape, BF16)],
    )(pos, *terms)


def back_body(pos, xr, dw, dwy, out, *tiers):
    hot = (iota((128, ZR), 0) == z_source(pos[1], 1, (128, ZR))).astype(BF16)
    for p in range(2):
        total = xr[0, p].astype(F32)
        for slot in range(1, 8):
            total = total + xr[slot, p].astype(F32)
        out[:, p] = dot(hot, total.astype(BF16)).astype(BF16).reshape(8, 16, H)
        start = 0
        for tier in tiers:
            rows = tier.shape[1]
            total = dw[p, start : start + rows] + dwy[p, start : start + rows].astype(F32)
            tier[p] = total.astype(BF16)
            start += rows


def back_slots(pos, xr, dw, dwy):
    outs = [(ZN, 2, 16, H), (2, 64, H), (2, 32, H), (2, 32, H)]
    return call(
        back_body,
        (1,),
        [whole(8, 2, ZR, H), whole(2, NR, H), whole(2, NR, H)],
        [(whole(*shape), (shape, BF16)) for shape in outs],
    )(pos, xr, dw, dwy)


def leaf_body(pos, zr, dkv, dn1, dy, g3, g4_a, g4_b, dq, xt, own_out, oth_out, grad_out):
    def split(grad):
        high = grad.astype(BF16)
        return [high, (grad - high.astype(F32)).astype(BF16)]

    def hot(hit, scale):
        return jnp.where(hit, scale, 0.0).astype(BF16)

    def wide(ref):
        return jnp.concatenate([ref[0], ref[1]], axis=1)

    zs = jnp.concatenate([zr[:, p].reshape(128, H) for p in range(2)], axis=1)
    ws = jnp.concatenate([wide(g3), wide(g4_a), wide(g4_b)], axis=0)
    ys = wide(dy)
    sides = ((pos[0], own_out), (1 - pos[0], oth_out))
    for e, pg_out in sides:
        t, k = iota((TOK, 128), 0), iota((TOK, 128), 1)
        far, row, chip = (k >> 4) ^ pos[1], k & 15, t + TOK * e
        first = hot(t >> 1 == k, 1.0)
        third = hot(chip >> 3 == k, 0.5)
        odd = hot((far == 1) & (row == chip >> 5), 0.25) + hot((far >= 4) & (row == chip >> 7), 0.125)
        second = hot(chip >> 2 == k, 0.5)
        fourth = hot((k >= 64) & (chip >> 4 == k & 31), 0.25)
        even = hot((far >> 1 == 1) & (row == chip >> 6), 0.125)
        up = dot(jnp.concatenate([first, first, third, odd], axis=1), jnp.concatenate(split(wide(dn1.at[e])) + [ws, zs], axis=0))
        up = up * HALF_ROOT + dot(jnp.concatenate([second, fourth, even], axis=1), jnp.concatenate([ys, ws, zs], axis=0))
        for p in range(2):
            pg_out[:, H * (1 + p) : H * (2 + p)] = (dkv[e, p] + up[:, H * p : H * p + H]).astype(BF16)
        pg_out[:, :H] = dq[e]
    for p in range(2):
        cols = slice(H * (1 + p), H * (2 + p))
        first, second = (dot(xt[e], pg_out[:, cols]) for e, pg_out in sides)
        total = first + second
        grad_out[:, p] = total.astype(BF16).reshape(8, 96, H)


def leaf_grads(pos, zr, dkv, dn1, dy, g3, g4_a, g4_b, dq, xt):
    return call(
        leaf_body,
        (1,),
        [
            whole(ZN, 2, 16, H), whole(2, 2, TOK, H), whole(2, 2, NR, H), whole(2, NR, H), whole(2, 64, H), whole(2, 32, H),
            whole(2, 32, H), whole(2, TOK, H), whole(2, D, TOK),
        ],
        [(whole(TOK, 3 * H), ((TOK, 3 * H), BF16))] * 2 + [(whole(8, 2, 96, H), ((8, 2, 96, H), BF16))],
    )(pos, zr, dkv, dn1, dy, g3, g4_a, g4_b, dq, xt)


def input_body(pos, pg_own, pg_oth, *rest):
    out = rest[-1]
    total = None
    for part in range(3):
        for pg, w in ((pg_own, rest[part]), (pg_oth, rest[3 + part])):
            term = dot_nt(pg[:, H * part : H * part + H], w[...])
            total = term if total is None else total + term
    out[...] = total.astype(BF16)


def input_side(pos, pg_own, pg_oth, w_qkv):
    col = lambda part, flip: pl.BlockSpec((D, H), lambda i, s: (0, 2 * part + (s[0] ^ flip)))
    return call(
        input_body,
        (1,),
        [whole(TOK, 3 * H)] * 2 + [col(part, flip) for flip in (0, 1) for part in range(3)],
        [(whole(TOK, D), ((TOK, D), BF16))],
    )(pos, pg_own, pg_oth, *[w_qkv] * 6)[0]


def total_of(refs):
    total = refs[0].astype(F32)
    for ref in refs[1:]:
        total = total + ref.astype(F32)
    return total


def middle_body(pos, f0, f1, f2, f3, second, out):
    first = total_of([f0[...], f1[...], f2[...], f3[...]]).astype(BF16)
    i, k = iota((256, 96), 0), iota((256, 96), 1)
    row, half = i & 7, (i >> 3) & 1
    hit = (k == 6 * (i >> 4) + row) & (row < 6)
    rows = dot((hit & (half == 0)).astype(BF16), first)
    rows = rows + dot((hit & (half == 1)).astype(BF16), total_of([second[slot] for slot in range(16)]).astype(BF16))
    rows = rows.astype(BF16).reshape(ZN, 2, 16, H)
    for core in range(2):
        out[:, core ^ pos[0]] = rows[:, core]


def middle_sum(pos, firsts, second):
    shape = (ZN, 2, 16, H)
    return call(
        middle_body, (1,), [whole(96, H)] * 4 + [whole(16, 96, H)], [(whole(*shape), (shape, BF16))]
    )(pos, *firsts, second)[0]


def last_body(pos, own, from_dp, from_core, from_both, qkv_out, out_out, parts):
    core, dp = pos[0], pos[3]
    parts[core, dp] = own[...]
    parts[core, 1 - dp] = from_dp[...]
    parts[1 - core, dp] = from_core[...]
    parts[1 - core, 1 - dp] = from_both[...]
    for core in range(2):
        low, high = parts[core, 0].astype(F32), parts[core, 1].astype(F32)
        cols = lambda part: slice(D * part + H * core, D * part + H * core + H)
        qkv_out[:, cols(0)] = low[:6]
        qkv_out[:, cols(1)] = low[8:14]
        qkv_out[:, cols(2)] = high[8:14]
        out_out[:, cols(0)] = high[:6]


def last_rows(pos, *parts):
    return call(
        last_body,
        (1,),
        [whole(16, H)] * 4,
        [(whole(6, 3 * D), ((6, 3 * D), F32)), (whole(6, D), ((6, D), F32))],
        [pltpu.VMEM((2, 2, 16, H), BF16)],
    )(pos, *parts)


def swap(value, axis):
    return lax.ppermute(value, axis, [(0, 1), (1, 0)])


def along(value, axes, far, count=4):
    return lax.ppermute(value, axes, [(i, i ^ far) for i in range(count)])


def row_order():
    f = np.arange(D)
    source = 96 * (f // 12 % 8) + 12 * (f // 96) + f % 12
    return jnp.asarray(source[:, None] == f[None, :], BF16)


def shards(x_tokens, cotangent, w_qkv, w_out):
    x_own, ct_own = x_tokens[0], cotangent[0]
    c, z, dp = lax.axis_index("c"), lax.axis_index("z"), lax.axis_index("dp")
    j = 2 * lax.axis_index("x") + lax.axis_index("y")
    pos = jnp.stack([c, z, j, dp]).astype(jnp.int32)
    x_oth, ct_oth = swap(x_own, "c"), swap(ct_own, "c")
    perm = row_order()

    kv, n1, n2, n3, n4, zs = tree(pos, x_own, x_oth, w_qkv)
    yr = swap(n2, "y")
    wr = jnp.concatenate([along(n3, "x", 1), along(n4, "x", 2), along(n4, "x", 3)], axis=1)
    zr = lax.all_to_all(zs, "z", 0, 0)
    zr, yr, wr, ct_oth = lax.optimization_barrier((zr, yr, wr, ct_oth))
    wy = swap(wr, "y")
    xs, wy = lax.optimization_barrier((plane_slots(pos, zr), wy))
    xr = lax.all_to_all(xs, ("x", "y"), 0, 0)
    q, ag, xt = project(pos, x_own, x_oth, ct_own, ct_oth, w_qkv, w_out, perm)
    att, dq, dkv, dn1, dy, dwy, dw, dx = attention(pos, q, ag, kv, n1, yr, wr, wy, xr)

    dx_r = lax.all_to_all(dx, ("x", "y"), 0, 0)
    att_oth = swap(att, "c")
    dwy = swap(dwy, "y")
    first, *firsts = output_terms(pos, att, att_oth, ct_own, ct_oth, dq, xt, perm)
    firsts = [along(firsts[far - 1], ("y", "dp"), far) for far in (1, 2, 3)]
    dy = swap(dy, "y")
    dx_r, first, dwy, dy = lax.optimization_barrier((dx_r, first, dwy, dy))
    dz, g3, g4_a, g4_b = back_slots(pos, dx_r, dw, dwy)
    dz_r = lax.all_to_all(dz, "z", 0, 0)
    g3, g4_a, g4_b, firsts = lax.optimization_barrier((g3, g4_a, g4_b, firsts))
    g3, g4_a, g4_b = along(g3, "x", 1), along(g4_a, "x", 2), along(g4_b, "x", 3)
    pg_own, pg_oth, terms = leaf_grads(pos, dz_r, dkv, dn1, dy, g3, g4_a, g4_b, dq, xt)
    terms, first, firsts = lax.optimization_barrier((terms, first, firsts))
    firsts = x_sum(pos, first, *firsts)
    firsts = list(firsts[:1]) + [along(firsts[far], "x", far) for far in (1, 2, 3)]
    terms = lax.all_to_all(terms.reshape(16, 96, H), ("x", "y", "dp"), 0, 0)
    input_grad = input_side(pos, pg_own, swap(pg_oth, "c"), w_qkv)
    terms, input_grad = lax.optimization_barrier((terms, input_grad))
    terms, att, att_oth = lax.optimization_barrier((middle_sum(pos, firsts, terms), att, att_oth))
    terms = lax.all_to_all(terms, "z", 0, 0)
    terms, layer_out = lax.optimization_barrier((terms, output_side(pos, att, att_oth, w_out)))
    own, oth = (jnp.sum(terms[:, core].astype(F32), axis=0).astype(BF16) for core in range(2))
    pair = ("c", "dp")
    qkv_grad, out_grad = last_rows(pos, own, along(own, pair, 1), along(oth, pair, 2), along(oth, pair, 3))
    return (layer_out[None], input_grad[None], qkv_grad, out_grad)


def solution(mesh):
    split = Mesh(mesh.devices.reshape(ZN, XN, YN, 2, 2), ("z", "x", "y", "c", "dp"))
    seq = ("z", "x", "y", "c")
    return jax.shard_map(
        shards,
        mesh=split,
        in_specs=(P("dp", seq, None), P("dp", seq, None), P(), P()),
        out_specs=(P("dp", seq, None), P("dp", seq, None), P(seq, None), P(seq, None)),
        check_vma=False,
    )
```
